128 devices in a mesh: segment: 2 (over x_lo), dp: 16 (over z, y), vocab: 4 (over x_hi, core).
Axes of the slice: x: 4 (x_hi: 2, x_lo: 2; x = x_hi * 2 + x_lo), y: 4, z: 4, core: 2. Of those that a mesh axis runs over, the one named last changes fastest.
Arguments:
- patches: bfloat16 [2, 16, 36, 1152], P(None, 'dp'), may hold values from -6 to 6
- text_embed: bfloat16 [2, 16, 96, 4096], P(None, 'dp'), may hold values from -6 to 6
- mask_embed: bfloat16 [4096], replicated, may hold values from -6 to 6
- image_counts: int32 [2, 16], P(None, 'dp'), may hold values from 1 to 6
- image_order: int32 [2, 16, 6], P(None, 'dp'), may hold values from 0 to 5, each once within a row
- masked_positions: int32 [2, 16, 4], P(None, 'dp'), may hold values from 36 to 95, as said below
- ratio_index: int32 [2, 16], replicated, may hold values from 1 to 8
- enc_up: bfloat16 [2, 1152, 4304], P(None, None, 'vocab'), may hold values from -0.1875 to 0.1875
- enc_down: bfloat16 [2, 4304, 1152], P(None, 'vocab'), may hold values from -0.09375 to 0.09375
- projector: bfloat16 [1152, 4096], P(None, 'vocab'), may hold values from -0.1875 to 0.1875
- lang_qkv: bfloat16 [2, 3, 4096, 2048], P('segment', None, 'dp', 'vocab'), may hold values from -0.09375 to 0.09375
- lang_out: bfloat16 [2, 2048, 4096], P('segment', 'vocab', 'dp'), may hold values from -0.125 to 0.125
- head_weight: bfloat16 [32768, 4096], P(('segment', 'dp', 'vocab')), may hold values from -0.25 to 0.25
- teacher_logits: bfloat16 [128, 32768], P(None, ('segment', 'dp', 'vocab')), may hold values from -18 to 320
Outputs:
- loss: float32 [], replicated
- projector_grad: float32 [1152, 4096], P(('segment', 'dp'), 'vocab')
The draws below stay inside these ranges and needn't reach their ends.
Inputs may be any that keep to these rules, and one draw needn't show every extreme that they name: `masked_positions`: distinct cells of the text part, from 36 on.
All inputs are finite; a program needn't handle non-finite values.
Results may differ from the reference program's by a relative error of at most 0.039.
Values may be sent and summed in bfloat16 or wider, within the bound.
No kernel may reach another device: no remote copies, remote signals or barrier semaphores. Data moves between devices by JAX's collectives and lax.ppermute only.
A program may use at most 128 MiB of HBM per device.

```python
import jax
import jax.numpy as jnp
from jax import lax

DE = 1152
FE = 4304
D = 4096
HD = 128
MAXIMG = 6
SEQ = 96
MASKED = 4
RATIOS = 8
ENC_LAYERS = 2
MB = 2
LAYERS = 2
SAMPLES = 16
MAXP = 36
HH = 2048
VOCAB = 32768
ROWS = 128
N_VOCAB = 4


def draw_masked_positions(key, part):
    key = jax.random.fold_in(key, 11)
    span = SEQ - MAXP
    row_keys = jax.random.split(key, MB * SAMPLES)
    orders = jax.vmap(lambda row_key: jax.random.permutation(row_key, span))(row_keys)
    chosen = orders[:, :MASKED].astype(jnp.int32)
    inner_perm = jax.random.permutation(jax.random.fold_in(key, 2), span - 2).astype(jnp.int32) + 1
    first_row = jnp.concatenate([jnp.array([0, span - 1], jnp.int32), inner_perm[:MASKED - 2]])
    chosen = chosen.at[0].set(first_row)
    return (chosen + MAXP).reshape(MB, SAMPLES, MASKED).astype(jnp.int32)


def draw_teacher_logits(key, part):
    key = jax.random.fold_in(key, 5)
    base = jnp.clip(3.0 * jax.random.normal(key, (ROWS, VOCAB), jnp.float32), -18.0, 18.0)
    return base.astype(jnp.bfloat16)


def touch_ends(entries, own_key, smallest, high):
    extent = entries.shape
    spot = [jax.random.randint(jax.random.fold_in(own_key, axis), (), 0, extent[axis]) for axis in range(len(extent))]
    entries = entries.at[tuple(spot)].set(smallest)
    longest = extent.index(max(extent))
    spot[longest] = (spot[longest] + 1) % extent[longest]
    return entries.at[tuple(spot)].set(high)


def block_levels(key, dims, cuts, smallest, top_value):
    def one(position, parts):
        steps = jax.random.uniform(jax.random.fold_in(jax.random.fold_in(key, 6), position), (parts,), jnp.float32, smallest / len(cuts), top_value / len(cuts))
        return jnp.repeat(jnp.exp(steps), dims[position] // parts).reshape((-1,) + (1,) * (len(dims) - position - 1))

    loudness = one(*cuts[0])
    for cut in cuts[1:]:
        loudness = loudness * one(*cut)
    return loudness


def noise(stream_key, extent, deviation, most, pieces=(), kind=jnp.bfloat16):
    drawn = deviation * jax.random.normal(stream_key, extent, jnp.float32)
    if pieces:
        drawn = drawn * block_levels(stream_key, extent, pieces, -0.22, 0.18)
    return jnp.clip(drawn, -most, most).astype(kind)


def setup_inputs(seed: int = 0) -> dict:
    streams_of = jax.random.split(jax.random.key(seed), 15)
    return {
        "patches": noise(streams_of[0], (MB, SAMPLES, MAXP, DE), 1.0, 6.0, ((1, 16),)),
        "text_embed": noise(streams_of[1], (MB, SAMPLES, SEQ, D), 1.0, 6.0, ((1, 16),)),
        "mask_embed": noise(streams_of[2], (D,), 1.0, 6.0),
        "image_counts": touch_ends(jax.random.randint(streams_of[3], (MB, SAMPLES), 1, 7), jax.random.fold_in(streams_of[3], 1), 1, 6).astype(jnp.int32),
        "image_order": jax.vmap(lambda own: jax.random.permutation(own, MAXIMG))(jax.random.split(streams_of[4], MB * SAMPLES)).reshape((MB, SAMPLES, MAXIMG)).astype(jnp.int32),
        "masked_positions": draw_masked_positions(jax.random.fold_in(streams_of[14], 71), 0),
        "ratio_index": touch_ends(jax.random.randint(streams_of[6], (MB, SAMPLES), 1, RATIOS + 1), jax.random.fold_in(streams_of[6], 1), 1, RATIOS).astype(jnp.int32),
        "enc_up": noise(streams_of[7], (ENC_LAYERS, DE, FE), DE ** -0.5, 0.1875, ((2, 4),)),
        "enc_down": noise(streams_of[8], (ENC_LAYERS, FE, DE), FE ** -0.5, 0.09375, ((1, 4),)),
        "projector": noise(streams_of[9], (DE, D), DE ** -0.5, 0.1875, ((1, 4),)),
        "lang_qkv": noise(streams_of[10], (LAYERS, 3, D, HH), D ** -0.5, 0.09375, ((0, 2), (2, 16), (3, 4))),
        "lang_out": noise(streams_of[11], (LAYERS, HH, D), HH ** -0.5, 0.125, ((0, 2), (1, 4), (2, 16))),
        "head_weight": noise(streams_of[12], (VOCAB, D), (D // 9) ** -0.5, 0.25, ((0, 128),)),
        "teacher_logits": draw_teacher_logits(jax.random.fold_in(streams_of[14], 71), 0),
    }


epsilon = 1e-06
rope_base = 500000.0

def norm_rows(values_in):
    return values_in * lax.rsqrt(lax.optimization_barrier(jnp.mean(values_in * values_in, axis=-1, keepdims=True)) + epsilon)

def layer_norm(values_in):
    centred = values_in - lax.optimization_barrier(jnp.mean(values_in, axis=-1, keepdims=True))
    return centred * lax.rsqrt(lax.optimization_barrier(jnp.mean(centred * centred, axis=-1, keepdims=True)) + epsilon)

def norm_back(values_in, cotangent):
    factor = lax.rsqrt(lax.optimization_barrier(jnp.mean(values_in * values_in, axis=-1, keepdims=True)) + epsilon)
    return factor * cotangent - values_in * factor ** 3 * lax.optimization_barrier(jnp.mean(cotangent * values_in, axis=-1, keepdims=True))

def rope_tables(length, head_size):
    halfway = head_size // 2
    inverse = rope_base ** (-2.0 * jnp.arange(halfway, dtype=jnp.float32) / head_size)
    angles = jnp.arange(length, dtype=jnp.float32)[:, None] * inverse[None, :]
    return (jnp.cos(angles)[:, None, :], jnp.sin(angles)[:, None, :])

def rotate(values_in, cosine, sine):
    halfway = values_in.shape[-1] // 2
    first_half = values_in[..., :halfway]
    second_half = values_in[..., halfway:]
    return jnp.concatenate([first_half * cosine - second_half * sine, second_half * cosine + first_half * sine], axis=-1)

def rotate_back(cotangent, cosine, sine):
    halfway = cotangent.shape[-1] // 2
    first_half = cotangent[..., :halfway]
    second_half = cotangent[..., halfway:]
    return jnp.concatenate([first_half * cosine + second_half * sine, second_half * cosine - first_half * sine], axis=-1)

def attend(queries, key_rows, value_rows):
    scores = jnp.einsum('qhd,khd->hqk', queries.astype(jnp.float32), key_rows.astype(jnp.float32)) * queries.shape[-1] ** (-0.5)
    probs = jax.nn.softmax(scores, axis=-1).astype(jnp.bfloat16)
    mixed = jnp.einsum('hqk,khd->qhd', probs.astype(jnp.float32), value_rows.astype(jnp.float32))
    return mixed.astype(jnp.bfloat16)

def attention_parts(hidden, qkv_weight, cosine, sine):
    seq_len = hidden.shape[0]
    heads_here = qkv_weight.shape[2] // HD
    shaped = (seq_len, heads_here, HD)
    normed = norm_rows(hidden.astype(jnp.float32)).astype(jnp.bfloat16)
    queries = rotate(jnp.dot(normed, qkv_weight[0], preferred_element_type=jnp.float32).reshape(shaped), cosine, sine).astype(jnp.bfloat16)
    key_rows = rotate(jnp.dot(normed, qkv_weight[1], preferred_element_type=jnp.float32).reshape(shaped), cosine, sine).astype(jnp.bfloat16)
    value_rows = jnp.dot(normed, qkv_weight[2], preferred_element_type=jnp.float32).astype(jnp.bfloat16).reshape(shaped)
    mixed = attend(queries, key_rows, value_rows).reshape(seq_len, heads_here * HD)
    return (queries, key_rows, value_rows, mixed)

def attention_back(gradient, queries, key_rows, value_rows, qkv_weight, out_weight, cosine, sine):
    seq_len = gradient.shape[0]
    d_mixed = jnp.dot(gradient, out_weight.T, preferred_element_type=jnp.float32).astype(jnp.bfloat16)
    pullback = jax.vjp(attend, queries, key_rows, value_rows)[1]
    d_query, d_key, d_value = pullback(d_mixed.reshape(queries.shape))
    d_query = rotate_back(d_query.astype(jnp.float32), cosine, sine).astype(jnp.bfloat16).reshape(seq_len, -1)
    d_key = rotate_back(d_key.astype(jnp.float32), cosine, sine).astype(jnp.bfloat16).reshape(seq_len, -1)
    d_value = d_value.reshape(seq_len, -1)
    return ((d_query, qkv_weight[0].T), (d_key, qkv_weight[1].T), (d_value, qkv_weight[2].T))

def grouped_sum(pairs):
    inner = pairs[0][0].shape[1] // N_VOCAB
    summed = jnp.zeros((pairs[0][0].shape[0], pairs[0][1].shape[1]), jnp.float32)
    for group in range(N_VOCAB):
        portion = jnp.zeros_like(summed)
        for left_op, right_op in pairs:
            portion = portion + jnp.dot(left_op[:, group * inner:(group + 1) * inner], right_op[group * inner:(group + 1) * inner], preferred_element_type=jnp.float32)
        summed = summed + lax.optimization_barrier(portion.astype(jnp.bfloat16)).astype(jnp.float32)
    return summed

def build_sequence(image_rows, text_rows, mask_row, image_total, ordering, positions):
    seq_len = text_rows.shape[0]
    per_image = image_rows.shape[0] // ordering.shape[0]
    slot_ids = jnp.arange(image_rows.shape[0], dtype=jnp.int32)
    image_of = slot_ids // per_image
    target = jnp.take(ordering, image_of) * per_image + slot_ids % per_image
    is_live = image_of < image_total
    cell_ids = jnp.arange(seq_len, dtype=jnp.int32)
    matches = (target[None, :] == cell_ids[:, None]) & is_live[None, :]
    placing = matches.astype(jnp.bfloat16)
    filled = jnp.any(matches, axis=1)
    placed = jnp.dot(placing, image_rows, preferred_element_type=jnp.float32).astype(jnp.bfloat16)
    sequence = jnp.where(filled[:, None], placed, text_rows)
    masked = jnp.any(positions[None, :] == cell_ids[:, None], axis=1)
    sequence = jnp.where(masked[:, None], mask_row[None, :], sequence)
    return (sequence, placing)

def pick_matrix(positions, seq_len):
    return (positions[:, None] == jnp.arange(seq_len, dtype=jnp.int32)[None, :]).astype(jnp.bfloat16)

def encode_rows(patch_rows, enc_up, enc_down):
    current = patch_rows
    for layer in range(ENC_LAYERS):
        normed = layer_norm(current.astype(jnp.float32)).astype(jnp.bfloat16)
        inner = jax.nn.gelu(jnp.dot(normed, enc_up[layer], preferred_element_type=jnp.float32), approximate=True).astype(jnp.bfloat16)
        current = (current.astype(jnp.float32) + grouped_sum(((inner, enc_down[layer]),))).astype(jnp.bfloat16)
    return current

def reference(patches, text_embed, mask_embed, image_counts, image_order, masked_positions, ratio_index, enc_up, enc_down, projector, lang_qkv, lang_out, head_weight, teacher_logits):
    cosine, sine = rope_tables(SEQ, HD)
    encoded = encode_rows(patches.reshape(MB * SAMPLES * MAXP, DE), enc_up, enc_down)
    images = jnp.dot(encoded, projector, preferred_element_type=jnp.float32).astype(jnp.bfloat16).reshape(MB, SAMPLES, MAXP, D)
    encoded = encoded.reshape(MB, SAMPLES, MAXP, DE)
    saves = []
    placings = []
    pickers = []
    pre_rows = []
    for micro_index in range(MB):
        for sample_index in range(SAMPLES):
            sequence, placing = build_sequence(images[micro_index, sample_index], text_embed[micro_index, sample_index], mask_embed, image_counts[micro_index, sample_index], image_order[micro_index, sample_index], masked_positions[micro_index, sample_index])
            hidden = sequence
            layer_saves = []
            for layer in range(LAYERS):
                queries, key_rows, value_rows, mixed = attention_parts(hidden, lang_qkv[layer], cosine, sine)
                layer_saves.append((hidden, queries, key_rows, value_rows))
                hidden = (hidden.astype(jnp.float32) + grouped_sum(((mixed, lang_out[layer]),))).astype(jnp.bfloat16)
            picker = pick_matrix(masked_positions[micro_index, sample_index], SEQ)
            pre_rows.append(jnp.dot(picker, hidden, preferred_element_type=jnp.float32))
            saves.append(layer_saves)
            placings.append(placing)
            pickers.append(picker)
    row_data = jnp.concatenate(pre_rows, axis=0)
    final = norm_rows(row_data).astype(jnp.bfloat16)
    logits = jnp.dot(final, head_weight.T, preferred_element_type=jnp.float32)
    teacher = teacher_logits.astype(jnp.float32)
    norm_student = jnp.log(lax.optimization_barrier(jnp.sum(jnp.exp(logits), axis=1, keepdims=True)))
    top_teacher = lax.optimization_barrier(jnp.max(teacher, axis=1, keepdims=True))
    norm_teacher = top_teacher + jnp.log(lax.optimization_barrier(jnp.sum(jnp.exp(teacher - top_teacher), axis=1, keepdims=True)))
    teacher_prob = jnp.exp(teacher - norm_teacher)
    divergence = lax.optimization_barrier(jnp.sum(teacher_prob * (teacher - logits), axis=1)) - norm_teacher[:, 0] + norm_student[:, 0]
    weights = jnp.repeat((RATIOS / ratio_index.astype(jnp.float32)).reshape(-1), MASKED)
    sequences = MB * SAMPLES
    loss = jnp.sum(weights * divergence) / sequences
    d_logits = ((weights / sequences)[:, None] * (jnp.exp(logits - norm_student) - teacher_prob)).astype(jnp.bfloat16)
    d_final = jnp.dot(d_logits, head_weight, preferred_element_type=jnp.float32)
    d_rows = norm_back(row_data, d_final)
    projector_grad = jnp.zeros((DE, D), jnp.float32)
    for seq_index in range(MB * SAMPLES):
        micro_index = seq_index // SAMPLES
        sample_index = seq_index % SAMPLES
        own_rows = d_rows[seq_index * MASKED:(seq_index + 1) * MASKED]
        gradient = jnp.dot(pickers[seq_index].astype(jnp.float32).T, own_rows, precision=lax.Precision.HIGHEST, preferred_element_type=jnp.float32).astype(jnp.bfloat16)
        for layer in range(LAYERS - 1, -1, -1):
            hidden, queries, key_rows, value_rows = saves[seq_index][layer]
            pairs = attention_back(gradient, queries, key_rows, value_rows, lang_qkv[layer], lang_out[layer], cosine, sine)
            d_normed = grouped_sum(pairs)
            gradient = (gradient.astype(jnp.float32) + norm_back(hidden.astype(jnp.float32), d_normed)).astype(jnp.bfloat16)
        d_image = jnp.dot(placings[seq_index].T, gradient, preferred_element_type=jnp.float32).astype(jnp.bfloat16)
        projector_grad = projector_grad + jnp.dot(encoded[micro_index, sample_index].T, d_image, preferred_element_type=jnp.float32)
    return (loss, projector_grad)
```

```python
import jax
import jax.numpy as jnp
from jax import lax
from jax.sharding import PartitionSpec as P

HD = 128
MASKED = 4
RATIOS = 8

epsilon = 1e-06
rope_base = 500000.0

LINE = ("vocab", "segment")
ALL = ("segment", "dp", "vocab")
f32 = jnp.float32
bf16 = jnp.bfloat16


def dot(a, b):
    return jnp.dot(a, b, preferred_element_type=f32)


def dot_nt(a, b):
    return lax.dot_general(a, b, (((1,), (1,)), ((), ())), preferred_element_type=f32)


def dot_tn(a, b):
    return lax.dot_general(a, b, (((0,), (0,)), ((), ())), preferred_element_type=f32)


def swap(block, axis, mask):
    return lax.ppermute(block, axis, [(i, i ^ mask) for i in range(lax.axis_size(axis))])


def exchange(chunks, axes):
    return lax.all_to_all(chunks, axes, 0, 0, tiled=True)


def spread(block, axes):
    size = lax.axis_size(axes)
    return exchange(jnp.broadcast_to(block[None], (size,) + block.shape), axes)


def inverse_rms(values_in):
    return lax.rsqrt(jnp.mean(values_in * values_in, axis=-1, keepdims=True) + epsilon)


def norm_rows(values_in):
    return values_in * inverse_rms(values_in)


def layer_norm(values_in):
    centred = values_in - jnp.mean(values_in, axis=-1, keepdims=True)
    return centred * lax.rsqrt(jnp.mean(centred * centred, axis=-1, keepdims=True) + epsilon)


def norm_back(values_in, cotangent):
    factor = inverse_rms(values_in)
    return factor * cotangent - values_in * factor**3 * jnp.mean(
        cotangent * values_in, axis=-1, keepdims=True
    )


def rope_tables(positions):
    halfway = HD // 2
    inverse = rope_base ** (-2.0 * jnp.arange(halfway, dtype=f32) / HD)
    angles = positions.astype(f32)[..., None] * inverse
    return jnp.cos(angles), jnp.sin(angles)


def rotate(values_in, cosine, sine):
    halfway = values_in.shape[-1] // 2
    first_half = values_in[..., :halfway]
    second_half = values_in[..., halfway:]
    return jnp.concatenate(
        [first_half * cosine - second_half * sine, second_half * cosine + first_half * sine],
        axis=-1,
    )


def encode_rows(current, enc_up, enc_down):
    for layer in range(enc_up.shape[0]):
        normed = layer_norm(current.astype(f32)).astype(bf16)
        inner = jax.nn.gelu(dot(normed, enc_up[layer]), approximate=True).astype(bf16)
        part = dot(inner, enc_down[layer]).astype(bf16)
        others = [swap(part, "vocab", mask).astype(f32) for mask in (1, 2, 3)]
        summed = (part.astype(f32) + others[0]) + (others[1] + others[2])
        current = (current.astype(f32) + summed).astype(bf16)
    return current


def scores_of(queries, keys):
    scores = jnp.einsum("sqhd,skhd->shqk", queries, keys, preferred_element_type=f32)
    return jax.nn.softmax(scores * HD ** (-0.5), axis=-1)


def mix(probs, values):
    return jnp.einsum(
        "shqk,skhd->sqhd", probs.astype(bf16), values, preferred_element_type=f32
    ).astype(bf16)


def score_back(probs, values, d_mixed):
    d_probs = jnp.einsum("sqhd,skhd->shqk", d_mixed, values, preferred_element_type=f32)
    d_probs = d_probs.astype(bf16).astype(f32)
    d_scores = probs * (d_probs - jnp.sum(probs * d_probs, axis=-1, keepdims=True))
    return (d_scores * HD ** (-0.5)).astype(bf16)


def shards(
    patches,
    text_embed,
    mask_embed,
    image_counts,
    image_order,
    masked_positions,
    ratio_index,
    enc_up,
    enc_down,
    projector,
    lang_qkv,
    lang_out,
    head_weight,
    teacher_logits,
):
    segment = lax.axis_index("segment")
    dp_index = lax.axis_index("dp")
    place = lax.axis_index("vocab") * 2 + segment
    line = lax.axis_size(LINE)
    dp_size = lax.axis_size("dp")
    micro = text_embed.shape[0]
    seq_len, width = text_embed.shape[2:]
    slots = patches.shape[2]
    depth = patches.shape[3]
    per_image = slots // image_order.shape[2]

    shard = jnp.concatenate(
        [lang_qkv[0], jnp.transpose(lang_out[0])[None]], axis=0
    )
    half = shard.shape[2] // 2
    rows_here = shard.shape[1]
    low, high = shard[:, :, :half], shard[:, :, half:]
    keep = jnp.where(segment == 0, low, high)
    give = jnp.where(segment == 0, high, low)
    got = swap(give, "segment", 1)
    sections = (
        jnp.where(segment == 0, keep, got),
        jnp.where(segment == 0, got, keep),
    )
    weights = [
        lax.all_gather(
            jnp.transpose(part, (1, 0, 2)).reshape(rows_here, 4 * half), "dp", axis=0, tiled=True
        )
        for part in sections
    ]
    w_qkv = [w[:, : 3 * half] for w in weights]
    w_out = [w[:, 3 * half :] for w in weights]
    heads = half // HD

    encoded = encode_rows(patches.reshape(micro * slots, depth), enc_up, enc_down)
    image_cols = dot(encoded, projector).astype(bf16)
    images = lax.all_gather(image_cols, "vocab", axis=1, tiled=True)

    slot_ids = jnp.arange(slots, dtype=jnp.int32)
    cell_ids = jnp.arange(seq_len, dtype=jnp.int32)
    image_of = slot_ids // per_image
    placings = []
    picks = []
    sequences = []
    for index in range(micro):
        target = jnp.take(image_order[index, 0], image_of) * per_image + slot_ids % per_image
        live = image_of < image_counts[index, 0]
        matches = (target[None, :] == slot_ids[:, None]) & live[None, :]
        placing = matches.astype(bf16)
        placings.append(placing)
        placed = dot(placing, images[index * slots : (index + 1) * slots]).astype(bf16)
        top = jnp.where(
            jnp.any(matches, axis=1)[:, None], placed, text_embed[index, 0, :slots]
        )
        pick = masked_positions[index, 0][:, None] == cell_ids[None, :]
        picks.append(pick.astype(bf16))
        bottom = jnp.where(
            jnp.any(pick, axis=0)[slots:, None], mask_embed[None, :], text_embed[index, 0, slots:]
        )
        sequences += [top, bottom]
    hidden0 = jnp.concatenate(sequences, axis=0)
    tokens = micro * seq_len
    chunk_rows = tokens // line
    pick_all = jnp.zeros((micro * MASKED, tokens), bf16)
    for index in range(micro):
        pick_all = lax.dynamic_update_slice(
            pick_all, picks[index], (index * MASKED, index * seq_len)
        )

    cosine, sine = (t[None, :, None, :] for t in rope_tables(cell_ids))
    mask_cos, mask_sin = (
        t.reshape(micro, MASKED, 1, HD // 2) for t in rope_tables(masked_positions[:, 0])
    )

    def project(hidden, w):
        normed = norm_rows(hidden.astype(f32)).astype(bf16)
        out = dot(normed, w).reshape(micro, seq_len, 3, heads, HD)
        return out[:, :, 0], out[:, :, 1], out[:, :, 2]

    def own_rows(array):
        return lax.dynamic_slice_in_dim(array, place * chunk_rows, chunk_rows, 0)

    def sum_rows(partial):
        parts = exchange(partial.astype(bf16).reshape(line, chunk_rows, width), LINE)
        return jnp.sum(parts.astype(f32), axis=0)

    q, k, v = project(hidden0, w_qkv[0])
    q0 = rotate(q, cosine, sine).astype(bf16)
    k0 = rotate(k, cosine, sine).astype(bf16)
    v0 = v.astype(bf16)
    probs0 = scores_of(q0, k0)
    mixed = mix(probs0, v0).reshape(tokens, half)
    mine = (own_rows(hidden0).astype(f32) + sum_rows(dot_nt(mixed, w_out[0]))).astype(bf16)
    hidden1 = spread(mine, LINE).reshape(tokens, width)

    q, k, v = project(hidden1, w_qkv[1])
    q = jnp.einsum(
        "smt,sthd->smhd", jnp.stack(picks).astype(f32), q, precision=lax.Precision.HIGHEST
    )
    q1 = rotate(q, mask_cos, mask_sin).astype(bf16)
    k1 = rotate(k, cosine, sine).astype(bf16)
    v1 = v.astype(bf16)
    probs1 = scores_of(q1, k1)
    mixed = mix(probs1, v1).reshape(micro * MASKED, half)
    partial = dot_nt(mixed, w_out[1]).astype(bf16)
    cols = width // line
    masked_rows = micro * MASKED
    parts = exchange(
        jnp.transpose(partial.reshape(masked_rows, line, cols), (1, 0, 2)), LINE
    )
    picked = lax.dynamic_slice_in_dim(dot(pick_all, hidden1), place * cols, cols, 1)
    last = (picked + jnp.sum(parts.astype(f32), axis=0)).astype(bf16)

    all_rows = spread(last, ALL).reshape(2, dp_size, 4, masked_rows, cols)
    all_rows = jnp.transpose(all_rows, (1, 3, 2, 0, 4)).reshape(dp_size * masked_rows, width)
    row_count = all_rows.shape[0]
    final = norm_rows(all_rows.astype(f32)).astype(bf16)
    logits = dot_nt(final, head_weight)

    teacher = (
        jnp.transpose(teacher_logits.reshape(micro, dp_size, MASKED, -1), (1, 0, 2, 3))
        .reshape(row_count, -1)
        .astype(f32)
    )
    top = jnp.max(teacher, axis=1)
    powers = jnp.exp(teacher - top[:, None])
    stats = jnp.stack(
        [
            jnp.sum(jnp.exp(logits), axis=1),
            top,
            jnp.sum(powers, axis=1),
            jnp.sum(powers * (teacher - logits), axis=1),
        ]
    )
    stats = spread(stats, ALL).reshape(-1, 4, row_count)
    sum_student = jnp.sum(stats[:, 0], axis=0)
    top_all = jnp.max(stats[:, 1], axis=0)
    scale = jnp.exp(stats[:, 1] - top_all[None])
    sum_teacher = jnp.sum(stats[:, 2] * scale, axis=0)
    cross = jnp.sum(stats[:, 3] * scale, axis=0)
    norm_student = jnp.log(sum_student)
    norm_teacher = top_all + jnp.log(sum_teacher)
    divergence = cross / sum_teacher - norm_teacher + norm_student
    ratio = RATIOS / ratio_index.astype(f32)
    row_weights = jnp.repeat(jnp.transpose(ratio), MASKED, axis=1).reshape(-1)
    total = micro * dp_size
    loss = jnp.sum(row_weights * divergence) / total
    d_logits = (
        (row_weights / total)[:, None]
        * (jnp.exp(logits - norm_student[:, None]) - jnp.exp(teacher - norm_teacher[:, None]))
    ).astype(bf16)
    d_final = dot(d_logits, head_weight).astype(bf16)
    d_final = jnp.transpose(
        d_final.reshape(dp_size, masked_rows, 4, 2, cols), (3, 0, 2, 1, 4)
    ).reshape(-1, masked_rows, cols)
    d_own = jnp.sum(exchange(d_final, ALL).astype(f32), axis=0).astype(bf16)
    d_own = jnp.transpose(spread(d_own, LINE).reshape(line, masked_rows, cols), (1, 0, 2)).reshape(
        masked_rows, width
    )
    rows = lax.dynamic_slice_in_dim(all_rows, dp_index * masked_rows, masked_rows, 0)
    grad_rows = norm_back(rows.astype(f32), d_own.astype(f32)).astype(bf16)

    d_mixed = dot(grad_rows, w_out[1]).astype(bf16).reshape(micro, MASKED, heads, HD)
    d_scores = score_back(probs1, v1, d_mixed)
    d_q = jnp.einsum("shqk,skhd->sqhd", d_scores, k1, preferred_element_type=f32)
    d_k = jnp.einsum("shqk,sqhd->skhd", d_scores, q1, preferred_element_type=f32)
    d_v = jnp.einsum("shqk,sqhd->skhd", probs1.astype(bf16), d_mixed, preferred_element_type=f32)
    d_q = rotate(d_q.astype(bf16).astype(f32), mask_cos, -mask_sin).astype(bf16)
    d_q = dot_tn(pick_all, d_q.reshape(masked_rows, half)).astype(bf16)
    d_k = rotate(d_k.astype(bf16).astype(f32), cosine, -sine).astype(bf16).reshape(tokens, half)
    d_v = d_v.astype(bf16).reshape(tokens, half)
    d_normed = sum_rows(dot_nt(jnp.concatenate([d_q, d_k, d_v], axis=1), w_qkv[1]))
    own_pick = lax.dynamic_slice_in_dim(pick_all, place * chunk_rows, chunk_rows, 1)
    grad_own = dot_tn(own_pick, grad_rows)
    grad_own = (grad_own + norm_back(own_rows(hidden1).astype(f32), d_normed)).astype(bf16)
    grad = spread(grad_own, LINE).reshape(tokens, width)

    d_mixed = dot(grad, w_out[0]).astype(bf16).reshape(micro, seq_len, heads, HD)
    d_scores = score_back(probs0, v0, d_mixed)
    d_q = jnp.einsum("shqk,skhd->sqhd", d_scores[:, :, :slots], k0, preferred_element_type=f32)
    d_k = jnp.einsum("shqk,sqhd->skhd", d_scores[..., :slots], q0, preferred_element_type=f32)
    d_v = jnp.einsum(
        "shqk,sqhd->skhd", probs0[..., :slots].astype(bf16), d_mixed, preferred_element_type=f32
    )
    cos_top, sin_top = cosine[:, :slots], sine[:, :slots]
    d_q = rotate(d_q.astype(bf16).astype(f32), cos_top, -sin_top).astype(bf16)
    d_k = rotate(d_k.astype(bf16).astype(f32), cos_top, -sin_top).astype(bf16)
    cells = micro * slots
    d_all = jnp.concatenate(
        [d_q.reshape(cells, half), d_k.reshape(cells, half), d_v.astype(bf16).reshape(cells, half)],
        axis=1,
    )
    partial = dot_nt(d_all, w_qkv[0]).astype(bf16)
    top_hidden = jnp.concatenate(
        [hidden0[i * seq_len : i * seq_len + slots] for i in range(micro)], axis=0
    ).astype(f32)
    top_grad = jnp.concatenate(
        [grad[i * seq_len : i * seq_len + slots] for i in range(micro)], axis=0
    )
    along = jnp.mean(partial.astype(f32) * top_hidden, axis=1)
    along_high = along.astype(bf16)
    along_low = (along - along_high.astype(f32)).astype(bf16)
    extra = jnp.zeros((8, cols), bf16)
    extra = extra.at[0, :cells].set(along_high).at[1, :cells].set(along_low)
    chunks = jnp.concatenate(
        [
            jnp.transpose(partial.reshape(cells, line, cols), (1, 0, 2)),
            jnp.broadcast_to(extra[None], (line,) + extra.shape),
        ],
        axis=1,
    )
    summed = jnp.sum(exchange(chunks, LINE).astype(f32), axis=0)
    d_normed = summed[:cells]
    along = (summed[cells, :cells] + summed[cells + 1, :cells])[:, None]
    factor = inverse_rms(top_hidden)
    hidden_cols = lax.dynamic_slice_in_dim(top_hidden, place * cols, cols, 1)
    grad_cols = lax.dynamic_slice_in_dim(top_grad, place * cols, cols, 1).astype(f32)
    new_grad = (grad_cols + factor * d_normed - hidden_cols * factor**3 * along).astype(bf16)
    d_image = jnp.concatenate(
        [
            dot_tn(placings[i], new_grad[i * slots : (i + 1) * slots]).astype(bf16)
            for i in range(micro)
        ],
        axis=0,
    )
    proj_part = dot_tn(encoded, d_image).astype(bf16)
    owners = 2 * dp_size
    parts = exchange(proj_part.reshape(owners, depth // owners, cols), ("segment", "dp"))
    parts = jnp.sum(parts.astype(f32).reshape(2, dp_size, depth // owners, cols), axis=1)
    projector_grad = jnp.transpose(parts, (1, 0, 2)).reshape(depth // owners, 2 * cols)
    return (loss, projector_grad)


def solution(mesh):
    placed = (
        P(None, "dp", None, None),
        P(None, "dp", None, None),
        P(),
        P(None, "dp"),
        P(None, "dp", None),
        P(None, "dp", None),
        P(),
        P(None, None, "vocab"),
        P(None, "vocab", None),
        P(None, "vocab"),
        P("segment", None, "dp", "vocab"),
        P("segment", "vocab", "dp"),
        P(("segment", "dp", "vocab"), None),
        P(None, ("segment", "dp", "vocab")),
    )
    return jax.shard_map(
        shards,
        mesh=mesh,
        in_specs=placed,
        out_specs=(P(), P(("segment", "dp"), "vocab")),
        check_vma=False,
    )
```

```python
import functools

import jax
import jax.numpy as jnp
from jax import lax
from jax.experimental import pallas as pl
from jax.experimental.pallas import tpu as pltpu
from jax.sharding import PartitionSpec as P

HD = 128
MASKED = 4
RATIOS = 8

epsilon = 1e-06
rope_base = 500000.0

LINE = ("vocab", "segment")
ALL = ("segment", "dp", "vocab")
f32 = jnp.float32
bf16 = jnp.bfloat16


def dot(a, b):
    return jnp.dot(a, b, preferred_element_type=f32)


def dot_nt(a, b):
    return lax.dot_general(a, b, (((1,), (1,)), ((), ())), preferred_element_type=f32)


def dot_tn(a, b):
    return lax.dot_general(a, b, (((0,), (0,)), ((), ())), preferred_element_type=f32)


def swap(block, axis, mask):
    return lax.ppermute(block, axis, [(i, i ^ mask) for i in range(lax.axis_size(axis))])


def exchange(chunks, axes):
    return lax.all_to_all(chunks, axes, 0, 0, tiled=True)


def spread(block, axes):
    size = lax.axis_size(axes)
    return exchange(jnp.broadcast_to(block[None], (size,) + block.shape), axes)


def inverse_rms(values_in):
    return lax.rsqrt(jnp.mean(values_in * values_in, axis=-1, keepdims=True) + epsilon)


def norm_rows(values_in):
    return values_in * inverse_rms(values_in)


def layer_norm(values_in):
    centred = values_in - jnp.mean(values_in, axis=-1, keepdims=True)
    return centred * lax.rsqrt(jnp.mean(centred * centred, axis=-1, keepdims=True) + epsilon)


def norm_back(values_in, cotangent):
    factor = inverse_rms(values_in)
    return factor * cotangent - values_in * factor**3 * jnp.mean(
        cotangent * values_in, axis=-1, keepdims=True
    )


SIDE = ("dp", "vocab")
TOKENS = ("segment", "vocab")


def in_vmem():
    return pl.BlockSpec(memory_space=pltpu.VMEM)


def call(body, name, outs, *args, smem=0):
    specs = [
        pl.BlockSpec(memory_space=pltpu.SMEM) if i < smem else in_vmem() for i in range(len(args))
    ]
    return pl.pallas_call(
        body,
        name=name,
        out_shape=[jax.ShapeDtypeStruct(shape, kind) for shape, kind in outs],
        in_specs=specs,
        out_specs=[in_vmem() for _ in outs],
        compiler_params=pltpu.CompilerParams(vmem_limit_bytes=56 << 20),
    )(*args)


def side_shift(block, step, first):
    sizes = (lax.axis_size("dp"), lax.axis_size("vocab"))
    edge = 4
    route = []
    for dp in range(sizes[0]):
        z, y = divmod(dp, edge)
        for v in range(sizes[1]):
            if (v % 2 == 0) == first:
                to = z * edge + (y + step) % edge
            else:
                to = ((z + step) % edge) * edge + y
            route.append((dp * sizes[1] + v, to * sizes[1] + v))
    return lax.ppermute(block, SIDE, route)


def line_move(block, lo, hi):
    count = lax.axis_size("vocab")
    route = [
        (s * count + v, (s ^ lo) * count + (v ^ (2 * hi)))
        for s in range(lax.axis_size("segment"))
        for v in range(count)
    ]
    return lax.ppermute(block, TOKENS, route)


def sum_rows(partial, core, chip):
    rows, width = partial.shape
    halves = partial.reshape(2, rows // 2, width)
    other = lax.dynamic_index_in_dim(halves, 1 - core, 0, False)
    mine = lax.dynamic_index_in_dim(halves, core, 0, False)
    both = (mine.astype(f32) + swap(other, "vocab", 1).astype(f32)).astype(bf16)
    both = both.reshape(4, rows // 8, width)

    def piece(mask):
        return lax.dynamic_index_in_dim(both, chip ^ mask, 0, False)

    moved = [line_move(piece(m), m & 1, m >> 1) for m in (1, 2, 3)]
    return (piece(0).astype(f32) + moved[0].astype(f32)) + (
        moved[1].astype(f32) + moved[2].astype(f32)
    )


def spread_rows(block, core, chip):
    rows, width = block.shape
    pieces = [block] + [line_move(block, m & 1, m >> 1) for m in (1, 2, 3)]
    half = jnp.zeros((4, rows, width), block.dtype)
    for mask in range(4):
        half = lax.dynamic_update_slice(half, pieces[mask][None], (chip ^ mask, 0, 0))
    other = swap(half, "vocab", 1)
    whole = jnp.zeros((2, 4, rows, width), block.dtype)
    whole = lax.dynamic_update_slice(whole, half[None], (core, 0, 0, 0))
    whole = lax.dynamic_update_slice(whole, other[None], (1 - core, 0, 0, 0))
    return whole.reshape(8 * rows, width)


def prepare(counts, order, masks, up, down, up_out, down_out, placing_out, pick_out, masked_out):
    up_out[...] = up[...].reshape(up_out.shape)
    down_out[...] = down[...].reshape(down_out.shape)
    micro, slots, _ = placing_out.shape
    images = order.shape[1]
    each = slots // images
    cell = lax.broadcasted_iota(jnp.int32, (slots, slots), 0)
    slot = lax.broadcasted_iota(jnp.int32, (slots, slots), 1)
    tokens = pick_out.shape[1]
    seq_len = tokens // micro
    row = lax.broadcasted_iota(jnp.int32, pick_out.shape, 0)
    column = lax.broadcasted_iota(jnp.int32, pick_out.shape, 1)
    token = lax.broadcasted_iota(jnp.int32, masked_out.shape, 0)
    pick = jnp.zeros(pick_out.shape, f32)
    masked = jnp.zeros(masked_out.shape, f32)
    for m in range(micro):
        hit = jnp.zeros((slots, slots), f32)
        for i in range(images):
            within = slot - i * each
            inside = (within >= 0) & (within < each) & (cell == order[m, i] * each + within)
            live = jnp.where(i < counts[m, 0], 1.0, 0.0)
            hit = jnp.where(inside, live, hit)
        placing_out[m] = hit.astype(bf16)
        for p in range(MASKED):
            where = m * seq_len + masks[m, p]
            pick = jnp.where((row == m * MASKED + p) & (column == where), 1.0, pick)
            masked = jnp.where(token == where, 1.0, masked)
    pick_out[...] = pick.astype(bf16)
    masked_out[...] = masked


def add_parts(x, parts):
    total = parts[0][...].astype(f32) + parts[1][...].astype(f32)
    total = total + (parts[2][...].astype(f32) + parts[3][...].astype(f32))
    return (x[...].astype(f32) + total).astype(bf16)


def mlp(layer, layers, current, up, down):
    normed = layer_norm(current.astype(f32)).astype(bf16)
    inner = dot_nt(normed, up[...])
    mine = lax.broadcasted_iota(jnp.int32, inner.shape, 1) % layers == layer
    inner = jnp.where(mine, jax.nn.gelu(inner, approximate=True), 0.0).astype(bf16)
    return dot(inner, down[...]).astype(bf16)


def encode_first(layers, x, up, down, part):
    part[...] = mlp(0, layers, x[...], up, down)


def encode_next(layer, layers, x, p0, p1, p2, p3, up, down, part, current):
    now = add_parts(x, (p0, p1, p2, p3))
    current[...] = now
    part[...] = mlp(layer, layers, now, up, down)


def encode_last(x, p0, p1, p2, p3, projector, current, columns):
    now = add_parts(x, (p0, p1, p2, p3))
    current[...] = now
    columns[...] = dot(now, projector[...]).astype(bf16)


def turn(values, cosine, sine):
    return values * cosine + pltpu.roll(values, HD // 2, 1) * sine


def softmax(scores):
    powers = jnp.exp(scores - jnp.max(scores, axis=-1, keepdims=True))
    return powers / jnp.sum(powers, axis=-1, keepdims=True)


def project_heads(hidden, w, cosine, sine, q_out, k_out, v_out):
    half = q_out.shape[1]
    normed = norm_rows(hidden.astype(f32)).astype(bf16)
    all_heads = dot(normed, w[:, : 3 * half])
    tokens = hidden.shape[0]
    seq_len = cosine.shape[0]
    for m in range(tokens // seq_len):
        rows = slice(m * seq_len, (m + 1) * seq_len)
        for h in range(half // HD):
            cols = slice(h * HD, (h + 1) * HD)
            q = all_heads[rows, h * HD : (h + 1) * HD]
            k = all_heads[rows, half + h * HD : half + (h + 1) * HD]
            q_out[rows, cols] = turn(q, cosine[...], sine[...]).astype(bf16)
            k_out[rows, cols] = turn(k, cosine[...], sine[...]).astype(bf16)
    v_out[...] = all_heads[:, 2 * half :].astype(bf16)


def attend(q, k, v):
    probs = softmax(dot_nt(q, k) * HD ** (-0.5))
    return dot(probs.astype(bf16), v).astype(bf16)


def attend_back(q, k, v, d_mixed):
    probs = softmax(dot_nt(q, k) * HD ** (-0.5))
    d_probs = dot_nt(d_mixed, v).astype(bf16).astype(f32)
    d_scores = probs * (d_probs - jnp.sum(probs * d_probs, axis=-1, keepdims=True))
    return (d_scores * HD ** (-0.5)).astype(bf16), probs.astype(bf16)


def first_section(
    images, text, mask_row, placing, masked, w, cosine, sine, hidden, q, k, v, partial, mixed
):
    micro, slots, _ = placing.shape
    seq_len = cosine.shape[0]
    tokens, width = hidden.shape
    blocks = images.shape[0] // micro
    part = width // blocks
    half = q.shape[1]
    for m in range(micro):
        rows = slice(m * seq_len, (m + 1) * seq_len)
        hidden[rows, :] = jnp.where(masked[rows, :] > 0.0, mask_row[...], text[m])
        place = placing[m]
        filled = jnp.sum(place.astype(f32), axis=1, keepdims=True) > 0.0
        for b in range(blocks):
            placed = dot(place, images[m * blocks + b]).astype(bf16)
            cols = slice(b * part, (b + 1) * part)
            hidden[m * seq_len : m * seq_len + slots, cols] = jnp.where(
                filled, placed, text[m, :slots, cols]
            )
    project_heads(hidden[...], w, cosine, sine, q, k, v)
    for m in range(micro):
        rows = slice(m * seq_len, (m + 1) * seq_len)
        for h in range(half // HD):
            cols = slice(h * HD, (h + 1) * HD)
            mixed[rows, cols] = attend(q[rows, cols], k[rows, cols], v[rows, cols])
    partial[...] = dot_nt(mixed[...], w[:, 3 * half :]).astype(bf16)


def last_section(hidden, pick, w, cosine, sine, q, k, v, partial, picked, q_all, mixed):
    half = k.shape[1]
    seq_len = cosine.shape[0]
    project_heads(hidden[...], w, cosine, sine, q_all, k, v)
    for m in range(hidden.shape[0] // seq_len):
        rows = slice(m * seq_len, (m + 1) * seq_len)
        mine = slice(m * MASKED, (m + 1) * MASKED)
        q_mine = dot(pick[...], q_all[...]).astype(bf16)[mine]
        q[mine, :] = q_mine
        for h in range(half // HD):
            cols = slice(h * HD, (h + 1) * HD)
            mixed[mine, cols] = attend(q_mine[:, cols], k[rows, cols], v[rows, cols])
    partial[...] = dot_nt(mixed[...], w[:, 3 * half :]).astype(bf16)
    picked[...] = dot(pick[...], hidden[...])


def last_section_back(grad, pick, q, k, v, w, cosine, sine, partial, d_all):
    half = k.shape[1]
    seq_len = cosine.shape[0]
    d_mixed = dot(grad[...], w[:, 3 * half :]).astype(bf16)
    for m in range(k.shape[0] // seq_len):
        rows = slice(m * seq_len, (m + 1) * seq_len)
        mine = slice(m * MASKED, (m + 1) * MASKED)
        spot = pick[mine, rows]
        for h in range(half // HD):
            cols = slice(h * HD, (h + 1) * HD)
            q_h, k_h, d_h = q[mine, cols], k[rows, cols], d_mixed[mine, cols]
            d_scores, probs = attend_back(q_h, k_h, v[rows, cols], d_h)
            d_q = dot_tn(spot, dot(d_scores, k_h).astype(bf16))
            d_k = dot_tn(d_scores, q_h).astype(bf16).astype(f32)
            d_v = dot_tn(probs, d_h)
            for part, d in enumerate(
                (turn(d_q, cosine[...], -sine[...]), turn(d_k, cosine[...], -sine[...]), d_v)
            ):
                at = part * half + h * HD
                d_all[rows, at : at + HD] = d.astype(bf16)
    partial[...] = dot_nt(d_all[...], w[:, : 3 * half]).astype(bf16)


def first_section_back(
    slots, grad, hidden, q, k, v, w, cosine, sine, partial, along, d_all
):
    half = k.shape[1]
    seq_len = cosine.shape[0]
    d_mixed = dot(grad[...], w[:, 3 * half :]).astype(bf16)
    micro = k.shape[0] // seq_len
    cos_top, sin_top = cosine[:slots, :], -sine[:slots, :]
    for m in range(micro):
        rows = slice(m * seq_len, (m + 1) * seq_len)
        top = slice(m * slots, (m + 1) * slots)
        for h in range(half // HD):
            cols = slice(h * HD, (h + 1) * HD)
            q_h, k_h, d_h = q[rows, cols], k[rows, cols], d_mixed[rows, cols]
            d_scores, probs = attend_back(q_h, k_h, v[rows, cols], d_h)
            d_q = dot(d_scores, k_h)[:slots].astype(bf16).astype(f32)
            d_k = dot_tn(d_scores, q_h)[:slots].astype(bf16).astype(f32)
            d_v = dot_tn(probs, d_h)[:slots]
            for part, d in enumerate(
                (turn(d_q, cos_top, sin_top), turn(d_k, cos_top, sin_top), d_v)
            ):
                at = part * half + h * HD
                d_all[top, at : at + HD] = d
    rounded = dot_nt(d_all[...].astype(bf16), w[:, : 3 * half]).astype(bf16)
    partial[...] = rounded
    for m in range(micro):
        top = slice(m * slots, (m + 1) * slots)
        own = hidden[m * seq_len : m * seq_len + slots, :].astype(f32)
        along[top, :] = jnp.mean(rounded[top, :].astype(f32) * own, axis=1, keepdims=True)


def collect(targets, near, ahead, far_low, far_high, behind, out, sems):
    rows = near.shape[1]
    copies = []
    sources = [near.at[i] for i in range(4)] + [ahead.at[i] for i in range(4)]
    sources += [far_low.at[0], far_low.at[1], far_high.at[0], far_high.at[1]]
    sources += [behind.at[i] for i in range(4)]
    for i, source in enumerate(sources):
        start = pl.multiple_of(targets[i] * rows, rows)
        copies.append(pltpu.make_async_copy(source, out.at[pl.ds(start, rows)], sems.at[i]))
    for copy in copies:
        copy.start()
    for copy in copies:
        copy.wait()


def collected(targets, near, ahead, far_low, far_high, behind):
    rows, cols = near.shape[1:]
    return pl.pallas_call(
        collect,
        name="collect",
        out_shape=jax.ShapeDtypeStruct((16 * rows, cols), near.dtype),
        in_specs=[pl.BlockSpec(memory_space=pltpu.SMEM)]
        + [pl.BlockSpec(memory_space=pl.ANY)] * 5,
        out_specs=pl.BlockSpec(memory_space=pl.ANY),
        scratch_shapes=[pltpu.SemaphoreType.DMA((16,))],
    )(targets, near, ahead, far_low, far_high, behind)


def gather_weights(sections, dp_index, core):
    both = jnp.stack(sections)
    behind = side_shift(both, 1, True)
    ahead = side_shift(both, -1, True)
    far = [side_shift(behind[0], 1, True), side_shift(ahead[1], -1, True)]
    z, y = dp_index // 4, dp_index % 4
    step = jnp.arange(4, dtype=jnp.int32)
    outer = jnp.where(core == 0, z, y)
    inner = jnp.where(core == 0, y, z)
    outer = ((outer + step) % 4)[:, None]
    inner = ((inner + step) % 4)[None, :]
    targets = jnp.where(core == 0, outer * 4 + inner, inner * 4 + outer).reshape(-1)
    whole = []
    for s in range(2):
        near = jnp.stack([both[s], ahead[s], far[s], behind[s]])
        from_behind = side_shift(near, 1, False)
        from_ahead = side_shift(near, -1, False)
        low = side_shift(from_behind[:2], 1, False)
        high = side_shift(from_ahead[2:], -1, False)
        whole.append(collected(targets, near, from_ahead, low, high, from_behind))
    return whole


def shards(
    patches,
    text_embed,
    mask_embed,
    image_counts,
    image_order,
    masked_positions,
    ratio_index,
    enc_up,
    enc_down,
    projector,
    lang_qkv,
    lang_out,
    head_weight,
    teacher_logits,
):
    segment = lax.axis_index("segment")
    dp_index = lax.axis_index("dp")
    place = lax.axis_index("vocab") * 2 + segment
    core = lax.axis_index("vocab") % 2
    chip = (lax.axis_index("vocab") // 2) * 2 + segment
    line = lax.axis_size(LINE)
    dp_size = lax.axis_size("dp")
    micro = text_embed.shape[0]
    seq_len, width = text_embed.shape[2:]
    slots = patches.shape[2]
    depth = patches.shape[3]

    shard = jnp.concatenate(
        [lang_qkv[0], jnp.transpose(lang_out[0])[None]], axis=0
    )
    half = shard.shape[2] // 2
    rows_here = shard.shape[1]
    low, high = shard[:, :, :half], shard[:, :, half:]
    keep = jnp.where(segment == 0, low, high)
    give = jnp.where(segment == 0, high, low)
    got = swap(give, "segment", 1)
    sections = (
        jnp.where(segment == 0, keep, got),
        jnp.where(segment == 0, got, keep),
    )
    w_first, w_last = gather_weights(
        [jnp.transpose(part, (1, 0, 2)).reshape(rows_here, 4 * half) for part in sections],
        dp_index,
        core,
    )

    layers, _, hidden_units = enc_up.shape
    tokens = micro * seq_len
    masked_rows = micro * MASKED
    up, down, placing, pick_all, masked = call(
        prepare,
        "prepare",
        [
            ((layers * hidden_units, depth), bf16),
            ((layers * hidden_units, depth), bf16),
            ((micro, slots, slots), bf16),
            ((masked_rows, tokens), bf16),
            ((tokens, 1), f32),
        ],
        image_counts,
        image_order[:, 0],
        masked_positions[:, 0],
        jnp.transpose(enc_up, (2, 0, 1)),
        jnp.transpose(enc_down, (1, 0, 2)),
        smem=3,
    )

    def parts_of(part):
        return [part] + [swap(part, "vocab", mask) for mask in (1, 2, 3)]

    small = ((slots, depth), bf16)
    current = lax.dynamic_index_in_dim(patches[:, 0], segment, 0, False)
    (part,) = call(
        functools.partial(encode_first, layers), "encode_first", [small], current, up, down
    )
    for layer in range(1, layers):
        part, current = call(
            functools.partial(encode_next, layer, layers),
            "encode_next",
            [small, small],
            current,
            *parts_of(part),
            up,
            down,
        )
    encoded_own, image_cols = call(
        encode_last,
        "encode_last",
        [small, ((slots, projector.shape[1]), bf16)],
        current,
        *parts_of(part),
        projector,
    )
    images = spread(image_cols, TOKENS).reshape(line, slots, projector.shape[1])
    encoded_other = swap(encoded_own, "segment", 1)
    encoded = jnp.concatenate(
        [
            jnp.where(segment == 0, encoded_own, encoded_other),
            jnp.where(segment == 0, encoded_other, encoded_own),
        ],
        axis=0,
    )

    angles = jnp.arange(seq_len, dtype=f32)[:, None] * (
        rope_base ** (-2.0 * jnp.arange(HD // 2, dtype=f32) / HD)
    )
    cosine = jnp.concatenate([jnp.cos(angles), jnp.cos(angles)], axis=1)
    sine = jnp.concatenate([-jnp.sin(angles), jnp.sin(angles)], axis=1)
    chunk_rows = tokens // line
    row_start = (core * 4 + chip) * chunk_rows
    whole = ((tokens, width), bf16)
    heads = ((tokens, half), bf16)

    def own_rows(array):
        return lax.dynamic_slice_in_dim(array, row_start, chunk_rows, 0)

    hidden0, q0, k0, v0, partial, _ = call(
        first_section,
        "first_section",
        [whole, heads, heads, heads, whole, heads],
        images,
        text_embed[:, 0],
        mask_embed[None, :],
        placing,
        masked,
        w_first,
        cosine,
        sine,
    )
    mine = (own_rows(hidden0).astype(f32) + sum_rows(partial, core, chip)).astype(bf16)
    hidden1 = spread_rows(mine, core, chip)

    few_heads = ((masked_rows, half), bf16)
    q1, k1, v1, partial, picked, _, _ = call(
        last_section,
        "last_section",
        [
            few_heads,
            heads,
            heads,
            ((masked_rows, width), bf16),
            ((masked_rows, width), f32),
            heads,
            few_heads,
        ],
        hidden1,
        pick_all,
        w_last,
        cosine,
        sine,
    )
    cols = width // line
    parts = exchange(
        jnp.transpose(partial.reshape(masked_rows, line, cols), (1, 0, 2)), LINE
    )
    picked = lax.dynamic_slice_in_dim(picked, place * cols, cols, 1)
    last = (picked + jnp.sum(parts.astype(f32), axis=0)).astype(bf16)

    all_rows = spread(last, ALL).reshape(2, dp_size, 4, masked_rows, cols)
    all_rows = jnp.transpose(all_rows, (1, 3, 2, 0, 4)).reshape(dp_size * masked_rows, width)
    row_count = all_rows.shape[0]
    final = norm_rows(all_rows.astype(f32)).astype(bf16)
    logits = dot_nt(final, head_weight)

    teacher = (
        jnp.transpose(teacher_logits.reshape(micro, dp_size, MASKED, -1), (1, 0, 2, 3))
        .reshape(row_count, -1)
        .astype(f32)
    )
    top = jnp.max(teacher, axis=1)
    powers = jnp.exp(teacher - top[:, None])
    stats = jnp.stack(
        [
            jnp.sum(jnp.exp(logits), axis=1),
            top,
            jnp.sum(powers, axis=1),
            jnp.sum(powers * (teacher - logits), axis=1),
        ]
    )
    stats = spread(stats, ALL).reshape(-1, 4, row_count)
    sum_student = jnp.sum(stats[:, 0], axis=0)
    top_all = jnp.max(stats[:, 1], axis=0)
    scale = jnp.exp(stats[:, 1] - top_all[None])
    sum_teacher = jnp.sum(stats[:, 2] * scale, axis=0)
    cross = jnp.sum(stats[:, 3] * scale, axis=0)
    norm_student = jnp.log(sum_student)
    norm_teacher = top_all + jnp.log(sum_teacher)
    divergence = cross / sum_teacher - norm_teacher + norm_student
    ratio = RATIOS / ratio_index.astype(f32)
    row_weights = jnp.repeat(jnp.transpose(ratio), MASKED, axis=1).reshape(-1)
    total = micro * dp_size
    loss = jnp.sum(row_weights * divergence) / total
    d_logits = (
        (row_weights / total)[:, None]
        * (jnp.exp(logits - norm_student[:, None]) - jnp.exp(teacher - norm_teacher[:, None]))
    ).astype(bf16)
    d_final = dot(d_logits, head_weight).astype(bf16)
    d_final = jnp.transpose(
        d_final.reshape(dp_size, masked_rows, 4, 2, cols), (3, 0, 2, 1, 4)
    ).reshape(-1, masked_rows, cols)
    d_own = jnp.sum(exchange(d_final, ALL).astype(f32), axis=0).astype(bf16)
    d_own = jnp.transpose(spread(d_own, LINE).reshape(line, masked_rows, cols), (1, 0, 2)).reshape(
        masked_rows, width
    )
    rows = lax.dynamic_slice_in_dim(all_rows, dp_index * masked_rows, masked_rows, 0)
    grad_rows = norm_back(rows.astype(f32), d_own.astype(f32)).astype(bf16)

    partial, _ = call(
        last_section_back,
        "last_section_back",
        [whole, ((tokens, 3 * half), bf16)],
        grad_rows,
        pick_all,
        q1,
        k1,
        v1,
        w_last,
        cosine,
        sine,
    )
    d_normed = sum_rows(partial, core, chip)
    own_pick = lax.dynamic_slice_in_dim(pick_all, row_start, chunk_rows, 1)
    grad_own = dot_tn(own_pick, grad_rows)
    grad_own = (grad_own + norm_back(own_rows(hidden1).astype(f32), d_normed)).astype(bf16)
    grad = spread_rows(grad_own, core, chip)

    cells = micro * slots
    partial, along, _ = call(
        functools.partial(first_section_back, slots),
        "first_section_back",
        [((cells, width), bf16), ((cells, 1), f32), ((cells, 3 * half), f32)],
        grad,
        hidden0,
        q0,
        k0,
        v0,
        w_first,
        cosine,
        sine,
    )
    along = along[:, 0]
    top_hidden = jnp.concatenate(
        [hidden0[i * seq_len : i * seq_len + slots] for i in range(micro)], axis=0
    ).astype(f32)
    top_grad = jnp.concatenate(
        [grad[i * seq_len : i * seq_len + slots] for i in range(micro)], axis=0
    )
    along_high = along.astype(bf16)
    along_low = (along - along_high.astype(f32)).astype(bf16)
    extra = jnp.zeros((8, cols), bf16)
    extra = extra.at[0, :cells].set(along_high).at[1, :cells].set(along_low)
    chunks = jnp.concatenate(
        [
            jnp.transpose(partial.reshape(cells, line, cols), (1, 0, 2)),
            jnp.broadcast_to(extra[None], (line,) + extra.shape),
        ],
        axis=1,
    )
    summed = jnp.sum(exchange(chunks, LINE).astype(f32), axis=0)
    d_normed = summed[:cells]
    along = (summed[cells, :cells] + summed[cells + 1, :cells])[:, None]
    factor = inverse_rms(top_hidden)
    hidden_cols = lax.dynamic_slice_in_dim(top_hidden, place * cols, cols, 1)
    grad_cols = lax.dynamic_slice_in_dim(top_grad, place * cols, cols, 1).astype(f32)
    new_grad = (grad_cols + factor * d_normed - hidden_cols * factor**3 * along).astype(bf16)
    d_image = jnp.concatenate(
        [
            dot_tn(placing[i], new_grad[i * slots : (i + 1) * slots]).astype(bf16)
            for i in range(micro)
        ],
        axis=0,
    )
    proj_part = dot_tn(encoded, d_image).astype(bf16)
    owners = 2 * dp_size
    parts = exchange(proj_part.reshape(owners, depth // owners, cols), ("segment", "dp"))
    parts = jnp.sum(parts.astype(f32).reshape(2, dp_size, depth // owners, cols), axis=1)
    projector_grad = jnp.transpose(parts, (1, 0, 2)).reshape(depth // owners, 2 * cols)
    return (loss, projector_grad)


def solution(mesh):
    placed = (
        P(None, "dp", None, None),
        P(None, "dp", None, None),
        P(),
        P(None, "dp"),
        P(None, "dp", None),
        P(None, "dp", None),
        P(),
        P(None, None, "vocab"),
        P(None, "vocab", None),
        P(None, "vocab"),
        P("segment", None, "dp", "vocab"),
        P("segment", "vocab", "dp"),
        P(("segment", "dp", "vocab"), None),
        P(None, ("segment", "dp", "vocab")),
    )
    return jax.shard_map(
        shards,
        mesh=mesh,
        in_specs=placed,
        out_specs=(P(), P(("segment", "dp"), "vocab")),
        check_vma=False,
    )
```

```python
import functools

import jax
import jax.numpy as jnp
from jax import lax
from jax.experimental import pallas as pl
from jax.experimental.pallas import tpu as pltpu
from jax.sharding import PartitionSpec as P

HD = 128
MASKED = 4
RATIOS = 8

epsilon = 1e-06
rope_base = 500000.0

LINE = ("vocab", "segment")
ALL = ("segment", "dp", "vocab")
f32 = jnp.float32
bf16 = jnp.bfloat16


def dot(a, b):
    return jnp.dot(a, b, preferred_element_type=f32)


def dot_nt(a, b):
    return lax.dot_general(a, b, (((1,), (1,)), ((), ())), preferred_element_type=f32)


def dot_tn(a, b):
    return lax.dot_general(a, b, (((0,), (0,)), ((), ())), preferred_element_type=f32)


def swap(block, axis, mask):
    return lax.ppermute(block, axis, [(i, i ^ mask) for i in range(lax.axis_size(axis))])


def exchange(chunks, axes):
    return lax.all_to_all(chunks, axes, 0, 0, tiled=True)


def spread(block, axes):
    size = lax.axis_size(axes)
    return exchange(jnp.broadcast_to(block[None], (size,) + block.shape), axes)


def inverse_rms(values_in):
    return lax.rsqrt(jnp.mean(values_in * values_in, axis=-1, keepdims=True) + epsilon)


def norm_rows(values_in):
    return values_in * inverse_rms(values_in)


def layer_norm(values_in):
    centred = values_in - jnp.mean(values_in, axis=-1, keepdims=True)
    return centred * lax.rsqrt(jnp.mean(centred * centred, axis=-1, keepdims=True) + epsilon)


def norm_back(values_in, cotangent):
    factor = inverse_rms(values_in)
    return factor * cotangent - values_in * factor**3 * jnp.mean(
        cotangent * values_in, axis=-1, keepdims=True
    )


SIDE = ("dp", "vocab")
TOKENS = ("segment", "vocab")


def call(body, name, outs, *args, smem=0, far=0, scratch=(), mb=0):
    specs = [pl.BlockSpec(memory_space=pltpu.SMEM)] * smem + [
        pl.BlockSpec(memory_space=pl.ANY)
    ] * far
    specs += [pl.BlockSpec(memory_space=pltpu.VMEM)] * (len(args) - len(specs))
    return pl.pallas_call(
        body,
        name=name,
        out_shape=[jax.ShapeDtypeStruct(shape, kind) for shape, kind in outs],
        in_specs=specs,
        out_specs=[pl.BlockSpec(memory_space=pltpu.VMEM) for _ in outs],
        scratch_shapes=list(scratch),
        cost_estimate=pl.CostEstimate(flops=0, bytes_accessed=mb * 1000000, transcendentals=0),
        compiler_params=pltpu.CompilerParams(vmem_limit_bytes=56 << 20),
    )(*args)


def side_shift(block, step, first):
    sizes = (lax.axis_size("dp"), lax.axis_size("vocab"))
    edge = 4
    route = []
    for dp in range(sizes[0]):
        z, y = divmod(dp, edge)
        for v in range(sizes[1]):
            if (v % 2 == 0) == first:
                to = z * edge + (y + step) % edge
            else:
                to = ((z + step) % edge) * edge + y
            route.append((dp * sizes[1] + v, to * sizes[1] + v))
    return lax.ppermute(block, SIDE, route)


def line_move(block, lo, hi):
    count = lax.axis_size("vocab")
    route = [
        (s * count + v, (s ^ lo) * count + (v ^ (2 * hi)))
        for s in range(lax.axis_size("segment"))
        for v in range(count)
    ]
    return lax.ppermute(block, TOKENS, route)


def sum_rows(partial, core, chip):
    rows, width = partial.shape
    halves = partial.reshape(2, rows // 2, width)
    other = lax.dynamic_index_in_dim(halves, 1 - core, 0, False)
    mine = lax.dynamic_index_in_dim(halves, core, 0, False)
    both = (mine.astype(f32) + swap(other, "vocab", 1).astype(f32)).astype(bf16)
    both = both.reshape(4, rows // 8, width)

    def piece(mask):
        return lax.dynamic_index_in_dim(both, chip ^ mask, 0, False)

    moved = [line_move(piece(m), m & 1, m >> 1) for m in (1, 2, 3)]
    return (piece(0).astype(f32) + moved[0].astype(f32)) + (
        moved[1].astype(f32) + moved[2].astype(f32)
    )


def spread_rows(block, core, chip):
    rows, width = block.shape
    pieces = [block] + [line_move(block, m & 1, m >> 1) for m in (1, 2, 3)]
    half = jnp.zeros((4, rows, width), block.dtype)
    for mask in range(4):
        half = lax.dynamic_update_slice(half, pieces[mask][None], (chip ^ mask, 0, 0))
    other = swap(half, "vocab", 1)
    whole = jnp.zeros((2, 4, rows, width), block.dtype)
    whole = lax.dynamic_update_slice(whole, half[None], (core, 0, 0, 0))
    whole = lax.dynamic_update_slice(whole, other[None], (1 - core, 0, 0, 0))
    return whole.reshape(8 * rows, width)


def prepare(counts, order, masks, placing_out, pick_out, masked_out):
    micro, slots, _ = placing_out.shape
    images = order.shape[1]
    each = slots // images
    cell = lax.broadcasted_iota(jnp.int32, (slots, slots), 0)
    slot = lax.broadcasted_iota(jnp.int32, (slots, slots), 1)
    tokens = pick_out.shape[1]
    seq_len = tokens // micro
    row = lax.broadcasted_iota(jnp.int32, pick_out.shape, 0)
    column = lax.broadcasted_iota(jnp.int32, pick_out.shape, 1)
    token = lax.broadcasted_iota(jnp.int32, masked_out.shape, 0)
    pick = jnp.zeros(pick_out.shape, f32)
    masked = jnp.zeros(masked_out.shape, f32)
    for m in range(micro):
        hit = jnp.zeros((slots, slots), f32)
        for i in range(images):
            within = slot - i * each
            inside = (within >= 0) & (within < each) & (cell == order[m, i] * each + within)
            live = jnp.where(i < counts[m, 0], 1.0, 0.0)
            hit = jnp.where(inside, live, hit)
        placing_out[m] = hit.astype(bf16)
        for p in range(MASKED):
            where = m * seq_len + masks[m, p]
            pick = jnp.where((row == m * MASKED + p) & (column == where), 1.0, pick)
            masked = jnp.where(token == where, 1.0, masked)
    pick_out[...] = pick.astype(bf16)
    masked_out[...] = masked


def add_parts(x, parts):
    total = parts[0][...].astype(f32) + parts[1][...].astype(f32)
    total = total + (parts[2][...].astype(f32) + parts[3][...].astype(f32))
    return (x[...].astype(f32) + total).astype(bf16)


def mlp(layer, layers, current, up, down):
    normed = layer_norm(current.astype(f32)).astype(bf16)
    units = up.shape[0] * layers
    inner = dot_nt(normed, up[...].reshape(units, up.shape[2]))
    mine = lax.broadcasted_iota(jnp.int32, inner.shape, 1) % layers == layer
    inner = jnp.where(mine, jax.nn.gelu(inner, approximate=True), 0.0).astype(bf16)
    return dot(inner, down[...].reshape(units, down.shape[2])).astype(bf16)


def encode_first(layers, x, up, down, part):
    part[...] = mlp(0, layers, x[...], up, down)


def encode_next(layer, layers, x, p0, p1, p2, p3, up, down, part, current):
    now = add_parts(x, (p0, p1, p2, p3))
    current[...] = now
    part[...] = mlp(layer, layers, now, up, down)


def encode_last(x, p0, p1, p2, p3, projector, current, columns):
    now = add_parts(x, (p0, p1, p2, p3))
    current[...] = now
    columns[...] = dot(now, projector[...]).astype(bf16)


def turn(values, cosine, sine):
    return values * cosine + pltpu.roll(values, HD // 2, 1) * sine


def softmax(scores):
    powers = jnp.exp(scores - jnp.max(scores, axis=-1, keepdims=True))
    return powers / jnp.sum(powers, axis=-1, keepdims=True)


def load_weights(targets, blocks, w, sems):
    rows = w.shape[1] // 16
    copies = []
    for i in range(16):
        start = pl.multiple_of(targets[i] * rows, rows)
        source = blocks[i // 2].at[i % 2]
        copies.append(pltpu.make_async_copy(source, w.at[:, pl.ds(start, rows), :], sems.at[i]))
    for copy in copies:
        copy.start()
    return copies


def wait_all(copies):
    for copy in copies:
        copy.wait()


def project_heads(hidden, w, cosine, sine, q_out, k_out, v_out, copies):
    normed = norm_rows(hidden.astype(f32)).astype(bf16)
    wait_all(copies)
    q_all, k_all, v_all = (dot(normed, w[i]) for i in range(3))
    tokens = hidden.shape[0]
    seq_len = cosine.shape[0]
    for m in range(tokens // seq_len):
        rows = slice(m * seq_len, (m + 1) * seq_len)
        for h in range(q_out.shape[1] // HD):
            cols = slice(h * HD, (h + 1) * HD)
            q, k = q_all[rows, cols], k_all[rows, cols]
            q_out[rows, cols] = turn(q, cosine[...], sine[...]).astype(bf16)
            k_out[rows, cols] = turn(k, cosine[...], sine[...]).astype(bf16)
    v_out[...] = v_all.astype(bf16)


def attend(q, k, v):
    probs = softmax(dot_nt(q, k) * HD ** (-0.5))
    return dot(probs.astype(bf16), v).astype(bf16)


def attend_back(q, k, v, d_mixed):
    probs = softmax(dot_nt(q, k) * HD ** (-0.5))
    d_probs = dot_nt(d_mixed, v).astype(bf16).astype(f32)
    d_scores = probs * (d_probs - jnp.sum(probs * d_probs, axis=-1, keepdims=True))
    return (d_scores * HD ** (-0.5)).astype(bf16), probs.astype(bf16)


def first_section(targets, *refs):
    blocks, refs = refs[:8], refs[8:]
    images, text, mask_row, placing, masked, cosine, sine = refs[:7]
    hidden, q, k, v, partial, mixed, w, sems = refs[7:]
    copies = load_weights(targets, blocks, w, sems)
    micro, slots, _ = placing.shape
    seq_len = cosine.shape[0]
    tokens, width = hidden.shape
    blocks = images.shape[0] // micro
    part = width // blocks
    half = q.shape[1]
    for m in range(micro):
        rows = slice(m * seq_len, (m + 1) * seq_len)
        hidden[rows, :] = jnp.where(masked[rows, :] > 0.0, mask_row[...], text[m])
        place = placing[m]
        filled = jnp.sum(place.astype(f32), axis=1, keepdims=True) > 0.0
        for b in range(blocks):
            placed = dot(place, images[m * blocks + b]).astype(bf16)
            cols = slice(b * part, (b + 1) * part)
            hidden[m * seq_len : m * seq_len + slots, cols] = jnp.where(
                filled, placed, text[m, :slots, cols]
            )
    project_heads(hidden[...], w, cosine, sine, q, k, v, copies)
    for m in range(micro):
        rows = slice(m * seq_len, (m + 1) * seq_len)
        for h in range(half // HD):
            cols = slice(h * HD, (h + 1) * HD)
            mixed[rows, cols] = attend(q[rows, cols], k[rows, cols], v[rows, cols])
    partial[...] = dot_nt(mixed[...], w[3]).astype(bf16)


def last_section(targets, *refs):
    blocks, refs = refs[:8], refs[8:]
    hidden, pick, cosine, sine, q, k, v, partial, picked, q_all, mixed, w, sems = refs
    copies = load_weights(targets, blocks, w, sems)
    half = k.shape[1]
    seq_len = cosine.shape[0]
    project_heads(hidden[...], w, cosine, sine, q_all, k, v, copies)
    for m in range(hidden.shape[0] // seq_len):
        rows = slice(m * seq_len, (m + 1) * seq_len)
        mine = slice(m * MASKED, (m + 1) * MASKED)
        q_mine = dot(pick[...], q_all[...]).astype(bf16)[mine]
        q[mine, :] = q_mine
        for h in range(half // HD):
            cols = slice(h * HD, (h + 1) * HD)
            mixed[mine, cols] = attend(q_mine[:, cols], k[rows, cols], v[rows, cols])
    partial[...] = dot_nt(mixed[...], w[3]).astype(bf16)
    picked[...] = dot(pick[...], hidden[...])


def last_section_back(targets, *refs):
    blocks, refs = refs[:8], refs[8:]
    grad, pick, q, k, v, cosine, sine, partial, d_all, w, sems = refs
    wait_all(load_weights(targets, blocks, w, sems))
    half = k.shape[1]
    seq_len = cosine.shape[0]
    d_mixed = dot(grad[...], w[3]).astype(bf16)
    for m in range(k.shape[0] // seq_len):
        rows = slice(m * seq_len, (m + 1) * seq_len)
        mine = slice(m * MASKED, (m + 1) * MASKED)
        spot = pick[mine, rows]
        for h in range(half // HD):
            cols = slice(h * HD, (h + 1) * HD)
            q_h, k_h, d_h = q[mine, cols], k[rows, cols], d_mixed[mine, cols]
            d_scores, probs = attend_back(q_h, k_h, v[rows, cols], d_h)
            d_q = dot_tn(spot, dot(d_scores, k_h).astype(bf16))
            d_k = dot_tn(d_scores, q_h).astype(bf16).astype(f32)
            d_v = dot_tn(probs, d_h)
            for part, d in enumerate(
                (turn(d_q, cosine[...], -sine[...]), turn(d_k, cosine[...], -sine[...]), d_v)
            ):
                at = part * half + h * HD
                d_all[rows, at : at + HD] = d.astype(bf16)
    total = dot_nt(d_all[:, :half], w[0])
    for i in (1, 2):
        total = total + dot_nt(d_all[:, i * half : (i + 1) * half], w[i])
    partial[...] = total.astype(bf16)


def first_section_back(slots, targets, *refs):
    blocks, refs = refs[:8], refs[8:]
    grad, hidden, q, k, v, cosine, sine, partial, along, d_all, w, sems = refs
    wait_all(load_weights(targets, blocks, w, sems))
    half = k.shape[1]
    seq_len = cosine.shape[0]
    d_mixed = dot(grad[...], w[3]).astype(bf16)
    micro = k.shape[0] // seq_len
    cos_top, sin_top = cosine[:slots, :], -sine[:slots, :]
    for m in range(micro):
        rows = slice(m * seq_len, (m + 1) * seq_len)
        top = slice(m * slots, (m + 1) * slots)
        for h in range(half // HD):
            cols = slice(h * HD, (h + 1) * HD)
            q_h, k_h, d_h = q[rows, cols], k[rows, cols], d_mixed[rows, cols]
            d_scores, probs = attend_back(q_h, k_h, v[rows, cols], d_h)
            d_q = dot(d_scores, k_h)[:slots].astype(bf16).astype(f32)
            d_k = dot_tn(d_scores, q_h)[:slots].astype(bf16).astype(f32)
            d_v = dot_tn(probs, d_h)[:slots]
            for part, d in enumerate(
                (turn(d_q, cos_top, sin_top), turn(d_k, cos_top, sin_top), d_v)
            ):
                at = part * half + h * HD
                d_all[top, at : at + HD] = d
    total = dot_nt(d_all[:, :half].astype(bf16), w[0])
    for i in (1, 2):
        total = total + dot_nt(d_all[:, i * half : (i + 1) * half].astype(bf16), w[i])
    rounded = total.astype(bf16)
    partial[...] = rounded
    for m in range(micro):
        top = slice(m * slots, (m + 1) * slots)
        own = hidden[m * seq_len : m * seq_len + slots, :].astype(f32)
        along[top, :] = jnp.mean(rounded[top, :].astype(f32) * own, axis=1, keepdims=True)


def slice_order(dp_index, core):
    z, y = dp_index // 4, dp_index % 4
    step = jnp.arange(4, dtype=jnp.int32)
    outer = ((jnp.where(core == 0, z, y) + step) % 4)[:, None]
    inner = ((jnp.where(core == 0, y, z) + step) % 4)[None, :]
    return jnp.where(core == 0, outer * 4 + inner, inner * 4 + outer).reshape(-1)


def second_moves(low, high):
    return (
        side_shift(low, 1, False),
        side_shift(high, -1, False),
        side_shift(high, 1, False),
        side_shift(low, -1, False),
    )


def in_order(low, high, moves):
    behind_low, ahead_high, behind_high, ahead_low = moves
    far_low = side_shift(behind_low, 1, False)
    far_high = side_shift(ahead_high, -1, False)
    return (low, high, ahead_low, ahead_high, far_low, far_high, behind_low, behind_high)


def shards(
    patches,
    text_embed,
    mask_embed,
    image_counts,
    image_order,
    masked_positions,
    ratio_index,
    enc_up,
    enc_down,
    projector,
    lang_qkv,
    lang_out,
    head_weight,
    teacher_logits,
):
    segment = lax.axis_index("segment")
    dp_index = lax.axis_index("dp")
    place = lax.axis_index("vocab") * 2 + segment
    core = lax.axis_index("vocab") % 2
    chip = (lax.axis_index("vocab") // 2) * 2 + segment
    line = lax.axis_size(LINE)
    dp_size = lax.axis_size("dp")
    micro = text_embed.shape[0]
    seq_len, width = text_embed.shape[2:]
    slots = patches.shape[2]
    depth = patches.shape[3]

    shard = jnp.concatenate(
        [lang_qkv[0], jnp.transpose(lang_out[0])[None]], axis=0
    )
    half = shard.shape[2] // 2
    low, high = shard[:, :, :half], shard[:, :, half:]
    keep = jnp.where(segment == 0, low, high)
    give = jnp.where(segment == 0, high, low)
    got = swap(give, "segment", 1)
    with_weights = dict(
        smem=1,
        far=8,
        scratch=(pltpu.VMEM((4, width, half), bf16), pltpu.SemaphoreType.DMA((16,))),
        mb=30,
    )

    layers, _, hidden_units = enc_up.shape
    tokens = micro * seq_len
    masked_rows = micro * MASKED
    placing, pick_all, masked = call(
        prepare,
        "prepare",
        [
            ((micro, slots, slots), bf16),
            ((masked_rows, tokens), bf16),
            ((tokens, 1), f32),
        ],
        image_counts,
        image_order[:, 0],
        masked_positions[:, 0],
        smem=3,
        mb=3,
    )
    up = jnp.transpose(enc_up, (2, 0, 1))
    down = jnp.transpose(enc_down, (1, 0, 2))

    def parts_of(part):
        return [part] + [swap(part, "vocab", mask) for mask in (1, 2, 3)]

    small = ((slots, depth), bf16)
    current = lax.dynamic_index_in_dim(patches[:, 0], segment, 0, False)
    (part,) = call(
        functools.partial(encode_first, layers), "encode_first", [small], current, up, down, mb=24
    )
    got, part = lax.optimization_barrier((got, part))
    first = segment == 0
    both = jnp.stack([jnp.where(first, keep, got), jnp.where(first, got, keep)])
    targets = slice_order(dp_index, core)
    behind = side_shift(both, 1, True)
    ahead = side_shift(both, -1, True)
    first_parts = parts_of(part)
    behind, ahead, first_parts = lax.optimization_barrier((behind, ahead, first_parts))
    far = [side_shift(behind[0], 1, True), side_shift(ahead[1], -1, True)]
    part, current = call(
        functools.partial(encode_next, 1, layers),
        "encode_next",
        [small, small],
        current,
        *first_parts,
        up,
        down,
        mb=24,
    )
    far, part = lax.optimization_barrier((far, part))
    low = [jnp.stack([both[s], ahead[s]]) for s in range(2)]
    high = [jnp.stack([far[s], behind[s]]) for s in range(2)]
    moves = second_moves(low[0], high[0])
    encoded_own, image_cols = call(
        encode_last,
        "encode_last",
        [small, ((slots, projector.shape[1]), bf16)],
        current,
        *parts_of(part),
        projector,
        mb=10,
    )
    early, image_cols = lax.optimization_barrier((moves[:2], image_cols))
    moves = (*early, *moves[2:])
    w_first = in_order(low[0], high[0], moves)
    w_first, low[1], high[1] = lax.optimization_barrier((w_first, low[1], high[1]))
    moves = second_moves(low[1], high[1])
    images = spread(image_cols, TOKENS).reshape(line, slots, projector.shape[1])
    encoded_other = swap(encoded_own, "segment", 1)
    encoded = jnp.concatenate(
        [
            jnp.where(segment == 0, encoded_own, encoded_other),
            jnp.where(segment == 0, encoded_other, encoded_own),
        ],
        axis=0,
    )

    angles = jnp.arange(seq_len, dtype=f32)[:, None] * (
        rope_base ** (-2.0 * jnp.arange(HD // 2, dtype=f32) / HD)
    )
    cosine = jnp.concatenate([jnp.cos(angles), jnp.cos(angles)], axis=1)
    sine = jnp.concatenate([-jnp.sin(angles), jnp.sin(angles)], axis=1)
    chunk_rows = tokens // line
    row_start = (core * 4 + chip) * chunk_rows
    whole = ((tokens, width), bf16)
    heads = ((tokens, half), bf16)

    def own_rows(array):
        return lax.dynamic_slice_in_dim(array, row_start, chunk_rows, 0)

    hidden0, q0, k0, v0, partial, _ = call(
        first_section,
        "first_section",
        [whole, heads, heads, heads, whole, heads],
        targets,
        *w_first,
        images,
        text_embed[:, 0],
        mask_embed[None, :],
        placing,
        masked,
        cosine,
        sine,
        **with_weights,
    )
    mine = (own_rows(hidden0).astype(f32) + sum_rows(partial, core, chip)).astype(bf16)
    early, mine = lax.optimization_barrier((moves[:2], mine))
    w_last = in_order(low[1], high[1], (*early, *moves[2:]))
    hidden1 = spread_rows(mine, core, chip)

    few_heads = ((masked_rows, half), bf16)
    q1, k1, v1, partial, picked, _, _ = call(
        last_section,
        "last_section",
        [
            few_heads,
            heads,
            heads,
            ((masked_rows, width), bf16),
            ((masked_rows, width), f32),
            heads,
            few_heads,
        ],
        targets,
        *w_last,
        hidden1,
        pick_all,
        cosine,
        sine,
        **with_weights,
    )
    cols = width // line
    parts = exchange(
        jnp.transpose(partial.reshape(masked_rows, line, cols), (1, 0, 2)), LINE
    )
    picked = lax.dynamic_slice_in_dim(picked, place * cols, cols, 1)
    last = (picked + jnp.sum(parts.astype(f32), axis=0)).astype(bf16)

    all_rows = spread(last, ALL).reshape(2, dp_size, 4, masked_rows, cols)
    all_rows = jnp.transpose(all_rows, (1, 3, 2, 0, 4)).reshape(dp_size * masked_rows, width)
    row_count = all_rows.shape[0]
    final = norm_rows(all_rows.astype(f32)).astype(bf16)
    logits = dot_nt(final, head_weight)

    teacher = (
        jnp.transpose(teacher_logits.reshape(micro, dp_size, MASKED, -1), (1, 0, 2, 3))
        .reshape(row_count, -1)
        .astype(f32)
    )
    top = jnp.max(teacher, axis=1)
    powers = jnp.exp(teacher - top[:, None])
    stats = jnp.stack(
        [
            jnp.sum(jnp.exp(logits), axis=1),
            top,
            jnp.sum(powers, axis=1),
            jnp.sum(powers * (teacher - logits), axis=1),
        ]
    )
    stats = spread(stats, ALL).reshape(-1, 4, row_count)
    sum_student = jnp.sum(stats[:, 0], axis=0)
    top_all = jnp.max(stats[:, 1], axis=0)
    scale = jnp.exp(stats[:, 1] - top_all[None])
    sum_teacher = jnp.sum(stats[:, 2] * scale, axis=0)
    cross = jnp.sum(stats[:, 3] * scale, axis=0)
    norm_student = jnp.log(sum_student)
    norm_teacher = top_all + jnp.log(sum_teacher)
    divergence = cross / sum_teacher - norm_teacher + norm_student
    ratio = RATIOS / ratio_index.astype(f32)
    row_weights = jnp.repeat(jnp.transpose(ratio), MASKED, axis=1).reshape(-1)
    total = micro * dp_size
    loss = jnp.sum(row_weights * divergence) / total
    d_logits = (
        (row_weights / total)[:, None]
        * (jnp.exp(logits - norm_student[:, None]) - jnp.exp(teacher - norm_teacher[:, None]))
    ).astype(bf16)
    d_final = dot(d_logits, head_weight).astype(bf16)
    d_final = jnp.transpose(
        d_final.reshape(dp_size, masked_rows, 4, 2, cols), (3, 0, 2, 1, 4)
    ).reshape(-1, masked_rows, cols)
    d_own = jnp.sum(exchange(d_final, ALL).astype(f32), axis=0).astype(bf16)
    d_own = jnp.transpose(spread(d_own, LINE).reshape(line, masked_rows, cols), (1, 0, 2)).reshape(
        masked_rows, width
    )
    rows = lax.dynamic_slice_in_dim(all_rows, dp_index * masked_rows, masked_rows, 0)
    grad_rows = norm_back(rows.astype(f32), d_own.astype(f32)).astype(bf16)

    partial, _ = call(
        last_section_back,
        "last_section_back",
        [whole, ((tokens, 3 * half), bf16)],
        targets,
        *w_last,
        grad_rows,
        pick_all,
        q1,
        k1,
        v1,
        cosine,
        sine,
        **with_weights,
    )
    d_normed = sum_rows(partial, core, chip)
    own_pick = lax.dynamic_slice_in_dim(pick_all, row_start, chunk_rows, 1)
    grad_own = dot_tn(own_pick, grad_rows)
    grad_own = (grad_own + norm_back(own_rows(hidden1).astype(f32), d_normed)).astype(bf16)
    grad = spread_rows(grad_own, core, chip)

    cells = micro * slots
    partial, along, _ = call(
        functools.partial(first_section_back, slots),
        "first_section_back",
        [((cells, width), bf16), ((cells, 1), f32), ((cells, 3 * half), f32)],
        targets,
        *w_first,
        grad,
        hidden0,
        q0,
        k0,
        v0,
        cosine,
        sine,
        **with_weights,
    )
    along = along[:, 0]
    top_hidden = jnp.concatenate(
        [hidden0[i * seq_len : i * seq_len + slots] for i in range(micro)], axis=0
    ).astype(f32)
    top_grad = jnp.concatenate(
        [grad[i * seq_len : i * seq_len + slots] for i in range(micro)], axis=0
    )
    along_high = along.astype(bf16)
    along_low = (along - along_high.astype(f32)).astype(bf16)
    extra = jnp.zeros((8, cols), bf16)
    extra = extra.at[0, :cells].set(along_high).at[1, :cells].set(along_low)
    chunks = jnp.concatenate(
        [
            jnp.transpose(partial.reshape(cells, line, cols), (1, 0, 2)),
            jnp.broadcast_to(extra[None], (line,) + extra.shape),
        ],
        axis=1,
    )
    summed = jnp.sum(exchange(chunks, LINE).astype(f32), axis=0)
    d_normed = summed[:cells]
    along = (summed[cells, :cells] + summed[cells + 1, :cells])[:, None]
    factor = inverse_rms(top_hidden)
    hidden_cols = lax.dynamic_slice_in_dim(top_hidden, place * cols, cols, 1)
    grad_cols = lax.dynamic_slice_in_dim(top_grad, place * cols, cols, 1).astype(f32)
    new_grad = (grad_cols + factor * d_normed - hidden_cols * factor**3 * along).astype(bf16)
    d_image = jnp.concatenate(
        [
            dot_tn(placing[i], new_grad[i * slots : (i + 1) * slots]).astype(bf16)
            for i in range(micro)
        ],
        axis=0,
    )
    proj_part = dot_tn(encoded, d_image).astype(bf16)
    owners = 2 * dp_size
    parts = exchange(proj_part.reshape(owners, depth // owners, cols), ("segment", "dp"))
    parts = jnp.sum(parts.astype(f32).reshape(2, dp_size, depth // owners, cols), axis=1)
    projector_grad = jnp.transpose(parts, (1, 0, 2)).reshape(depth // owners, 2 * cols)
    return (loss, projector_grad)


def solution(mesh):
    placed = (
        P(None, "dp", None, None),
        P(None, "dp", None, None),
        P(),
        P(None, "dp"),
        P(None, "dp", None),
        P(None, "dp", None),
        P(),
        P(None, None, "vocab"),
        P(None, "vocab", None),
        P(None, "vocab"),
        P("segment", None, "dp", "vocab"),
        P("segment", "vocab", "dp"),
        P(("segment", "dp", "vocab"), None),
        P(None, ("segment", "dp", "vocab")),
    )
    return jax.shard_map(
        shards,
        mesh=mesh,
        in_specs=placed,
        out_specs=(P(), P(("segment", "dp"), "vocab")),
        check_vma=False,
    )
```

```python
import functools

import jax
import jax.numpy as jnp
from jax import lax
from jax.experimental import pallas as pl
from jax.experimental.pallas import tpu as pltpu
from jax.sharding import PartitionSpec as P

HD = 128
MASKED = 4
RATIOS = 8

epsilon = 1e-06
rope_base = 500000.0

LINE = ("vocab", "segment")
ALL = ("segment", "dp", "vocab")
f32 = jnp.float32
bf16 = jnp.bfloat16


def dot(a, b):
    return jnp.dot(a, b, preferred_element_type=f32)


def dot_nt(a, b):
    return lax.dot_general(a, b, (((1,), (1,)), ((), ())), preferred_element_type=f32)


def dot_tn(a, b):
    return lax.dot_general(a, b, (((0,), (0,)), ((), ())), preferred_element_type=f32)


def swap(block, axis, mask):
    return lax.ppermute(block, axis, [(i, i ^ mask) for i in range(lax.axis_size(axis))])


def exchange(chunks, axes):
    return lax.all_to_all(chunks, axes, 0, 0, tiled=True)


def spread(block, axes):
    size = lax.axis_size(axes)
    return exchange(jnp.broadcast_to(block[None], (size,) + block.shape), axes)


def inverse_rms(values_in):
    return lax.rsqrt(jnp.mean(values_in * values_in, axis=-1, keepdims=True) + epsilon)


def norm_rows(values_in):
    return values_in * inverse_rms(values_in)


def layer_norm(values_in):
    centred = values_in - jnp.mean(values_in, axis=-1, keepdims=True)
    return centred * lax.rsqrt(jnp.mean(centred * centred, axis=-1, keepdims=True) + epsilon)


def norm_back(values_in, cotangent):
    factor = inverse_rms(values_in)
    return factor * cotangent - values_in * factor**3 * jnp.mean(
        cotangent * values_in, axis=-1, keepdims=True
    )


SIDE = ("dp", "vocab")
TOKENS = ("segment", "vocab")


def call(body, name, outs, *args, smem=0, far=0, scratch=(), mb=0):
    specs = [pl.BlockSpec(memory_space=pltpu.SMEM)] * smem + [
        pl.BlockSpec(memory_space=pl.ANY)
    ] * far
    specs += [pl.BlockSpec(memory_space=pltpu.VMEM)] * (len(args) - len(specs))
    return pl.pallas_call(
        body,
        name=name,
        out_shape=[jax.ShapeDtypeStruct(shape, kind) for shape, kind in outs],
        in_specs=specs,
        out_specs=[pl.BlockSpec(memory_space=pltpu.VMEM) for _ in outs],
        scratch_shapes=list(scratch),
        cost_estimate=pl.CostEstimate(flops=0, bytes_accessed=mb * 1000000, transcendentals=0),
        compiler_params=pltpu.CompilerParams(vmem_limit_bytes=56 << 20),
    )(*args)


def side_shift(block, step, first):
    sizes = (lax.axis_size("dp"), lax.axis_size("vocab"))
    edge = 4
    route = []
    for dp in range(sizes[0]):
        z, y = divmod(dp, edge)
        for v in range(sizes[1]):
            if (v % 2 == 0) == first:
                to = z * edge + (y + step) % edge
            else:
                to = ((z + step) % edge) * edge + y
            route.append((dp * sizes[1] + v, to * sizes[1] + v))
    return lax.ppermute(block, SIDE, route)


def line_move(block, lo, hi):
    count = lax.axis_size("vocab")
    route = [
        (s * count + v, (s ^ lo) * count + (v ^ (2 * hi)))
        for s in range(lax.axis_size("segment"))
        for v in range(count)
    ]
    return lax.ppermute(block, TOKENS, route)


def sum_rows(mine, give, chip):
    rows, width = mine.shape
    both = (mine.astype(f32) + swap(give, "vocab", 1).astype(f32)).astype(bf16)
    both = both.reshape(4, rows // 4, width)

    def piece(mask):
        return lax.dynamic_index_in_dim(both, chip ^ mask, 0, False)

    moved = [line_move(piece(m), m & 1, m >> 1) for m in (1, 2, 3)]
    return (piece(0).astype(f32) + moved[0].astype(f32)) + (
        moved[1].astype(f32) + moved[2].astype(f32)
    )


def spread_rows(block, chip):
    rows, width = block.shape
    pieces = [block] + [line_move(block, m & 1, m >> 1) for m in (1, 2, 3)]
    half = jnp.zeros((4, rows, width), block.dtype)
    for mask in range(4):
        half = lax.dynamic_update_slice(half, pieces[mask][None], (chip ^ mask, 0, 0))
    half = half.reshape(4 * rows, width)
    return half, swap(half, "vocab", 1)


def prepare(counts, order, masks, placing_out, pick_out, masked_out):
    micro, slots, _ = placing_out.shape
    images = order.shape[1]
    each = slots // images
    cell = lax.broadcasted_iota(jnp.int32, (slots, slots), 0)
    slot = lax.broadcasted_iota(jnp.int32, (slots, slots), 1)
    tokens = pick_out.shape[1]
    seq_len = tokens // micro
    row = lax.broadcasted_iota(jnp.int32, pick_out.shape, 0)
    column = lax.broadcasted_iota(jnp.int32, pick_out.shape, 1)
    token = lax.broadcasted_iota(jnp.int32, masked_out.shape, 0)
    pick = jnp.zeros(pick_out.shape, f32)
    masked = jnp.zeros(masked_out.shape, f32)
    for m in range(micro):
        hit = jnp.zeros((slots, slots), f32)
        for i in range(images):
            within = slot - i * each
            inside = (within >= 0) & (within < each) & (cell == order[m, i] * each + within)
            live = jnp.where(i < counts[m, 0], 1.0, 0.0)
            hit = jnp.where(inside, live, hit)
        placing_out[m] = hit.astype(bf16)
        for p in range(MASKED):
            where = m * seq_len + masks[m, p]
            pick = jnp.where((row == m * MASKED + p) & (column == where), 1.0, pick)
            masked = jnp.where(token == where, 1.0, masked)
    pick_out[...] = pick.astype(bf16)
    masked_out[...] = masked


def add_parts(x, parts):
    total = parts[0][...].astype(f32) + parts[1][...].astype(f32)
    total = total + (parts[2][...].astype(f32) + parts[3][...].astype(f32))
    return (x[...].astype(f32) + total).astype(bf16)


STEP = 272


def mlp(layer, current, up_far, down_far, up, down, sems):
    units, layers, _ = up.shape
    starts = list(range(0, units, STEP))
    copies = []
    for i, start in enumerate(starts):
        part = pl.ds(start, min(STEP, units - start))
        for j, (far, near) in enumerate(((up_far, up), (down_far, down))):
            copies.append(pltpu.make_async_copy(far.at[part], near.at[part], sems.at[i, j]))
    start_all(copies)
    normed = layer_norm(current().astype(f32)).astype(bf16)
    total = jnp.zeros(normed.shape, f32)
    for i, start in enumerate(starts):
        part = slice(start, min(start + STEP, units))
        shape = ((part.stop - start) * layers, up.shape[2])
        copies[2 * i].wait()
        inner = dot_nt(normed, up[part].reshape(shape))
        mine = lax.broadcasted_iota(jnp.int32, inner.shape, 1) % layers == layer
        inner = jnp.where(mine, jax.nn.gelu(inner, approximate=True), 0.0).astype(bf16)
        copies[2 * i + 1].wait()
        total = total + dot(inner, down[part].reshape(shape))
    return total.astype(bf16)


def encode_first(up_far, down_far, x, part, up, down, sems):
    part[...] = mlp(0, lambda: x[...], up_far, down_far, up, down, sems)


def encode_next(layer, up_far, down_far, x, p0, p1, p2, p3, part, current, up, down, sems):
    def now():
        value = add_parts(x, (p0, p1, p2, p3))
        current[...] = value
        return value

    part[...] = mlp(layer, now, up_far, down_far, up, down, sems)


def encode_last(x, p0, p1, p2, p3, projector, current, columns):
    now = add_parts(x, (p0, p1, p2, p3))
    current[...] = now
    columns[...] = dot(now, projector[...]).astype(bf16)


def turn(values, cosine, sine):
    return values * cosine + pltpu.roll(values, HD // 2, 1) * sine


def load_weights(targets, blocks, w, sems):
    rows = w.shape[1] // 16
    sources = [array.at[i] for array in blocks for i in range(array.shape[0])]
    parts = []
    for number, mats in enumerate((pl.ds(3, 1), pl.ds(0, 3))):
        copies = []
        for i, source in enumerate(sources):
            start = pl.multiple_of(targets[i] * rows, rows)
            copies.append(
                pltpu.make_async_copy(
                    source.at[mats], w.at[mats, pl.ds(start, rows), :], sems.at[number, i]
                )
            )
        parts.append(copies)
    return parts


def start_all(copies):
    for copy in copies:
        copy.start()


def wait_all(copies):
    for copy in copies:
        copy.wait()


def pairs_of(tokens, seq_len, half):
    return [
        (m, slice(m * seq_len, (m + 1) * seq_len), slice(h * HD, (h + 1) * HD))
        for m in range(tokens // seq_len)
        for h in range(half // HD)
    ]


def project_heads(hidden, w, cosine, sine, copies):
    half = w.shape[2]
    normed = norm_rows(hidden.astype(f32)).astype(bf16)
    wait_all(copies)
    q_all, k_all, v_all = (dot(normed, w[i]) for i in range(3))
    repeat = hidden.shape[0] // cosine.shape[0]
    cosine = jnp.concatenate([cosine[...]] * repeat, axis=0)
    sine = jnp.concatenate([sine[...]] * repeat, axis=0)

    def turned(values):
        return jnp.concatenate(
            [
                turn(values[:, h * HD : (h + 1) * HD], cosine, sine).astype(bf16)
                for h in range(half // HD)
            ],
            axis=1,
        )

    return turned(q_all), turned(k_all), v_all.astype(bf16)


def softmax(scores):
    powers = jnp.exp(scores - jnp.max(scores, axis=-1, keepdims=True))
    return powers / jnp.sum(powers, axis=-1, keepdims=True)


def attend(queries, keys, values):
    scores = [dot_nt(q, k) * HD ** (-0.5) for q, k in zip(queries, keys)]
    probs = [softmax(x).astype(bf16) for x in scores]
    return [dot(p, v).astype(bf16) for p, v in zip(probs, values)]


def attend_back(queries, keys, values, d_mixed):
    scores = [dot_nt(q, k) * HD ** (-0.5) for q, k in zip(queries, keys)]
    d_probs = [dot_nt(d, v).astype(bf16).astype(f32) for d, v in zip(d_mixed, values)]
    probs = [softmax(x) for x in scores]
    d_scores = [
        p * (d - jnp.sum(p * d, axis=-1, keepdims=True)) for p, d in zip(probs, d_probs)
    ]
    return (
        [(d * HD ** (-0.5)).astype(bf16) for d in d_scores],
        [p.astype(bf16) for p in probs],
    )


def split_halves(scalars, partial, keep, give):
    core, rows = scalars[16], keep.shape[0]
    keep[...] = partial[pl.ds(pl.multiple_of(core * rows, rows), rows), :]
    give[...] = partial[pl.ds(pl.multiple_of((1 - core) * rows, rows), rows), :]


def join_halves(scalars, own, other, whole):
    core, rows = scalars[16], own.shape[0]
    whole[pl.ds(pl.multiple_of(core * rows, rows), rows), :] = own[...]
    whole[pl.ds(pl.multiple_of((1 - core) * rows, rows), rows), :] = other[...]


def first_section(targets, *refs):
    blocks, refs = refs[:8], refs[8:]
    images, text, mask_row, placing, masked, cosine, sine = refs[:7]
    hidden, q, k, v, keep, give, mixed, w, sems, partial = refs[7:]
    out_copies, in_copies = load_weights(targets, blocks, w, sems)
    start_all(in_copies)
    start_all(out_copies)
    micro, slots, _ = placing.shape
    seq_len = cosine.shape[0]
    tokens, width = hidden.shape
    blocks_wide = images.shape[0] // micro
    part = width // blocks_wide
    half = q.shape[1]
    for m in range(micro):
        rows = slice(m * seq_len, (m + 1) * seq_len)
        hidden[rows, :] = jnp.where(masked[rows, :] > 0.0, mask_row[...], text[m])
        place = placing[m]
        filled = jnp.sum(place.astype(f32), axis=1, keepdims=True) > 0.0
        for b in range(blocks_wide):
            placed = dot(place, images[m * blocks_wide + b]).astype(bf16)
            cols = slice(b * part, (b + 1) * part)
            hidden[m * seq_len : m * seq_len + slots, cols] = jnp.where(
                filled, placed, text[m, :slots, cols]
            )
    q_all, k_all, v_all = project_heads(hidden[...], w, cosine, sine, in_copies)
    q[...] = q_all
    k[...] = k_all
    v[...] = v_all
    pairs = pairs_of(tokens, seq_len, half)
    results = attend(*([x[rows, cols] for _, rows, cols in pairs] for x in (q_all, k_all, v_all)))
    for (_, rows, cols), result in zip(pairs, results):
        mixed[rows, cols] = result
    wait_all(out_copies)
    partial[...] = dot_nt(mixed[...], w[3]).astype(bf16)
    split_halves(targets, partial, keep, give)


def last_section(targets, *refs):
    blocks, refs = refs[:8], refs[8:]
    own, other, pick, cosine, sine, q, k, v, partial, picked, mixed, w, sems, hidden = refs
    out_copies, in_copies = load_weights(targets, blocks, w, sems)
    start_all(in_copies)
    start_all(out_copies)
    join_halves(targets, own, other, hidden)
    picked[...] = dot(pick[...], hidden[...])
    q_all, k_all, v_all = project_heads(hidden[...], w, cosine, sine, in_copies)
    q_few = dot(pick[...], q_all).astype(bf16)
    q[...] = q_few
    k[...] = k_all
    v[...] = v_all
    pairs = pairs_of(hidden.shape[0], cosine.shape[0], k.shape[1])
    few = [slice(m * MASKED, (m + 1) * MASKED) for m, _, _ in pairs]
    results = attend(
        [q_few[mine, cols] for mine, (_, _, cols) in zip(few, pairs)],
        *([x[rows, cols] for _, rows, cols in pairs] for x in (k_all, v_all)),
    )
    for mine, (_, _, cols), result in zip(few, pairs, results):
        mixed[mine, cols] = result
    wait_all(out_copies)
    partial[...] = dot_nt(mixed[...], w[3]).astype(bf16)


def back_to_width(d_all, w):
    half = w.shape[2]
    total = dot_nt(d_all[:, :half].astype(bf16), w[0])
    for i in (1, 2):
        total = total + dot_nt(d_all[:, i * half : (i + 1) * half].astype(bf16), w[i])
    return total.astype(bf16)


def last_section_back(targets, *refs):
    blocks, refs = refs[:8], refs[8:]
    grad, pick, q, k, v, cosine, sine, keep, give, d_all, w, sems, partial = refs
    out_copies, in_copies = load_weights(targets, blocks, w, sems)
    start_all(out_copies)
    start_all(in_copies)
    half = k.shape[1]
    pairs = pairs_of(k.shape[0], cosine.shape[0], half)
    few = [slice(m * MASKED, (m + 1) * MASKED) for m, _, _ in pairs]
    queries = [q[mine, cols] for mine, (_, _, cols) in zip(few, pairs)]
    keys, values = ([x[rows, cols] for _, rows, cols in pairs] for x in (k, v))
    wait_all(out_copies)
    d_mixed = dot(grad[...], w[3]).astype(bf16)
    d_heads = [d_mixed[mine, cols] for mine, (_, _, cols) in zip(few, pairs)]
    d_scores, probs = attend_back(queries, keys, values, d_heads)
    d_q = [dot(d, k_h).astype(bf16) for d, k_h in zip(d_scores, keys)]
    d_k = [dot_tn(d, q_h).astype(bf16).astype(f32) for d, q_h in zip(d_scores, queries)]
    d_v = [dot_tn(p, d_h) for p, d_h in zip(probs, d_heads)]
    d_q = [
        dot_tn(pick[mine, rows], d) for mine, (_, rows, _), d in zip(few, pairs, d_q)
    ]
    back_sine = -sine[...]
    for i, (_, rows, cols) in enumerate(pairs):
        for part, d in enumerate(
            (turn(d_q[i], cosine[...], back_sine), turn(d_k[i], cosine[...], back_sine), d_v[i])
        ):
            at = part * half + cols.start
            d_all[rows, at : at + HD] = d.astype(bf16)
    wait_all(in_copies)
    partial[...] = back_to_width(d_all, w)
    split_halves(targets, partial, keep, give)


def first_section_back(slots, targets, *refs):
    blocks, refs = refs[:8], refs[8:]
    own, other, hidden, q, k, v, cosine, sine = refs[:8]
    chunks, grad_cols, hidden_cols, factor, d_all, w, sems, grad = refs[8:]
    join_halves(targets, own, other, grad)
    out_copies, in_copies = load_weights(targets, blocks, w, sems)
    start_all(out_copies)
    start_all(in_copies)
    half = k.shape[1]
    seq_len = cosine.shape[0]
    pairs = pairs_of(k.shape[0], seq_len, half)
    queries, keys, values = ([x[rows, cols] for _, rows, cols in pairs] for x in (q, k, v))
    wait_all(out_copies)
    d_mixed = dot(grad[...], w[3]).astype(bf16)
    d_heads = [d_mixed[rows, cols] for _, rows, cols in pairs]
    d_scores, probs = attend_back(queries, keys, values, d_heads)
    d_q = [dot(d, k_h)[:slots].astype(bf16).astype(f32) for d, k_h in zip(d_scores, keys)]
    d_k = [
        dot_tn(d, q_h)[:slots].astype(bf16).astype(f32) for d, q_h in zip(d_scores, queries)
    ]
    d_v = [dot_tn(p, d_h)[:slots] for p, d_h in zip(probs, d_heads)]
    cos_top, sin_top = cosine[:slots, :], -sine[:slots, :]
    for i, (m, _, cols) in enumerate(pairs):
        top = slice(m * slots, (m + 1) * slots)
        for part, d in enumerate(
            (turn(d_q[i], cos_top, sin_top), turn(d_k[i], cos_top, sin_top), d_v[i])
        ):
            at = part * half + cols.start
            d_all[top, at : at + HD] = d
    wait_all(in_copies)
    rounded = back_to_width(d_all, w)
    line, cells, _ = chunks.shape
    cols = grad_cols.shape[1]
    at = pl.multiple_of(targets[17] * cols, cols)
    lane = lax.broadcasted_iota(jnp.int32, (slots, chunks.shape[2] - cols), 1)
    for m in range(k.shape[0] // seq_len):
        top = slice(m * slots, (m + 1) * slots)
        rows = slice(m * seq_len, m * seq_len + slots)
        values = hidden[rows, :].astype(f32)
        mine = rounded[top, :]
        along = jnp.mean(mine.astype(f32) * values, axis=1, keepdims=True)
        high = along.astype(bf16).astype(f32)
        notes = jnp.where(lane == 0, high, jnp.where(lane == 1, along - high, 0.0)).astype(bf16)
        for c in range(line):
            chunks[c, top, :cols] = mine[:, c * cols : (c + 1) * cols]
            chunks[c, top, cols:] = notes
        factor[top, :] = inverse_rms(values)
        grad_cols[top, :] = grad[rows, pl.ds(at, cols)].astype(f32)
        hidden_cols[top, :] = hidden[rows, pl.ds(at, cols)].astype(f32)


def finish(parts, grad_cols, hidden_cols, factor, placing, encoded, out):
    cells, cols = grad_cols.shape
    total = parts[0].astype(f32)
    for c in range(1, parts.shape[0]):
        total = total + parts[c].astype(f32)
    along = total[:, cols : cols + 1] + total[:, cols + 1 : cols + 2]
    scale = factor[...]
    grad = grad_cols[...] + scale * total[:, :cols] - hidden_cols[...] * scale**3 * along
    grad = grad.astype(bf16)
    micro, slots, _ = placing.shape
    d_image = jnp.concatenate(
        [
            dot_tn(placing[m], grad[m * slots : (m + 1) * slots]).astype(bf16)
            for m in range(micro)
        ],
        axis=0,
    )
    total = dot_tn(encoded[...], d_image)
    owners, rows, _ = out.shape
    for i in range(owners):
        out[i] = total[i * rows : (i + 1) * rows].astype(bf16)


def slice_order(dp_index, core):
    z, y = dp_index // 4, dp_index % 4
    step = jnp.arange(4, dtype=jnp.int32)
    outer = ((jnp.where(core == 0, z, y) + step) % 4)[:, None]
    inner = ((jnp.where(core == 0, y, z) + step) % 4)[None, :]
    return jnp.where(core == 0, outer * 4 + inner, inner * 4 + outer).reshape(-1)


def second_moves(low, high):
    return (
        side_shift(low, 1, False),
        side_shift(high, -1, False),
        side_shift(high, 1, False),
        side_shift(low, -1, False),
    )


def in_order(low, high, moves):
    behind_low, ahead_high, behind_high, ahead_low = moves
    far_low = side_shift(behind_low, 1, False)
    far_high = side_shift(ahead_high, -1, False)
    return (low, high, ahead_low, ahead_high, far_low, far_high, behind_low, behind_high)


def shards(
    patches,
    text_embed,
    mask_embed,
    image_counts,
    image_order,
    masked_positions,
    ratio_index,
    enc_up,
    enc_down,
    projector,
    lang_qkv,
    lang_out,
    head_weight,
    teacher_logits,
):
    segment = lax.axis_index("segment")
    dp_index = lax.axis_index("dp")
    place = lax.axis_index("vocab") * 2 + segment
    core = lax.axis_index("vocab") % 2
    chip = (lax.axis_index("vocab") // 2) * 2 + segment
    line = lax.axis_size(LINE)
    dp_size = lax.axis_size("dp")
    micro = text_embed.shape[0]
    seq_len, width = text_embed.shape[2:]
    slots = patches.shape[2]
    depth = patches.shape[3]

    shard = jnp.concatenate(
        [lang_qkv[0], jnp.transpose(lang_out[0])[None]], axis=0
    )
    half = shard.shape[2] // 2
    low, high = shard[:, :, :half], shard[:, :, half:]
    keep = jnp.where(segment == 0, low, high)
    give = jnp.where(segment == 0, high, low)
    got = swap(give, "segment", 1)
    with_weights = dict(
        smem=1,
        far=8,
        scratch=(
            pltpu.VMEM((4, width, half), bf16),
            pltpu.SemaphoreType.DMA((2, 16)),
            pltpu.VMEM((micro * seq_len, width), bf16),
        ),
        mb=30,
    )

    layers, _, hidden_units = enc_up.shape
    tokens = micro * seq_len
    masked_rows = micro * MASKED
    placing, pick_all, masked = call(
        prepare,
        "prepare",
        [
            ((micro, slots, slots), bf16),
            ((masked_rows, tokens), bf16),
            ((tokens, 1), f32),
        ],
        image_counts,
        image_order[:, 0],
        masked_positions[:, 0],
        smem=3,
        mb=3,
    )
    up = jnp.transpose(enc_up, (2, 0, 1))
    down = jnp.transpose(enc_down, (1, 0, 2))

    def parts_of(part):
        return [part] + [swap(part, "vocab", mask) for mask in (1, 2, 3)]

    small = ((slots, depth), bf16)
    current = lax.dynamic_index_in_dim(patches[:, 0], segment, 0, False)
    with_layers = dict(
        far=2,
        scratch=(
            pltpu.VMEM(up.shape, bf16),
            pltpu.VMEM(down.shape, bf16),
            pltpu.SemaphoreType.DMA((-(-hidden_units // STEP), 2)),
        ),
        mb=20,
    )
    (part,) = call(encode_first, "encode_first", [small], up, down, current, **with_layers)
    got, part = lax.optimization_barrier((got, part))
    first = segment == 0
    both = jnp.stack([jnp.where(first, keep, got), jnp.where(first, got, keep)])
    targets = jnp.concatenate(
        [slice_order(dp_index, core), jnp.stack([core, place]).astype(jnp.int32)]
    )
    behind = side_shift(both, 1, True)
    ahead = side_shift(both, -1, True)
    first_parts = parts_of(part)
    behind, ahead, first_parts = lax.optimization_barrier((behind, ahead, first_parts))
    far = [side_shift(behind[0], 1, True), side_shift(ahead[1], -1, True)]
    part, current = call(
        functools.partial(encode_next, 1),
        "encode_next",
        [small, small],
        up,
        down,
        current,
        *first_parts,
        **with_layers,
    )
    far, part = lax.optimization_barrier((far, part))
    low = [jnp.stack([both[s], ahead[s]]) for s in range(2)]
    high = [jnp.stack([far[s], behind[s]]) for s in range(2)]
    moves = second_moves(low[0], high[0])
    encoded_own, image_cols = call(
        encode_last,
        "encode_last",
        [small, ((slots, projector.shape[1]), bf16)],
        current,
        *parts_of(part),
        projector,
        mb=10,
    )
    early, image_cols = lax.optimization_barrier((moves[:2], image_cols))
    moves = (*early, *moves[2:])
    w_first = in_order(low[0], high[0], moves)
    w_first, low[1], high[1] = lax.optimization_barrier((w_first, low[1], high[1]))
    moves = second_moves(low[1], high[1])
    images = spread(image_cols, TOKENS).reshape(line, slots, projector.shape[1])
    encoded_other = swap(encoded_own, "segment", 1)
    encoded = jnp.concatenate(
        [
            jnp.where(segment == 0, encoded_own, encoded_other),
            jnp.where(segment == 0, encoded_other, encoded_own),
        ],
        axis=0,
    )

    angles = jnp.arange(seq_len, dtype=f32)[:, None] * (
        rope_base ** (-2.0 * jnp.arange(HD // 2, dtype=f32) / HD)
    )
    cosine = jnp.concatenate([jnp.cos(angles), jnp.cos(angles)], axis=1)
    sine = jnp.concatenate([-jnp.sin(angles), jnp.sin(angles)], axis=1)
    chunk_rows = tokens // line
    row_start = (core * 4 + chip) * chunk_rows
    whole = ((tokens, width), bf16)
    halved = ((tokens // 2, width), bf16)
    heads = ((tokens, half), bf16)

    def own_rows(array):
        return lax.dynamic_slice_in_dim(array, row_start, chunk_rows, 0)

    hidden0, q0, k0, v0, keep_rows, give_rows, _ = call(
        first_section,
        "first_section",
        [whole, heads, heads, heads, halved, halved, heads],
        targets,
        *w_first,
        images,
        text_embed[:, 0],
        mask_embed[None, :],
        placing,
        masked,
        cosine,
        sine,
        **with_weights,
    )
    mine = (own_rows(hidden0).astype(f32) + sum_rows(keep_rows, give_rows, chip)).astype(bf16)
    early, mine = lax.optimization_barrier((moves[:2], mine))
    w_last = in_order(low[1], high[1], (*early, *moves[2:]))
    hidden_halves = spread_rows(mine, chip)

    few_heads = ((masked_rows, half), bf16)
    q1, k1, v1, partial, picked, _ = call(
        last_section,
        "last_section",
        [
            few_heads,
            heads,
            heads,
            ((masked_rows, width), bf16),
            ((masked_rows, width), f32),
            few_heads,
        ],
        targets,
        *w_last,
        *hidden_halves,
        pick_all,
        cosine,
        sine,
        **with_weights,
    )
    cols = width // line
    parts = exchange(
        jnp.transpose(partial.reshape(masked_rows, line, cols), (1, 0, 2)), LINE
    )
    picked = lax.dynamic_slice_in_dim(picked, place * cols, cols, 1)
    last = (picked + jnp.sum(parts.astype(f32), axis=0)).astype(bf16)

    all_rows = spread(last, ALL).reshape(2, dp_size, 4, masked_rows, cols)
    all_rows = jnp.transpose(all_rows, (1, 3, 2, 0, 4)).reshape(dp_size * masked_rows, width)
    row_count = all_rows.shape[0]
    final = norm_rows(all_rows.astype(f32)).astype(bf16)
    logits = dot_nt(final, head_weight)

    teacher = (
        jnp.transpose(teacher_logits.reshape(micro, dp_size, MASKED, -1), (1, 0, 2, 3))
        .reshape(row_count, -1)
        .astype(f32)
    )
    top = jnp.max(teacher, axis=1)
    powers = jnp.exp(teacher - top[:, None])
    stats = jnp.stack(
        [
            jnp.sum(jnp.exp(logits), axis=1),
            top,
            jnp.sum(powers, axis=1),
            jnp.sum(powers * (teacher - logits), axis=1),
        ]
    )
    stats = spread(stats, ALL).reshape(-1, 4, row_count)
    sum_student = jnp.sum(stats[:, 0], axis=0)
    top_all = jnp.max(stats[:, 1], axis=0)
    scale = jnp.exp(stats[:, 1] - top_all[None])
    sum_teacher = jnp.sum(stats[:, 2] * scale, axis=0)
    cross = jnp.sum(stats[:, 3] * scale, axis=0)
    norm_student = jnp.log(sum_student)
    norm_teacher = top_all + jnp.log(sum_teacher)
    divergence = cross / sum_teacher - norm_teacher + norm_student
    ratio = RATIOS / ratio_index.astype(f32)
    row_weights = jnp.repeat(jnp.transpose(ratio), MASKED, axis=1).reshape(-1)
    total = micro * dp_size
    loss = jnp.sum(row_weights * divergence) / total
    d_logits = (
        (row_weights / total)[:, None]
        * (jnp.exp(logits - norm_student[:, None]) - jnp.exp(teacher - norm_teacher[:, None]))
    ).astype(bf16)
    d_final = dot(d_logits, head_weight).astype(bf16)
    d_final = jnp.transpose(
        d_final.reshape(dp_size, masked_rows, 4, 2, cols), (3, 0, 2, 1, 4)
    ).reshape(-1, masked_rows, cols)
    d_own = jnp.sum(exchange(d_final, ALL).astype(f32), axis=0).astype(bf16)
    d_own = jnp.transpose(spread(d_own, LINE).reshape(line, masked_rows, cols), (1, 0, 2)).reshape(
        masked_rows, width
    )
    rows = lax.dynamic_slice_in_dim(all_rows, dp_index * masked_rows, masked_rows, 0)
    grad_rows = norm_back(rows.astype(f32), d_own.astype(f32)).astype(bf16)

    keep_rows, give_rows, _ = call(
        last_section_back,
        "last_section_back",
        [halved, halved, ((tokens, 3 * half), bf16)],
        targets,
        *w_last,
        grad_rows,
        pick_all,
        q1,
        k1,
        v1,
        cosine,
        sine,
        **with_weights,
    )
    d_normed = sum_rows(keep_rows, give_rows, chip)
    own_pick = lax.dynamic_slice_in_dim(pick_all, row_start, chunk_rows, 1)
    grad_own = dot_tn(own_pick, grad_rows)
    grad_own = (grad_own + norm_back(mine.astype(f32), d_normed)).astype(bf16)
    grad_halves = spread_rows(grad_own, chip)

    cells = micro * slots
    columns = ((cells, cols), f32)
    chunks, grad_cols, hidden_cols, factor, _ = call(
        functools.partial(first_section_back, slots),
        "first_section_back",
        [
            ((line, cells, cols + 128), bf16),
            columns,
            columns,
            ((cells, 1), f32),
            ((cells, 3 * half), f32),
        ],
        targets,
        *w_first,
        *grad_halves,
        hidden0,
        q0,
        k0,
        v0,
        cosine,
        sine,
        **with_weights,
    )
    owners = 2 * dp_size
    (proj_part,) = call(
        finish,
        "finish",
        [((owners, depth // owners, cols), bf16)],
        exchange(chunks, LINE),
        grad_cols,
        hidden_cols,
        factor,
        placing,
        encoded,
        mb=8,
    )
    parts = exchange(proj_part, ("segment", "dp"))
    parts = jnp.sum(parts.astype(f32).reshape(2, dp_size, depth // owners, cols), axis=1)
    projector_grad = jnp.transpose(parts, (1, 0, 2)).reshape(depth // owners, 2 * cols)
    return (loss, projector_grad)


def solution(mesh):
    placed = (
        P(None, "dp", None, None),
        P(None, "dp", None, None),
        P(),
        P(None, "dp"),
        P(None, "dp", None),
        P(None, "dp", None),
        P(),
        P(None, None, "vocab"),
        P(None, "vocab", None),
        P(None, "vocab"),
        P("segment", None, "dp", "vocab"),
        P("segment", "vocab", "dp"),
        P(("segment", "dp", "vocab"), None),
        P(None, ("segment", "dp", "vocab")),
    )
    return jax.shard_map(
        shards,
        mesh=mesh,
        in_specs=placed,
        out_specs=(P(), P(("segment", "dp"), "vocab")),
        check_vma=False,
    )
```

```python
import functools

import jax
import jax.numpy as jnp
from jax import lax
from jax.experimental import pallas as pl
from jax.experimental.pallas import tpu as pltpu
from jax.sharding import PartitionSpec as P

HD = 128
MASKED = 4
RATIOS = 8

epsilon = 1e-06
rope_base = 500000.0

LINE = ("vocab", "segment")
ALL = ("segment", "dp", "vocab")
f32 = jnp.float32
bf16 = jnp.bfloat16


def dot(a, b):
    return jnp.dot(a, b, preferred_element_type=f32)


def dot_nt(a, b):
    return lax.dot_general(a, b, (((1,), (1,)), ((), ())), preferred_element_type=f32)


def dot_tn(a, b):
    return lax.dot_general(a, b, (((0,), (0,)), ((), ())), preferred_element_type=f32)


def swap(block, axis, mask):
    return lax.ppermute(block, axis, [(i, i ^ mask) for i in range(lax.axis_size(axis))])


def exchange(chunks, axes):
    return lax.all_to_all(chunks, axes, 0, 0, tiled=True)


def spread(block, axes):
    size = lax.axis_size(axes)
    return exchange(jnp.broadcast_to(block[None], (size,) + block.shape), axes)


def inverse_rms(values_in):
    return lax.rsqrt(jnp.mean(values_in * values_in, axis=-1, keepdims=True) + epsilon)


def norm_rows(values_in):
    return values_in * inverse_rms(values_in)


def layer_norm(values_in):
    centred = values_in - jnp.mean(values_in, axis=-1, keepdims=True)
    return centred * lax.rsqrt(jnp.mean(centred * centred, axis=-1, keepdims=True) + epsilon)


def norm_back(values_in, cotangent):
    factor = inverse_rms(values_in)
    return factor * cotangent - values_in * factor**3 * jnp.mean(
        cotangent * values_in, axis=-1, keepdims=True
    )


SIDE = ("dp", "vocab")
TOKENS = ("segment", "vocab")


def call(body, name, outs, *args, smem=0, far=0, scratch=(), mb=0):
    specs = [pl.BlockSpec(memory_space=pltpu.SMEM)] * smem + [
        pl.BlockSpec(memory_space=pl.ANY)
    ] * far
    specs += [pl.BlockSpec(memory_space=pltpu.VMEM)] * (len(args) - len(specs))
    return pl.pallas_call(
        body,
        name=name,
        out_shape=[jax.ShapeDtypeStruct(shape, kind) for shape, kind in outs],
        in_specs=specs,
        out_specs=[pl.BlockSpec(memory_space=pltpu.VMEM) for _ in outs],
        scratch_shapes=list(scratch),
        cost_estimate=pl.CostEstimate(flops=0, bytes_accessed=mb * 1000000, transcendentals=0),
        compiler_params=pltpu.CompilerParams(vmem_limit_bytes=56 << 20),
    )(*args)


def side_shift(block, step, first):
    sizes = (lax.axis_size("dp"), lax.axis_size("vocab"))
    edge = 4
    route = []
    for dp in range(sizes[0]):
        z, y = divmod(dp, edge)
        for v in range(sizes[1]):
            if (v % 2 == 0) == first:
                to = z * edge + (y + step) % edge
            else:
                to = ((z + step) % edge) * edge + y
            route.append((dp * sizes[1] + v, to * sizes[1] + v))
    return lax.ppermute(block, SIDE, route)


def line_move(block, lo, hi):
    count = lax.axis_size("vocab")
    route = [
        (s * count + v, (s ^ lo) * count + (v ^ (2 * hi)))
        for s in range(lax.axis_size("segment"))
        for v in range(count)
    ]
    return lax.ppermute(block, TOKENS, route)


def core_groups():
    total = lax.axis_size(ALL)
    return [list(range(core, total, 2)) for core in range(2)]


def spread_within(block, axes, groups):
    copies = jnp.broadcast_to(block[None], (len(groups[0]),) + block.shape)
    return lax.all_to_all(copies, axes, 0, 0, axis_index_groups=groups, tiled=True)


def sum_rows(mine, give, chip):
    rows, width = mine.shape
    both = (mine.astype(f32) + swap(give, "vocab", 1).astype(f32)).astype(bf16)
    both = both.reshape(4, rows // 4, width)

    def piece(mask):
        return lax.dynamic_index_in_dim(both, chip ^ mask, 0, False)

    moved = [line_move(piece(m), m & 1, m >> 1) for m in (1, 2, 3)]
    return (piece(0).astype(f32) + moved[0].astype(f32)) + (
        moved[1].astype(f32) + moved[2].astype(f32)
    )


def spread_rows(block, chip):
    rows, width = block.shape
    pieces = [block] + [line_move(block, m & 1, m >> 1) for m in (1, 2, 3)]
    half = jnp.zeros((4, rows, width), block.dtype)
    for mask in range(4):
        half = lax.dynamic_update_slice(half, pieces[mask][None], (chip ^ mask, 0, 0))
    half = half.reshape(4 * rows, width)
    return half, swap(half, "vocab", 1)


def prepare(counts, order, masks, placing_out, pick_out, masked_out):
    micro, slots, _ = placing_out.shape
    images = order.shape[1]
    each = slots // images
    cell = lax.broadcasted_iota(jnp.int32, (slots, slots), 0)
    slot = lax.broadcasted_iota(jnp.int32, (slots, slots), 1)
    tokens = pick_out.shape[1]
    seq_len = tokens // micro
    row = lax.broadcasted_iota(jnp.int32, pick_out.shape, 0)
    column = lax.broadcasted_iota(jnp.int32, pick_out.shape, 1)
    token = lax.broadcasted_iota(jnp.int32, masked_out.shape, 0)
    pick = jnp.zeros(pick_out.shape, f32)
    masked = jnp.zeros(masked_out.shape, f32)
    for m in range(micro):
        hit = jnp.zeros((slots, slots), f32)
        for i in range(images):
            within = slot - i * each
            inside = (within >= 0) & (within < each) & (cell == order[m, i] * each + within)
            live = jnp.where(i < counts[m, 0], 1.0, 0.0)
            hit = jnp.where(inside, live, hit)
        placing_out[m] = hit.astype(bf16)
        for p in range(MASKED):
            where = m * seq_len + masks[m, p]
            pick = jnp.where((row == m * MASKED + p) & (column == where), 1.0, pick)
            masked = jnp.where(token == where, 1.0, masked)
    pick_out[...] = pick.astype(bf16)
    masked_out[...] = masked


def add_parts(x, parts):
    total = parts[0][...].astype(f32) + parts[1][...].astype(f32)
    total = total + (parts[2][...].astype(f32) + parts[3][...].astype(f32))
    return (x[...].astype(f32) + total).astype(bf16)


STEP = 272


def mlp(layer, current, up_far, down_far, up, down, sems):
    units, layers, _ = up.shape
    starts = list(range(0, units, STEP))
    copies = []
    for i, start in enumerate(starts):
        part = pl.ds(start, min(STEP, units - start))
        for j, (far, near) in enumerate(((up_far, up), (down_far, down))):
            copies.append(pltpu.make_async_copy(far.at[part], near.at[part], sems.at[i, j]))
    start_all(copies)
    normed = layer_norm(current().astype(f32)).astype(bf16)
    total = jnp.zeros(normed.shape, f32)
    for i, start in enumerate(starts):
        part = slice(start, min(start + STEP, units))
        shape = ((part.stop - start) * layers, up.shape[2])
        copies[2 * i].wait()
        inner = dot_nt(normed, up[part].reshape(shape))
        mine = lax.broadcasted_iota(jnp.int32, inner.shape, 1) % layers == layer
        inner = jnp.where(mine, jax.nn.gelu(inner, approximate=True), 0.0).astype(bf16)
        copies[2 * i + 1].wait()
        total = total + dot(inner, down[part].reshape(shape))
    return total.astype(bf16)


def encode_first(up_far, down_far, x, part, up, down, sems):
    part[...] = mlp(0, lambda: x[...], up_far, down_far, up, down, sems)


def encode_next(layer, up_far, down_far, x, p0, p1, p2, p3, part, current, up, down, sems):
    def now():
        value = add_parts(x, (p0, p1, p2, p3))
        current[...] = value
        return value

    part[...] = mlp(layer, now, up_far, down_far, up, down, sems)


def encode_last(x, p0, p1, p2, p3, projector, current, columns):
    now = add_parts(x, (p0, p1, p2, p3))
    current[...] = now
    columns[...] = dot(now, projector[...]).astype(bf16)


def turn(values, cosine, sine):
    return values * cosine + pltpu.roll(values, HD // 2, 1) * sine


def load_weights(targets, blocks, w, sems):
    rows = w.shape[1] // 16
    sources = [array.at[i] for array in blocks for i in range(array.shape[0])]
    parts = []
    for number, mats in enumerate((pl.ds(3, 1), pl.ds(0, 3))):
        copies = []
        for i, source in enumerate(sources):
            start = pl.multiple_of(targets[i] * rows, rows)
            copies.append(
                pltpu.make_async_copy(
                    source.at[mats], w.at[mats, pl.ds(start, rows), :], sems.at[number, i]
                )
            )
        parts.append(copies)
    return parts


def start_all(copies):
    for copy in copies:
        copy.start()


def wait_all(copies):
    for copy in copies:
        copy.wait()


def pairs_of(tokens, seq_len, half):
    return [
        (m, slice(m * seq_len, (m + 1) * seq_len), slice(h * HD, (h + 1) * HD))
        for m in range(tokens // seq_len)
        for h in range(half // HD)
    ]


def project_heads(hidden, w, cosine, sine, copies):
    half = w.shape[2]
    normed = norm_rows(hidden.astype(f32)).astype(bf16)
    wait_all(copies)
    q_all, k_all, v_all = (dot(normed, w[i]) for i in range(3))
    repeat = hidden.shape[0] // cosine.shape[0]
    cosine = jnp.concatenate([cosine[...]] * repeat, axis=0)
    sine = jnp.concatenate([sine[...]] * repeat, axis=0)

    def turned(values):
        return jnp.concatenate(
            [
                turn(values[:, h * HD : (h + 1) * HD], cosine, sine).astype(bf16)
                for h in range(half // HD)
            ],
            axis=1,
        )

    return turned(q_all), turned(k_all), v_all.astype(bf16)


def softmax(scores):
    powers = jnp.exp(scores - jnp.max(scores, axis=-1, keepdims=True))
    return powers / jnp.sum(powers, axis=-1, keepdims=True)


def attend(queries, keys, values):
    scores = [dot_nt(q, k) * HD ** (-0.5) for q, k in zip(queries, keys)]
    probs = [softmax(x).astype(bf16) for x in scores]
    return [dot(p, v).astype(bf16) for p, v in zip(probs, values)]


def attend_back(queries, keys, values, d_mixed):
    scores = [dot_nt(q, k) * HD ** (-0.5) for q, k in zip(queries, keys)]
    d_probs = [dot_nt(d, v).astype(bf16).astype(f32) for d, v in zip(d_mixed, values)]
    probs = [softmax(x) for x in scores]
    d_scores = [
        p * (d - jnp.sum(p * d, axis=-1, keepdims=True)) for p, d in zip(probs, d_probs)
    ]
    return (
        [(d * HD ** (-0.5)).astype(bf16) for d in d_scores],
        [p.astype(bf16) for p in probs],
    )


def split_halves(scalars, partial, keep, give):
    core, rows = scalars[16], keep.shape[0]
    keep[...] = partial[pl.ds(pl.multiple_of(core * rows, rows), rows), :]
    give[...] = partial[pl.ds(pl.multiple_of((1 - core) * rows, rows), rows), :]


def join_halves(scalars, own, other, whole):
    core, rows = scalars[16], own.shape[0]
    whole[pl.ds(pl.multiple_of(core * rows, rows), rows), :] = own[...]
    whole[pl.ds(pl.multiple_of((1 - core) * rows, rows), rows), :] = other[...]


def first_section(targets, *refs):
    blocks, refs = refs[:8], refs[8:]
    images, text, mask_row, placing, masked, cosine, sine = refs[:7]
    hidden, q, k, v, keep, give, mixed, w, sems, partial = refs[7:]
    out_copies, in_copies = load_weights(targets, blocks, w, sems)
    start_all(in_copies)
    start_all(out_copies)
    micro, slots, _ = placing.shape
    seq_len = cosine.shape[0]
    tokens, width = hidden.shape
    blocks_wide = images.shape[0] // micro
    part = width // blocks_wide
    half = q.shape[1]
    for m in range(micro):
        rows = slice(m * seq_len, (m + 1) * seq_len)
        hidden[rows, :] = jnp.where(masked[rows, :] > 0.0, mask_row[...], text[m])
        place = placing[m]
        filled = jnp.sum(place.astype(f32), axis=1, keepdims=True) > 0.0
        for b in range(blocks_wide):
            placed = dot(place, images[m * blocks_wide + b]).astype(bf16)
            cols = slice(b * part, (b + 1) * part)
            hidden[m * seq_len : m * seq_len + slots, cols] = jnp.where(
                filled, placed, text[m, :slots, cols]
            )
    q_all, k_all, v_all = project_heads(hidden[...], w, cosine, sine, in_copies)
    q[...] = q_all
    k[...] = k_all
    v[...] = v_all
    pairs = pairs_of(tokens, seq_len, half)
    results = attend(*([x[rows, cols] for _, rows, cols in pairs] for x in (q_all, k_all, v_all)))
    for (_, rows, cols), result in zip(pairs, results):
        mixed[rows, cols] = result
    wait_all(out_copies)
    partial[...] = dot_nt(mixed[...], w[3]).astype(bf16)
    split_halves(targets, partial, keep, give)


def last_section(targets, *refs):
    blocks, refs = refs[:8], refs[8:]
    own, other, pick, cosine, sine, q, k, v, partial, picked, mixed, w, sems, hidden = refs
    out_copies, in_copies = load_weights(targets, blocks, w, sems)
    start_all(in_copies)
    start_all(out_copies)
    join_halves(targets, own, other, hidden)
    picked[...] = dot(pick[...], hidden[...])
    q_all, k_all, v_all = project_heads(hidden[...], w, cosine, sine, in_copies)
    q_few = dot(pick[...], q_all).astype(bf16)
    q[...] = q_few
    k[...] = k_all
    v[...] = v_all
    pairs = pairs_of(hidden.shape[0], cosine.shape[0], k.shape[1])
    few = [slice(m * MASKED, (m + 1) * MASKED) for m, _, _ in pairs]
    results = attend(
        [q_few[mine, cols] for mine, (_, _, cols) in zip(few, pairs)],
        *([x[rows, cols] for _, rows, cols in pairs] for x in (k_all, v_all)),
    )
    for mine, (_, _, cols), result in zip(few, pairs, results):
        mixed[mine, cols] = result
    wait_all(out_copies)
    partial[...] = dot_nt(mixed[...], w[3]).astype(bf16)


def back_to_width(d_all, w):
    half = w.shape[2]
    total = dot_nt(d_all[:, :half].astype(bf16), w[0])
    for i in (1, 2):
        total = total + dot_nt(d_all[:, i * half : (i + 1) * half].astype(bf16), w[i])
    return total.astype(bf16)


def last_section_back(targets, *refs):
    blocks, refs = refs[:8], refs[8:]
    grad, pick, q, k, v, cosine, sine, keep, give, d_all, w, sems, partial = refs
    out_copies, in_copies = load_weights(targets, blocks, w, sems)
    start_all(out_copies)
    start_all(in_copies)
    half = k.shape[1]
    pairs = pairs_of(k.shape[0], cosine.shape[0], half)
    few = [slice(m * MASKED, (m + 1) * MASKED) for m, _, _ in pairs]
    queries = [q[mine, cols] for mine, (_, _, cols) in zip(few, pairs)]
    keys, values = ([x[rows, cols] for _, rows, cols in pairs] for x in (k, v))
    wait_all(out_copies)
    d_mixed = dot(grad[...], w[3]).astype(bf16)
    d_heads = [d_mixed[mine, cols] for mine, (_, _, cols) in zip(few, pairs)]
    d_scores, probs = attend_back(queries, keys, values, d_heads)
    d_q = [dot(d, k_h).astype(bf16) for d, k_h in zip(d_scores, keys)]
    d_k = [dot_tn(d, q_h).astype(bf16).astype(f32) for d, q_h in zip(d_scores, queries)]
    d_v = [dot_tn(p, d_h) for p, d_h in zip(probs, d_heads)]
    d_q = [
        dot_tn(pick[mine, rows], d) for mine, (_, rows, _), d in zip(few, pairs, d_q)
    ]
    back_sine = -sine[...]
    for i, (_, rows, cols) in enumerate(pairs):
        for part, d in enumerate(
            (turn(d_q[i], cosine[...], back_sine), turn(d_k[i], cosine[...], back_sine), d_v[i])
        ):
            at = part * half + cols.start
            d_all[rows, at : at + HD] = d.astype(bf16)
    wait_all(in_copies)
    partial[...] = back_to_width(d_all, w)
    split_halves(targets, partial, keep, give)


def first_section_back(slots, targets, *refs):
    blocks, refs = refs[:8], refs[8:]
    own, other, hidden, q, k, v, cosine, sine = refs[:8]
    chunks, grad_cols, hidden_cols, factor, d_all, w, sems, grad = refs[8:]
    join_halves(targets, own, other, grad)
    out_copies, in_copies = load_weights(targets, blocks, w, sems)
    start_all(out_copies)
    start_all(in_copies)
    half = k.shape[1]
    seq_len = cosine.shape[0]
    pairs = pairs_of(k.shape[0], seq_len, half)
    queries, keys, values = ([x[rows, cols] for _, rows, cols in pairs] for x in (q, k, v))
    wait_all(out_copies)
    d_mixed = dot(grad[...], w[3]).astype(bf16)
    d_heads = [d_mixed[rows, cols] for _, rows, cols in pairs]
    d_scores, probs = attend_back(queries, keys, values, d_heads)
    d_q = [dot(d, k_h)[:slots].astype(bf16).astype(f32) for d, k_h in zip(d_scores, keys)]
    d_k = [
        dot_tn(d, q_h)[:slots].astype(bf16).astype(f32) for d, q_h in zip(d_scores, queries)
    ]
    d_v = [dot_tn(p, d_h)[:slots] for p, d_h in zip(probs, d_heads)]
    cos_top, sin_top = cosine[:slots, :], -sine[:slots, :]
    for i, (m, _, cols) in enumerate(pairs):
        top = slice(m * slots, (m + 1) * slots)
        for part, d in enumerate(
            (turn(d_q[i], cos_top, sin_top), turn(d_k[i], cos_top, sin_top), d_v[i])
        ):
            at = part * half + cols.start
            d_all[top, at : at + HD] = d
    wait_all(in_copies)
    rounded = back_to_width(d_all, w)
    line, cells, _ = chunks.shape
    cols = grad_cols.shape[1]
    at = pl.multiple_of(targets[17] * cols, cols)
    lane = lax.broadcasted_iota(jnp.int32, (slots, chunks.shape[2] - cols), 1)
    for m in range(k.shape[0] // seq_len):
        top = slice(m * slots, (m + 1) * slots)
        rows = slice(m * seq_len, m * seq_len + slots)
        values = hidden[rows, :].astype(f32)
        mine = rounded[top, :]
        along = jnp.mean(mine.astype(f32) * values, axis=1, keepdims=True)
        high = along.astype(bf16).astype(f32)
        notes = jnp.where(lane == 0, high, jnp.where(lane == 1, along - high, 0.0)).astype(bf16)
        for c in range(line):
            chunks[c, top, :cols] = mine[:, c * cols : (c + 1) * cols]
            chunks[c, top, cols:] = notes
        factor[top, :] = inverse_rms(values)
        grad_cols[top, :] = grad[rows, pl.ds(at, cols)].astype(f32)
        hidden_cols[top, :] = hidden[rows, pl.ds(at, cols)].astype(f32)


def finish(parts, grad_cols, hidden_cols, factor, placing, encoded, out):
    cells, cols = grad_cols.shape
    total = parts[0].astype(f32)
    for c in range(1, parts.shape[0]):
        total = total + parts[c].astype(f32)
    along = total[:, cols : cols + 1] + total[:, cols + 1 : cols + 2]
    scale = factor[...]
    grad = grad_cols[...] + scale * total[:, :cols] - hidden_cols[...] * scale**3 * along
    grad = grad.astype(bf16)
    micro, slots, _ = placing.shape
    d_image = jnp.concatenate(
        [
            dot_tn(placing[m], grad[m * slots : (m + 1) * slots]).astype(bf16)
            for m in range(micro)
        ],
        axis=0,
    )
    total = dot_tn(encoded[...], d_image)
    owners, rows, _ = out.shape
    for i in range(owners):
        out[i] = total[i * rows : (i + 1) * rows].astype(bf16)


def slice_order(dp_index, core):
    z, y = dp_index // 4, dp_index % 4
    step = jnp.arange(4, dtype=jnp.int32)
    outer = ((jnp.where(core == 0, z, y) + step) % 4)[:, None]
    inner = ((jnp.where(core == 0, y, z) + step) % 4)[None, :]
    return jnp.where(core == 0, outer * 4 + inner, inner * 4 + outer).reshape(-1)


def second_moves(low, high):
    return (
        side_shift(low, 1, False),
        side_shift(high, -1, False),
        side_shift(high, 1, False),
        side_shift(low, -1, False),
    )


def in_order(low, high, moves):
    behind_low, ahead_high, behind_high, ahead_low = moves
    far_low = side_shift(behind_low, 1, False)
    far_high = side_shift(ahead_high, -1, False)
    return (low, high, ahead_low, ahead_high, far_low, far_high, behind_low, behind_high)


def shards(
    patches,
    text_embed,
    mask_embed,
    image_counts,
    image_order,
    masked_positions,
    ratio_index,
    enc_up,
    enc_down,
    projector,
    lang_qkv,
    lang_out,
    head_weight,
    teacher_logits,
):
    segment = lax.axis_index("segment")
    dp_index = lax.axis_index("dp")
    place = lax.axis_index("vocab") * 2 + segment
    core = lax.axis_index("vocab") % 2
    chip = (lax.axis_index("vocab") // 2) * 2 + segment
    line = lax.axis_size(LINE)
    dp_size = lax.axis_size("dp")
    micro = text_embed.shape[0]
    seq_len, width = text_embed.shape[2:]
    slots = patches.shape[2]
    depth = patches.shape[3]

    shard = jnp.concatenate(
        [lang_qkv[0], jnp.transpose(lang_out[0])[None]], axis=0
    )
    half = shard.shape[2] // 2
    low, high = shard[:, :, :half], shard[:, :, half:]
    keep = jnp.where(segment == 0, low, high)
    give = jnp.where(segment == 0, high, low)
    got = swap(give, "segment", 1)
    with_weights = dict(
        smem=1,
        far=8,
        scratch=(
            pltpu.VMEM((4, width, half), bf16),
            pltpu.SemaphoreType.DMA((2, 16)),
            pltpu.VMEM((micro * seq_len, width), bf16),
        ),
        mb=30,
    )

    layers, _, hidden_units = enc_up.shape
    tokens = micro * seq_len
    masked_rows = micro * MASKED
    placing, pick_all, masked = call(
        prepare,
        "prepare",
        [
            ((micro, slots, slots), bf16),
            ((masked_rows, tokens), bf16),
            ((tokens, 1), f32),
        ],
        image_counts,
        image_order[:, 0],
        masked_positions[:, 0],
        smem=3,
        mb=3,
    )
    up = jnp.transpose(enc_up, (2, 0, 1))
    down = jnp.transpose(enc_down, (1, 0, 2))

    def parts_of(part):
        return [part] + [swap(part, "vocab", mask) for mask in (1, 2, 3)]

    small = ((slots, depth), bf16)
    current = lax.dynamic_index_in_dim(patches[:, 0], segment, 0, False)
    with_layers = dict(
        far=2,
        scratch=(
            pltpu.VMEM(up.shape, bf16),
            pltpu.VMEM(down.shape, bf16),
            pltpu.SemaphoreType.DMA((-(-hidden_units // STEP), 2)),
        ),
        mb=20,
    )
    (part,) = call(encode_first, "encode_first", [small], up, down, current, **with_layers)
    angles = jnp.arange(seq_len, dtype=f32)[:, None] * (
        rope_base ** (-2.0 * jnp.arange(HD // 2, dtype=f32) / HD)
    )
    cosine = jnp.concatenate([jnp.cos(angles), jnp.cos(angles)], axis=1)
    sine = jnp.concatenate([-jnp.sin(angles), jnp.sin(angles)], axis=1)
    targets = jnp.concatenate(
        [slice_order(dp_index, core), jnp.stack([core, place]).astype(jnp.int32)]
    )
    got, part, placing, pick_all, masked, cosine, sine, targets = lax.optimization_barrier(
        (got, part, placing, pick_all, masked, cosine, sine, targets)
    )
    first = segment == 0
    both = jnp.stack([jnp.where(first, keep, got), jnp.where(first, got, keep)])
    behind = side_shift(both, 1, True)
    ahead = side_shift(both, -1, True)
    first_parts = parts_of(part)
    behind, ahead, first_parts = lax.optimization_barrier((behind, ahead, first_parts))
    far = [side_shift(behind[0], 1, True), side_shift(ahead[1], -1, True)]
    part, current = call(
        functools.partial(encode_next, 1),
        "encode_next",
        [small, small],
        up,
        down,
        current,
        *first_parts,
        **with_layers,
    )
    far, part = lax.optimization_barrier((far, part))
    low = [jnp.stack([both[s], ahead[s]]) for s in range(2)]
    high = [jnp.stack([far[s], behind[s]]) for s in range(2)]
    moves = second_moves(low[0], high[0])
    encoded_own, image_cols = call(
        encode_last,
        "encode_last",
        [small, ((slots, projector.shape[1]), bf16)],
        current,
        *parts_of(part),
        projector,
        mb=10,
    )
    early, image_cols = lax.optimization_barrier((moves[:2], image_cols))
    moves = (*early, *moves[2:])
    w_first = in_order(low[0], high[0], moves)
    images = spread(image_cols, TOKENS).reshape(line, slots, projector.shape[1])
    w_first, images, low[1], high[1] = lax.optimization_barrier(
        (w_first, images, low[1], high[1])
    )
    moves = second_moves(low[1], high[1])
    encoded_other = swap(encoded_own, "segment", 1)
    encoded = jnp.concatenate(
        [
            jnp.where(segment == 0, encoded_own, encoded_other),
            jnp.where(segment == 0, encoded_other, encoded_own),
        ],
        axis=0,
    )

    chunk_rows = tokens // line
    row_start = (core * 4 + chip) * chunk_rows
    whole = ((tokens, width), bf16)
    halved = ((tokens // 2, width), bf16)
    heads = ((tokens, half), bf16)

    def own_rows(array):
        return lax.dynamic_slice_in_dim(array, row_start, chunk_rows, 0)

    hidden0, q0, k0, v0, keep_rows, give_rows, _ = call(
        first_section,
        "first_section",
        [whole, heads, heads, heads, halved, halved, heads],
        targets,
        *w_first,
        images,
        text_embed[:, 0],
        mask_embed[None, :],
        placing,
        masked,
        cosine,
        sine,
        **with_weights,
    )
    early, give_rows = lax.optimization_barrier((moves[:2], give_rows))
    mine = (own_rows(hidden0).astype(f32) + sum_rows(keep_rows, give_rows, chip)).astype(bf16)
    w_last = in_order(low[1], high[1], (*early, *moves[2:]))
    far, mine = lax.optimization_barrier((w_last[4:6], mine))
    w_last = (*w_last[:4], *far, *w_last[6:])
    hidden_halves = spread_rows(mine, chip)

    few_heads = ((masked_rows, half), bf16)
    q1, k1, v1, partial, picked, _ = call(
        last_section,
        "last_section",
        [
            few_heads,
            heads,
            heads,
            ((masked_rows, width), bf16),
            ((masked_rows, width), f32),
            few_heads,
        ],
        targets,
        *w_last,
        *hidden_halves,
        pick_all,
        cosine,
        sine,
        **with_weights,
    )
    cols = width // line
    parts = exchange(
        jnp.transpose(partial.reshape(masked_rows, line, cols), (1, 0, 2)), LINE
    )
    picked = lax.dynamic_slice_in_dim(picked, place * cols, cols, 1)
    last = (picked + jnp.sum(parts.astype(f32), axis=0)).astype(bf16)

    own_cols = spread_within(last, ALL, core_groups())
    other_cols = swap(own_cols, "vocab", 1)
    by_core = jnp.stack(
        [
            jnp.where(core == 0, own_cols, other_cols),
            jnp.where(core == 0, other_cols, own_cols),
        ]
    ).reshape(2, 2, dp_size, 2, masked_rows, cols)
    all_rows = jnp.transpose(by_core, (2, 4, 3, 0, 1, 5)).reshape(dp_size * masked_rows, width)
    row_count = all_rows.shape[0]
    final = norm_rows(all_rows.astype(f32)).astype(bf16)
    logits = dot_nt(final, head_weight)

    teacher = (
        jnp.transpose(teacher_logits.reshape(micro, dp_size, MASKED, -1), (1, 0, 2, 3))
        .reshape(row_count, -1)
        .astype(f32)
    )
    top = jnp.max(teacher, axis=1)
    powers = jnp.exp(teacher - top[:, None])
    stats = jnp.stack(
        [
            jnp.sum(jnp.exp(logits), axis=1),
            top,
            jnp.sum(powers, axis=1),
            jnp.sum(powers * (teacher - logits), axis=1),
        ]
    )
    stats = spread(stats, ALL).reshape(-1, 4, row_count)
    sum_student = jnp.sum(stats[:, 0], axis=0)
    top_all = jnp.max(stats[:, 1], axis=0)
    scale = jnp.exp(stats[:, 1] - top_all[None])
    sum_teacher = jnp.sum(stats[:, 2] * scale, axis=0)
    cross = jnp.sum(stats[:, 3] * scale, axis=0)
    norm_student = jnp.log(sum_student)
    norm_teacher = top_all + jnp.log(sum_teacher)
    divergence = cross / sum_teacher - norm_teacher + norm_student
    ratio = RATIOS / ratio_index.astype(f32)
    row_weights = jnp.repeat(jnp.transpose(ratio), MASKED, axis=1).reshape(-1)
    total = micro * dp_size
    loss = jnp.sum(row_weights * divergence) / total
    d_logits = (
        (row_weights / total)[:, None]
        * (jnp.exp(logits - norm_student[:, None]) - jnp.exp(teacher - norm_teacher[:, None]))
    ).astype(bf16)
    d_final = dot(d_logits, head_weight).astype(bf16)
    d_final = jnp.transpose(
        d_final.reshape(dp_size, masked_rows, 4, 2, cols), (3, 0, 2, 1, 4)
    ).reshape(-1, masked_rows, cols)
    d_own = jnp.sum(exchange(d_final, ALL).astype(f32), axis=0).astype(bf16)
    d_own = jnp.transpose(spread(d_own, LINE).reshape(line, masked_rows, cols), (1, 0, 2)).reshape(
        masked_rows, width
    )
    rows = lax.dynamic_slice_in_dim(all_rows, dp_index * masked_rows, masked_rows, 0)
    grad_rows = norm_back(rows.astype(f32), d_own.astype(f32)).astype(bf16)

    keep_rows, give_rows, _ = call(
        last_section_back,
        "last_section_back",
        [halved, halved, ((tokens, 3 * half), bf16)],
        targets,
        *w_last,
        grad_rows,
        pick_all,
        q1,
        k1,
        v1,
        cosine,
        sine,
        **with_weights,
    )
    d_normed = sum_rows(keep_rows, give_rows, chip)
    own_pick = lax.dynamic_slice_in_dim(pick_all, row_start, chunk_rows, 1)
    grad_own = dot_tn(own_pick, grad_rows)
    grad_own = (grad_own + norm_back(mine.astype(f32), d_normed)).astype(bf16)
    grad_halves = spread_rows(grad_own, chip)

    cells = micro * slots
    columns = ((cells, cols), f32)
    chunks, grad_cols, hidden_cols, factor, _ = call(
        functools.partial(first_section_back, slots),
        "first_section_back",
        [
            ((line, cells, cols + 128), bf16),
            columns,
            columns,
            ((cells, 1), f32),
            ((cells, 3 * half), f32),
        ],
        targets,
        *w_first,
        *grad_halves,
        hidden0,
        q0,
        k0,
        v0,
        cosine,
        sine,
        **with_weights,
    )
    owners = 2 * dp_size
    (proj_part,) = call(
        finish,
        "finish",
        [((owners, depth // owners, cols), bf16)],
        exchange(chunks, LINE),
        grad_cols,
        hidden_cols,
        factor,
        placing,
        encoded,
        mb=8,
    )
    parts = exchange(proj_part, ("segment", "dp"))
    parts = jnp.sum(parts.astype(f32).reshape(2, dp_size, depth // owners, cols), axis=1)
    projector_grad = jnp.transpose(parts, (1, 0, 2)).reshape(depth // owners, 2 * cols)
    return (loss, projector_grad)


def solution(mesh):
    placed = (
        P(None, "dp", None, None),
        P(None, "dp", None, None),
        P(),
        P(None, "dp"),
        P(None, "dp", None),
        P(None, "dp", None),
        P(),
        P(None, None, "vocab"),
        P(None, "vocab", None),
        P(None, "vocab"),
        P("segment", None, "dp", "vocab"),
        P("segment", "vocab", "dp"),
        P(("segment", "dp", "vocab"), None),
        P(None, ("segment", "dp", "vocab")),
    )
    return jax.shard_map(
        shards,
        mesh=mesh,
        in_specs=placed,
        out_specs=(P(), P(("segment", "dp"), "vocab")),
        check_vma=False,
    )
```

```python
import functools

import jax
import jax.numpy as jnp
from jax import lax
from jax.experimental import pallas as pl
from jax.experimental.pallas import tpu as pltpu
from jax.sharding import PartitionSpec as P

HD = 128
MASKED = 4
RATIOS = 8

epsilon = 1e-06
rope_base = 500000.0

LINE = ("vocab", "segment")
ALL = ("segment", "dp", "vocab")
f32 = jnp.float32
bf16 = jnp.bfloat16


def dot(a, b):
    return jnp.dot(a, b, preferred_element_type=f32)


def dot_nt(a, b):
    return lax.dot_general(a, b, (((1,), (1,)), ((), ())), preferred_element_type=f32)


def dot_tn(a, b):
    return lax.dot_general(a, b, (((0,), (0,)), ((), ())), preferred_element_type=f32)


def swap(block, axis, mask):
    return lax.ppermute(block, axis, [(i, i ^ mask) for i in range(lax.axis_size(axis))])


def exchange(chunks, axes):
    return lax.all_to_all(chunks, axes, 0, 0, tiled=True)


def spread(block, axes):
    size = lax.axis_size(axes)
    return exchange(jnp.broadcast_to(block[None], (size,) + block.shape), axes)


def inverse_rms(values_in):
    return lax.rsqrt(jnp.mean(values_in * values_in, axis=-1, keepdims=True) + epsilon)


def norm_rows(values_in):
    return values_in * inverse_rms(values_in)


def layer_norm(values_in):
    centred = values_in - jnp.mean(values_in, axis=-1, keepdims=True)
    return centred * lax.rsqrt(jnp.mean(centred * centred, axis=-1, keepdims=True) + epsilon)


def norm_back(values_in, cotangent):
    factor = inverse_rms(values_in)
    return factor * cotangent - values_in * factor**3 * jnp.mean(
        cotangent * values_in, axis=-1, keepdims=True
    )


SIDE = ("dp", "vocab")
TOKENS = ("segment", "vocab")


def call(body, name, outs, *args, smem=0, far=0, scratch=(), mb=0, vmem=56):
    specs = [pl.BlockSpec(memory_space=pltpu.SMEM)] * smem + [
        pl.BlockSpec(memory_space=pl.ANY)
    ] * far
    specs += [pl.BlockSpec(memory_space=pltpu.VMEM)] * (len(args) - len(specs))
    return pl.pallas_call(
        body,
        name=name,
        out_shape=[jax.ShapeDtypeStruct(shape, kind) for shape, kind in outs],
        in_specs=specs,
        out_specs=[pl.BlockSpec(memory_space=pltpu.VMEM) for _ in outs],
        scratch_shapes=list(scratch),
        cost_estimate=pl.CostEstimate(flops=0, bytes_accessed=mb * 1000000, transcendentals=0),
        compiler_params=pltpu.CompilerParams(vmem_limit_bytes=vmem << 20),
    )(*args)


def side_shift(block, step, first):
    sizes = (lax.axis_size("dp"), lax.axis_size("vocab"))
    edge = 4
    route = []
    for dp in range(sizes[0]):
        z, y = divmod(dp, edge)
        for v in range(sizes[1]):
            if (v % 2 == 0) == first:
                to = z * edge + (y + step) % edge
            else:
                to = ((z + step) % edge) * edge + y
            route.append((dp * sizes[1] + v, to * sizes[1] + v))
    return lax.ppermute(block, SIDE, route)


def line_move(block, lo, hi):
    count = lax.axis_size("vocab")
    route = [
        (s * count + v, (s ^ lo) * count + (v ^ (2 * hi)))
        for s in range(lax.axis_size("segment"))
        for v in range(count)
    ]
    return lax.ppermute(block, TOKENS, route)


def core_groups():
    total = lax.axis_size(ALL)
    return [list(range(core, total, 2)) for core in range(2)]


def spread_within(block, axes, groups):
    copies = jnp.broadcast_to(block[None], (len(groups[0]),) + block.shape)
    return lax.all_to_all(copies, axes, 0, 0, axis_index_groups=groups, tiled=True)


def sum_rows(mine, give, chip):
    rows, width = mine.shape
    both = (mine.astype(f32) + swap(give, "vocab", 1).astype(f32)).astype(bf16)
    both = both.reshape(4, rows // 4, width)

    def piece(mask):
        return lax.dynamic_index_in_dim(both, chip ^ mask, 0, False)

    moved = [line_move(piece(m), m & 1, m >> 1) for m in (1, 2, 3)]
    return (piece(0).astype(f32) + moved[0].astype(f32)) + (
        moved[1].astype(f32) + moved[2].astype(f32)
    )


def spread_rows(block, chip):
    rows, width = block.shape
    pieces = [block] + [line_move(block, m & 1, m >> 1) for m in (1, 2, 3)]
    half = jnp.zeros((4, rows, width), block.dtype)
    for mask in range(4):
        half = lax.dynamic_update_slice(half, pieces[mask][None], (chip ^ mask, 0, 0))
    half = half.reshape(4 * rows, width)
    return half, swap(half, "vocab", 1)


def prepare(counts, order, masks, placing_out, pick_out, masked_out):
    micro, slots, _ = placing_out.shape
    images = order.shape[1]
    each = slots // images
    cell = lax.broadcasted_iota(jnp.int32, (slots, slots), 0)
    slot = lax.broadcasted_iota(jnp.int32, (slots, slots), 1)
    tokens = pick_out.shape[1]
    seq_len = tokens // micro
    row = lax.broadcasted_iota(jnp.int32, pick_out.shape, 0)
    column = lax.broadcasted_iota(jnp.int32, pick_out.shape, 1)
    token = lax.broadcasted_iota(jnp.int32, masked_out.shape, 0)
    pick = jnp.zeros(pick_out.shape, f32)
    masked = jnp.zeros(masked_out.shape, f32)
    for m in range(micro):
        hit = jnp.zeros((slots, slots), f32)
        for i in range(images):
            within = slot - i * each
            inside = (within >= 0) & (within < each) & (cell == order[m, i] * each + within)
            live = jnp.where(i < counts[m, 0], 1.0, 0.0)
            hit = jnp.where(inside, live, hit)
        placing_out[m] = hit.astype(bf16)
        for p in range(MASKED):
            where = m * seq_len + masks[m, p]
            pick = jnp.where((row == m * MASKED + p) & (column == where), 1.0, pick)
            masked = jnp.where(token == where, 1.0, masked)
    pick_out[...] = pick.astype(bf16)
    masked_out[...] = masked


def add_parts(x, parts):
    total = parts[0][...].astype(f32) + parts[1][...].astype(f32)
    total = total + (parts[2][...].astype(f32) + parts[3][...].astype(f32))
    return (x[...].astype(f32) + total).astype(bf16)


STEP = 272


def hidden_of(layer, layers, normed, up):
    inner = dot_nt(normed, up)
    mine = lax.broadcasted_iota(jnp.int32, inner.shape, 1) % layers == layer
    return jnp.where(mine, jax.nn.gelu(inner, approximate=True), 0.0).astype(bf16)


def encode_first(up_far, down_far, x, part, up_rows, down_rows, up, down, sems):
    units, layers, depth = up.shape
    starts = list(range(0, units, STEP))
    copies = []
    for i, start in enumerate(starts):
        piece = pl.ds(start, min(STEP, units - start))
        for j, (far, near) in enumerate(((up_far, up), (down_far, down))):
            copies.append(pltpu.make_async_copy(far.at[piece], near.at[piece], sems.at[i, j]))
    start_all(copies)
    normed = layer_norm(x[...].astype(f32)).astype(bf16)
    total = jnp.zeros(normed.shape, f32)
    for i, start in enumerate(starts):
        stop = min(start + STEP, units)
        rows = slice(start * layers, stop * layers)
        shape = ((stop - start) * layers, depth)
        copies[2 * i].wait()
        up_piece = up[start:stop].reshape(shape)
        up_rows[rows, :] = up_piece
        inner = hidden_of(0, layers, normed, up_piece)
        copies[2 * i + 1].wait()
        down_piece = down[start:stop].reshape(shape)
        down_rows[rows, :] = down_piece
        total = total + dot(inner, down_piece)
    part[...] = total.astype(bf16)


def encode_next(layer, layers, up, down, x, p0, p1, p2, p3, part, current):
    now = add_parts(x, (p0, p1, p2, p3))
    current[...] = now
    normed = layer_norm(now.astype(f32)).astype(bf16)
    inner = hidden_of(layer, layers, normed, up[...])
    part[...] = dot(inner, down[...]).astype(bf16)


def encode_last(x, p0, p1, p2, p3, projector, current, columns):
    now = add_parts(x, (p0, p1, p2, p3))
    current[...] = now
    mine = dot(now, projector[...]).astype(bf16)
    for i in range(columns.shape[0]):
        columns[i] = mine


def turn(values, cosine, sine):
    return values * cosine + pltpu.roll(values, HD // 2, 1) * sine


def load_weights(targets, blocks, w, sems):
    rows = w.shape[1] // 16
    sources = [array.at[i] for array in blocks for i in range(array.shape[0])]
    parts = []
    for number, mats in enumerate((pl.ds(3, 1), pl.ds(0, 3))):
        copies = []
        for i, source in enumerate(sources):
            start = pl.multiple_of(targets[i] * rows, rows)
            copies.append(
                pltpu.make_async_copy(
                    source.at[mats], w.at[mats, pl.ds(start, rows), :], sems.at[number, i]
                )
            )
        parts.append(copies)
    return parts


def start_all(copies):
    for copy in copies:
        copy.start()


def wait_all(copies):
    for copy in copies:
        copy.wait()


def pairs_of(tokens, seq_len, half):
    return [
        (m, slice(m * seq_len, (m + 1) * seq_len), slice(h * HD, (h + 1) * HD))
        for m in range(tokens // seq_len)
        for h in range(half // HD)
    ]


def project_heads(hidden, w, cosine, sine, copies):
    half = w.shape[2]
    normed = norm_rows(hidden.astype(f32)).astype(bf16)
    wait_all(copies)
    q_all, k_all, v_all = (dot(normed, w[i]) for i in range(3))
    repeat = hidden.shape[0] // cosine.shape[0]
    cosine = jnp.concatenate([cosine[...]] * repeat, axis=0)
    sine = jnp.concatenate([sine[...]] * repeat, axis=0)

    def turned(values):
        return jnp.concatenate(
            [
                turn(values[:, h * HD : (h + 1) * HD], cosine, sine).astype(bf16)
                for h in range(half // HD)
            ],
            axis=1,
        )

    return turned(q_all), turned(k_all), v_all.astype(bf16)


def softmax(scores):
    powers = jnp.exp(scores - jnp.max(scores, axis=-1, keepdims=True))
    return powers / jnp.sum(powers, axis=-1, keepdims=True)


def attend(queries, keys, values):
    scores = [dot_nt(q, k) * HD ** (-0.5) for q, k in zip(queries, keys)]
    probs = [softmax(x).astype(bf16) for x in scores]
    return [dot(p, v).astype(bf16) for p, v in zip(probs, values)]


def attend_back(queries, keys, values, d_mixed):
    scores = [dot_nt(q, k) * HD ** (-0.5) for q, k in zip(queries, keys)]
    d_probs = [dot_nt(d, v).astype(bf16).astype(f32) for d, v in zip(d_mixed, values)]
    probs = [softmax(x) for x in scores]
    d_scores = [
        p * (d - jnp.sum(p * d, axis=-1, keepdims=True)) for p, d in zip(probs, d_probs)
    ]
    return (
        [(d * HD ** (-0.5)).astype(bf16) for d in d_scores],
        [p.astype(bf16) for p in probs],
    )


def split_halves(scalars, partial, keep, give):
    core, rows = scalars[16], keep.shape[0]
    keep[...] = partial[pl.ds(pl.multiple_of(core * rows, rows), rows), :]
    give[...] = partial[pl.ds(pl.multiple_of((1 - core) * rows, rows), rows), :]


def join_halves(scalars, own, other, whole):
    core, rows = scalars[16], own.shape[0]
    whole[pl.ds(pl.multiple_of(core * rows, rows), rows), :] = own[...]
    whole[pl.ds(pl.multiple_of((1 - core) * rows, rows), rows), :] = other[...]


def first_section(targets, *refs):
    blocks, refs = refs[:8], refs[8:]
    images, text, mask_row, placing, masked, cosine, sine = refs[:7]
    hidden, q, k, v, keep, give, mixed, w, sems, partial = refs[7:]
    out_copies, in_copies = load_weights(targets, blocks, w, sems)
    start_all(in_copies)
    start_all(out_copies)
    micro, slots, _ = placing.shape
    seq_len = cosine.shape[0]
    tokens, width = hidden.shape
    blocks_wide = images.shape[0] // micro
    part = width // blocks_wide
    half = q.shape[1]
    for m in range(micro):
        rows = slice(m * seq_len, (m + 1) * seq_len)
        hidden[rows, :] = jnp.where(masked[rows, :] > 0.0, mask_row[...], text[m])
        place = placing[m]
        filled = jnp.sum(place.astype(f32), axis=1, keepdims=True) > 0.0
        for b in range(blocks_wide):
            placed = dot(place, images[m * blocks_wide + b]).astype(bf16)
            cols = slice(b * part, (b + 1) * part)
            hidden[m * seq_len : m * seq_len + slots, cols] = jnp.where(
                filled, placed, text[m, :slots, cols]
            )
    q_all, k_all, v_all = project_heads(hidden[...], w, cosine, sine, in_copies)
    q[...] = q_all
    k[...] = k_all
    v[...] = v_all
    pairs = pairs_of(tokens, seq_len, half)
    results = attend(*([x[rows, cols] for _, rows, cols in pairs] for x in (q_all, k_all, v_all)))
    for (_, rows, cols), result in zip(pairs, results):
        mixed[rows, cols] = result
    wait_all(out_copies)
    partial[...] = dot_nt(mixed[...], w[3]).astype(bf16)
    split_halves(targets, partial, keep, give)


def last_section(targets, *refs):
    blocks, refs = refs[:8], refs[8:]
    own, other, pick, cosine, sine, q, k, v, partial, picked, mixed, w, sems, hidden = refs
    out_copies, in_copies = load_weights(targets, blocks, w, sems)
    start_all(in_copies)
    start_all(out_copies)
    join_halves(targets, own, other, hidden)
    picked[...] = dot(pick[...], hidden[...])
    q_all, k_all, v_all = project_heads(hidden[...], w, cosine, sine, in_copies)
    q_few = dot(pick[...], q_all).astype(bf16)
    q[...] = q_few
    k[...] = k_all
    v[...] = v_all
    pairs = pairs_of(hidden.shape[0], cosine.shape[0], k.shape[1])
    few = [slice(m * MASKED, (m + 1) * MASKED) for m, _, _ in pairs]
    results = attend(
        [q_few[mine, cols] for mine, (_, _, cols) in zip(few, pairs)],
        *([x[rows, cols] for _, rows, cols in pairs] for x in (k_all, v_all)),
    )
    for mine, (_, _, cols), result in zip(few, pairs, results):
        mixed[mine, cols] = result
    wait_all(out_copies)
    partial[...] = dot_nt(mixed[...], w[3]).astype(bf16)


def back_to_width(d_all, w):
    half = w.shape[2]
    total = dot_nt(d_all[:, :half].astype(bf16), w[0])
    for i in (1, 2):
        total = total + dot_nt(d_all[:, i * half : (i + 1) * half].astype(bf16), w[i])
    return total.astype(bf16)


def last_section_back(targets, *refs):
    blocks, refs = refs[:8], refs[8:]
    grad, pick, q, k, v, cosine, sine, keep, give, d_all, w, sems, partial = refs
    out_copies, in_copies = load_weights(targets, blocks, w, sems)
    start_all(out_copies)
    start_all(in_copies)
    half = k.shape[1]
    pairs = pairs_of(k.shape[0], cosine.shape[0], half)
    few = [slice(m * MASKED, (m + 1) * MASKED) for m, _, _ in pairs]
    queries = [q[mine, cols] for mine, (_, _, cols) in zip(few, pairs)]
    keys, values = ([x[rows, cols] for _, rows, cols in pairs] for x in (k, v))
    wait_all(out_copies)
    d_mixed = dot(grad[...], w[3]).astype(bf16)
    d_heads = [d_mixed[mine, cols] for mine, (_, _, cols) in zip(few, pairs)]
    d_scores, probs = attend_back(queries, keys, values, d_heads)
    d_q = [dot(d, k_h).astype(bf16) for d, k_h in zip(d_scores, keys)]
    d_k = [dot_tn(d, q_h).astype(bf16).astype(f32) for d, q_h in zip(d_scores, queries)]
    d_v = [dot_tn(p, d_h) for p, d_h in zip(probs, d_heads)]
    d_q = [
        dot_tn(pick[mine, rows], d) for mine, (_, rows, _), d in zip(few, pairs, d_q)
    ]
    back_sine = -sine[...]
    for i, (_, rows, cols) in enumerate(pairs):
        for part, d in enumerate(
            (turn(d_q[i], cosine[...], back_sine), turn(d_k[i], cosine[...], back_sine), d_v[i])
        ):
            at = part * half + cols.start
            d_all[rows, at : at + HD] = d.astype(bf16)
    wait_all(in_copies)
    partial[...] = back_to_width(d_all, w)
    split_halves(targets, partial, keep, give)


def first_section_back(slots, targets, *refs):
    blocks, refs = refs[:8], refs[8:]
    own, other, hidden, q, k, v, cosine, sine = refs[:8]
    chunks, grad_cols, hidden_cols, factor, d_all, w, sems, grad = refs[8:]
    join_halves(targets, own, other, grad)
    out_copies, in_copies = load_weights(targets, blocks, w, sems)
    start_all(out_copies)
    start_all(in_copies)
    half = k.shape[1]
    seq_len = cosine.shape[0]
    pairs = pairs_of(k.shape[0], seq_len, half)
    queries, keys, values = ([x[rows, cols] for _, rows, cols in pairs] for x in (q, k, v))
    wait_all(out_copies)
    d_mixed = dot(grad[...], w[3]).astype(bf16)
    d_heads = [d_mixed[rows, cols] for _, rows, cols in pairs]
    d_scores, probs = attend_back(queries, keys, values, d_heads)
    d_q = [dot(d, k_h)[:slots].astype(bf16).astype(f32) for d, k_h in zip(d_scores, keys)]
    d_k = [
        dot_tn(d, q_h)[:slots].astype(bf16).astype(f32) for d, q_h in zip(d_scores, queries)
    ]
    d_v = [dot_tn(p, d_h)[:slots] for p, d_h in zip(probs, d_heads)]
    cos_top, sin_top = cosine[:slots, :], -sine[:slots, :]
    for i, (m, _, cols) in enumerate(pairs):
        top = slice(m * slots, (m + 1) * slots)
        for part, d in enumerate(
            (turn(d_q[i], cos_top, sin_top), turn(d_k[i], cos_top, sin_top), d_v[i])
        ):
            at = part * half + cols.start
            d_all[top, at : at + HD] = d
    wait_all(in_copies)
    rounded = back_to_width(d_all, w)
    line, cells, _ = chunks.shape
    cols = grad_cols.shape[1]
    at = pl.multiple_of(targets[17] * cols, cols)
    lane = lax.broadcasted_iota(jnp.int32, (slots, chunks.shape[2] - cols), 1)
    for m in range(k.shape[0] // seq_len):
        top = slice(m * slots, (m + 1) * slots)
        rows = slice(m * seq_len, m * seq_len + slots)
        values = hidden[rows, :].astype(f32)
        mine = rounded[top, :]
        along = jnp.mean(mine.astype(f32) * values, axis=1, keepdims=True)
        high = along.astype(bf16).astype(f32)
        notes = jnp.where(lane == 0, high, jnp.where(lane == 1, along - high, 0.0)).astype(bf16)
        for c in range(line):
            chunks[c, top, :cols] = mine[:, c * cols : (c + 1) * cols]
            chunks[c, top, cols:] = notes
        factor[top, :] = inverse_rms(values)
        grad_cols[top, :] = grad[rows, pl.ds(at, cols)].astype(f32)
        hidden_cols[top, :] = hidden[rows, pl.ds(at, cols)].astype(f32)


def finish(parts, grad_cols, hidden_cols, factor, placing, encoded, out):
    cells, cols = grad_cols.shape
    total = parts[0].astype(f32)
    for c in range(1, parts.shape[0]):
        total = total + parts[c].astype(f32)
    along = total[:, cols : cols + 1] + total[:, cols + 1 : cols + 2]
    scale = factor[...]
    grad = grad_cols[...] + scale * total[:, :cols] - hidden_cols[...] * scale**3 * along
    grad = grad.astype(bf16)
    micro, slots, _ = placing.shape
    d_image = jnp.concatenate(
        [
            dot_tn(placing[m], grad[m * slots : (m + 1) * slots]).astype(bf16)
            for m in range(micro)
        ],
        axis=0,
    )
    total = dot_tn(encoded[...], d_image)
    owners, rows, _ = out.shape
    for i in range(owners):
        out[i] = total[i * rows : (i + 1) * rows].astype(bf16)


def slice_order(dp_index, core):
    z, y = dp_index // 4, dp_index % 4
    step = jnp.arange(4, dtype=jnp.int32)
    outer = ((jnp.where(core == 0, z, y) + step) % 4)[:, None]
    inner = ((jnp.where(core == 0, y, z) + step) % 4)[None, :]
    return jnp.where(core == 0, outer * 4 + inner, inner * 4 + outer).reshape(-1)


def second_moves(low, high):
    return (
        side_shift(low, 1, False),
        side_shift(high, -1, False),
        side_shift(high, 1, False),
        side_shift(low, -1, False),
    )


def in_order(low, high, moves):
    behind_low, ahead_high, behind_high, ahead_low = moves
    far_low = side_shift(behind_low, 1, False)
    far_high = side_shift(ahead_high, -1, False)
    return (low, high, ahead_low, ahead_high, far_low, far_high, behind_low, behind_high)


def shards(
    patches,
    text_embed,
    mask_embed,
    image_counts,
    image_order,
    masked_positions,
    ratio_index,
    enc_up,
    enc_down,
    projector,
    lang_qkv,
    lang_out,
    head_weight,
    teacher_logits,
):
    segment = lax.axis_index("segment")
    dp_index = lax.axis_index("dp")
    place = lax.axis_index("vocab") * 2 + segment
    core = lax.axis_index("vocab") % 2
    chip = (lax.axis_index("vocab") // 2) * 2 + segment
    line = lax.axis_size(LINE)
    dp_size = lax.axis_size("dp")
    micro = text_embed.shape[0]
    seq_len, width = text_embed.shape[2:]
    slots = patches.shape[2]
    depth = patches.shape[3]

    shard = jnp.concatenate(
        [lang_qkv[0], jnp.transpose(lang_out[0])[None]], axis=0
    )
    half = shard.shape[2] // 2
    low, high = shard[:, :, :half], shard[:, :, half:]
    keep = jnp.where(segment == 0, low, high)
    give = jnp.where(segment == 0, high, low)
    got = swap(give, "segment", 1)
    with_weights = dict(
        smem=1,
        far=8,
        scratch=(
            pltpu.VMEM((4, width, half), bf16),
            pltpu.SemaphoreType.DMA((2, 16)),
            pltpu.VMEM((micro * seq_len, width), bf16),
        ),
        mb=30,
    )

    layers, _, hidden_units = enc_up.shape
    tokens = micro * seq_len
    masked_rows = micro * MASKED
    placing, pick_all, masked = call(
        prepare,
        "prepare",
        [
            ((micro, slots, slots), bf16),
            ((masked_rows, tokens), bf16),
            ((tokens, 1), f32),
        ],
        image_counts,
        image_order[:, 0],
        masked_positions[:, 0],
        smem=3,
        mb=3,
        vmem=8,
    )
    up = jnp.transpose(enc_up, (2, 0, 1))
    down = jnp.transpose(enc_down, (1, 0, 2))

    def parts_of(part):
        return [part] + [swap(part, "vocab", mask) for mask in (1, 2, 3)]

    small = ((slots, depth), bf16)
    current = lax.dynamic_index_in_dim(patches[:, 0], segment, 0, False)
    layer_rows = (layers * hidden_units, depth)
    part, up_rows, down_rows = call(
        encode_first,
        "encode_first",
        [small, (layer_rows, bf16), (layer_rows, bf16)],
        up,
        down,
        current,
        far=2,
        scratch=(
            pltpu.VMEM(up.shape, bf16),
            pltpu.VMEM(down.shape, bf16),
            pltpu.SemaphoreType.DMA((-(-hidden_units // STEP), 2)),
        ),
        mb=30,
        vmem=36,
    )
    angles = jnp.arange(seq_len, dtype=f32)[:, None] * (
        rope_base ** (-2.0 * jnp.arange(HD // 2, dtype=f32) / HD)
    )
    cosine = jnp.concatenate([jnp.cos(angles), jnp.cos(angles)], axis=1)
    sine = jnp.concatenate([-jnp.sin(angles), jnp.sin(angles)], axis=1)
    targets = jnp.concatenate(
        [slice_order(dp_index, core), jnp.stack([core, place]).astype(jnp.int32)]
    )
    got, part = lax.optimization_barrier((got, part))
    first = segment == 0
    both = jnp.stack([jnp.where(first, keep, got), jnp.where(first, got, keep)])
    behind = side_shift(both, 1, True)
    ahead = side_shift(both, -1, True)
    first_parts = parts_of(part)
    behind, ahead, first_parts = lax.optimization_barrier((behind, ahead, first_parts))
    far = [side_shift(behind[0], 1, True), side_shift(ahead[1], -1, True)]
    part, current = call(
        functools.partial(encode_next, 1, layers),
        "encode_next",
        [small, small],
        up_rows,
        down_rows,
        current,
        *first_parts,
        mb=9,
        vmem=20,
    )
    far, part, placing, pick_all, masked, cosine, sine, targets = lax.optimization_barrier(
        (far, part, placing, pick_all, masked, cosine, sine, targets)
    )
    low = [jnp.stack([both[s], ahead[s]]) for s in range(2)]
    high = [jnp.stack([far[s], behind[s]]) for s in range(2)]
    moves = second_moves(low[0], high[0])
    encoded_own, image_cols = call(
        encode_last,
        "encode_last",
        [small, ((line, slots, projector.shape[1]), bf16)],
        current,
        *parts_of(part),
        projector,
        mb=10,
        vmem=12,
    )
    early, image_cols = lax.optimization_barrier((moves[:2], image_cols))
    moves = (*early, *moves[2:])
    w_first = in_order(low[0], high[0], moves)
    images = exchange(image_cols, TOKENS)
    w_first, images, low[1], high[1] = lax.optimization_barrier(
        (w_first, images, low[1], high[1])
    )
    moves = second_moves(low[1], high[1])
    encoded_other = swap(encoded_own, "segment", 1)
    encoded = jnp.concatenate(
        [
            jnp.where(segment == 0, encoded_own, encoded_other),
            jnp.where(segment == 0, encoded_other, encoded_own),
        ],
        axis=0,
    )

    chunk_rows = tokens // line
    row_start = (core * 4 + chip) * chunk_rows
    whole = ((tokens, width), bf16)
    halved = ((tokens // 2, width), bf16)
    heads = ((tokens, half), bf16)

    def own_rows(array):
        return lax.dynamic_slice_in_dim(array, row_start, chunk_rows, 0)

    hidden0, q0, k0, v0, keep_rows, give_rows, _ = call(
        first_section,
        "first_section",
        [whole, heads, heads, heads, halved, halved, heads],
        targets,
        *w_first,
        images,
        text_embed[:, 0],
        mask_embed[None, :],
        placing,
        masked,
        cosine,
        sine,
        **with_weights,
    )
    early, give_rows = lax.optimization_barrier((moves[:2], give_rows))
    mine = (own_rows(hidden0).astype(f32) + sum_rows(keep_rows, give_rows, chip)).astype(bf16)
    w_last = in_order(low[1], high[1], (*early, *moves[2:]))
    far, mine = lax.optimization_barrier((w_last[4:6], mine))
    w_last = (*w_last[:4], *far, *w_last[6:])
    hidden_halves = spread_rows(mine, chip)

    few_heads = ((masked_rows, half), bf16)
    q1, k1, v1, partial, picked, _ = call(
        last_section,
        "last_section",
        [
            few_heads,
            heads,
            heads,
            ((masked_rows, width), bf16),
            ((masked_rows, width), f32),
            few_heads,
        ],
        targets,
        *w_last,
        *hidden_halves,
        pick_all,
        cosine,
        sine,
        **with_weights,
    )
    cols = width // line
    parts = exchange(
        jnp.transpose(partial.reshape(masked_rows, line, cols), (1, 0, 2)), LINE
    )
    picked = lax.dynamic_slice_in_dim(picked, place * cols, cols, 1)
    last = (picked + jnp.sum(parts.astype(f32), axis=0)).astype(bf16)

    own_cols = spread_within(last, ALL, core_groups())
    other_cols = swap(own_cols, "vocab", 1)
    by_core = jnp.stack(
        [
            jnp.where(core == 0, own_cols, other_cols),
            jnp.where(core == 0, other_cols, own_cols),
        ]
    ).reshape(2, 2, dp_size, 2, masked_rows, cols)
    all_rows = jnp.transpose(by_core, (2, 4, 3, 0, 1, 5)).reshape(dp_size * masked_rows, width)
    row_count = all_rows.shape[0]
    final = norm_rows(all_rows.astype(f32)).astype(bf16)
    logits = dot_nt(final, head_weight)

    teacher = (
        jnp.transpose(teacher_logits.reshape(micro, dp_size, MASKED, -1), (1, 0, 2, 3))
        .reshape(row_count, -1)
        .astype(f32)
    )
    top = jnp.max(teacher, axis=1)
    powers = jnp.exp(teacher - top[:, None])
    stats = jnp.stack(
        [
            jnp.sum(jnp.exp(logits), axis=1),
            top,
            jnp.sum(powers, axis=1),
            jnp.sum(powers * (teacher - logits), axis=1),
        ]
    )
    stats = spread(stats, ALL).reshape(-1, 4, row_count)
    sum_student = jnp.sum(stats[:, 0], axis=0)
    top_all = jnp.max(stats[:, 1], axis=0)
    scale = jnp.exp(stats[:, 1] - top_all[None])
    sum_teacher = jnp.sum(stats[:, 2] * scale, axis=0)
    cross = jnp.sum(stats[:, 3] * scale, axis=0)
    norm_student = jnp.log(sum_student)
    norm_teacher = top_all + jnp.log(sum_teacher)
    divergence = cross / sum_teacher - norm_teacher + norm_student
    ratio = RATIOS / ratio_index.astype(f32)
    row_weights = jnp.repeat(jnp.transpose(ratio), MASKED, axis=1).reshape(-1)
    total = micro * dp_size
    loss = jnp.sum(row_weights * divergence) / total
    d_logits = (
        (row_weights / total)[:, None]
        * (jnp.exp(logits - norm_student[:, None]) - jnp.exp(teacher - norm_teacher[:, None]))
    ).astype(bf16)
    d_final = dot(d_logits, head_weight).astype(bf16)
    d_final = jnp.transpose(
        d_final.reshape(dp_size, masked_rows, 4, 2, cols), (3, 0, 2, 1, 4)
    ).reshape(-1, masked_rows, cols)
    d_own = jnp.sum(exchange(d_final, ALL).astype(f32), axis=0).astype(bf16)
    d_own = jnp.transpose(spread(d_own, LINE).reshape(line, masked_rows, cols), (1, 0, 2)).reshape(
        masked_rows, width
    )
    rows = lax.dynamic_slice_in_dim(all_rows, dp_index * masked_rows, masked_rows, 0)
    grad_rows = norm_back(rows.astype(f32), d_own.astype(f32)).astype(bf16)

    keep_rows, give_rows, _ = call(
        last_section_back,
        "last_section_back",
        [halved, halved, ((tokens, 3 * half), bf16)],
        targets,
        *w_last,
        grad_rows,
        pick_all,
        q1,
        k1,
        v1,
        cosine,
        sine,
        **with_weights,
    )
    d_normed = sum_rows(keep_rows, give_rows, chip)
    own_pick = lax.dynamic_slice_in_dim(pick_all, row_start, chunk_rows, 1)
    grad_own = dot_tn(own_pick, grad_rows)
    grad_own = (grad_own + norm_back(mine.astype(f32), d_normed)).astype(bf16)
    grad_halves = spread_rows(grad_own, chip)

    cells = micro * slots
    columns = ((cells, cols), f32)
    chunks, grad_cols, hidden_cols, factor, _ = call(
        functools.partial(first_section_back, slots),
        "first_section_back",
        [
            ((line, cells, cols + 128), bf16),
            columns,
            columns,
            ((cells, 1), f32),
            ((cells, 3 * half), f32),
        ],
        targets,
        *w_first,
        *grad_halves,
        hidden0,
        q0,
        k0,
        v0,
        cosine,
        sine,
        **with_weights,
    )
    owners = 2 * dp_size
    (proj_part,) = call(
        finish,
        "finish",
        [((owners, depth // owners, cols), bf16)],
        exchange(chunks, LINE),
        grad_cols,
        hidden_cols,
        factor,
        placing,
        encoded,
        mb=8,
    )
    parts = exchange(proj_part, ("segment", "dp"))
    parts = jnp.sum(parts.astype(f32).reshape(2, dp_size, depth // owners, cols), axis=1)
    projector_grad = jnp.transpose(parts, (1, 0, 2)).reshape(depth // owners, 2 * cols)
    return (loss, projector_grad)


def solution(mesh):
    placed = (
        P(None, "dp", None, None),
        P(None, "dp", None, None),
        P(),
        P(None, "dp"),
        P(None, "dp", None),
        P(None, "dp", None),
        P(),
        P(None, None, "vocab"),
        P(None, "vocab", None),
        P(None, "vocab"),
        P("segment", None, "dp", "vocab"),
        P("segment", "vocab", "dp"),
        P(("segment", "dp", "vocab"), None),
        P(None, ("segment", "dp", "vocab")),
    )
    return jax.shard_map(
        shards,
        mesh=mesh,
        in_specs=placed,
        out_specs=(P(), P(("segment", "dp"), "vocab")),
        check_vma=False,
    )
```

```python
import functools

import jax
import jax.numpy as jnp
from jax import lax
from jax.experimental import pallas as pl
from jax.experimental.pallas import tpu as pltpu
from jax.sharding import PartitionSpec as P

HD = 128
MASKED = 4
RATIOS = 8

epsilon = 1e-06
rope_base = 500000.0

LINE = ("vocab", "segment")
ALL = ("segment", "dp", "vocab")
f32 = jnp.float32
bf16 = jnp.bfloat16


def dot(a, b):
    return jnp.dot(a, b, preferred_element_type=f32)


def dot_nt(a, b):
    return lax.dot_general(a, b, (((1,), (1,)), ((), ())), preferred_element_type=f32)


def dot_tn(a, b):
    return lax.dot_general(a, b, (((0,), (0,)), ((), ())), preferred_element_type=f32)


def swap(block, axis, mask):
    return lax.ppermute(block, axis, [(i, i ^ mask) for i in range(lax.axis_size(axis))])


def exchange(chunks, axes):
    return lax.all_to_all(chunks, axes, 0, 0, tiled=True)


def spread(block, axes):
    size = lax.axis_size(axes)
    return exchange(jnp.broadcast_to(block[None], (size,) + block.shape), axes)


def inverse_rms(values_in):
    return lax.rsqrt(jnp.mean(values_in * values_in, axis=-1, keepdims=True) + epsilon)


def norm_rows(values_in):
    return values_in * inverse_rms(values_in)


def layer_norm(values_in):
    centred = values_in - jnp.mean(values_in, axis=-1, keepdims=True)
    return centred * lax.rsqrt(jnp.mean(centred * centred, axis=-1, keepdims=True) + epsilon)


def norm_back(values_in, cotangent):
    factor = inverse_rms(values_in)
    return factor * cotangent - values_in * factor**3 * jnp.mean(
        cotangent * values_in, axis=-1, keepdims=True
    )


SIDE = ("dp", "vocab")
TOKENS = ("segment", "vocab")


def call(body, name, outs, *args, smem=0, far=0, scratch=(), mb=0, vmem=56):
    specs = [pl.BlockSpec(memory_space=pltpu.SMEM)] * smem + [
        pl.BlockSpec(memory_space=pl.ANY)
    ] * far
    specs += [pl.BlockSpec(memory_space=pltpu.VMEM)] * (len(args) - len(specs))
    return pl.pallas_call(
        body,
        name=name,
        out_shape=[jax.ShapeDtypeStruct(shape, kind) for shape, kind in outs],
        in_specs=specs,
        out_specs=[pl.BlockSpec(memory_space=pltpu.VMEM) for _ in outs],
        scratch_shapes=list(scratch),
        cost_estimate=pl.CostEstimate(flops=0, bytes_accessed=mb * 1000000, transcendentals=0),
        compiler_params=pltpu.CompilerParams(vmem_limit_bytes=vmem << 20),
    )(*args)


def side_shift(block, step, first):
    sizes = (lax.axis_size("dp"), lax.axis_size("vocab"))
    edge = 4
    route = []
    for dp in range(sizes[0]):
        z, y = divmod(dp, edge)
        for v in range(sizes[1]):
            if (v % 2 == 0) == first:
                to = z * edge + (y + step) % edge
            else:
                to = ((z + step) % edge) * edge + y
            route.append((dp * sizes[1] + v, to * sizes[1] + v))
    return lax.ppermute(block, SIDE, route)


def line_move(block, lo, hi):
    count = lax.axis_size("vocab")
    route = [
        (s * count + v, (s ^ lo) * count + (v ^ (2 * hi)))
        for s in range(lax.axis_size("segment"))
        for v in range(count)
    ]
    return lax.ppermute(block, TOKENS, route)


def core_groups():
    total = lax.axis_size(ALL)
    return [list(range(core, total, 2)) for core in range(2)]


def spread_within(block, axes, groups):
    copies = jnp.broadcast_to(block[None], (len(groups[0]),) + block.shape)
    return lax.all_to_all(copies, axes, 0, 0, axis_index_groups=groups, tiled=True)


def sum_rows(mine, give, chip):
    rows, width = mine.shape
    both = (mine.astype(f32) + swap(give, "vocab", 1).astype(f32)).astype(bf16)
    both = both.reshape(4, rows // 4, width)

    def piece(mask):
        return lax.dynamic_index_in_dim(both, chip ^ mask, 0, False)

    moved = [line_move(piece(m), m & 1, m >> 1) for m in (1, 2, 3)]
    return (piece(0).astype(f32) + moved[0].astype(f32)) + (
        moved[1].astype(f32) + moved[2].astype(f32)
    )


def spread_rows(block, chip):
    rows, width = block.shape
    pieces = [block] + [line_move(block, m & 1, m >> 1) for m in (1, 2, 3)]
    half = jnp.zeros((4, rows, width), block.dtype)
    for mask in range(4):
        half = lax.dynamic_update_slice(half, pieces[mask][None], (chip ^ mask, 0, 0))
    half = half.reshape(4 * rows, width)
    return half, swap(half, "vocab", 1)


def prepare(counts, order, masks, placing_out, pick_out, masked_out):
    micro, slots, _ = placing_out.shape
    images = order.shape[1]
    each = slots // images
    cell = lax.broadcasted_iota(jnp.int32, (slots, slots), 0)
    slot = lax.broadcasted_iota(jnp.int32, (slots, slots), 1)
    tokens = pick_out.shape[1]
    seq_len = tokens // micro
    row = lax.broadcasted_iota(jnp.int32, pick_out.shape, 0)
    column = lax.broadcasted_iota(jnp.int32, pick_out.shape, 1)
    token = lax.broadcasted_iota(jnp.int32, masked_out.shape, 0)
    pick = jnp.zeros(pick_out.shape, f32)
    masked = jnp.zeros(masked_out.shape, f32)
    for m in range(micro):
        hit = jnp.zeros((slots, slots), f32)
        for i in range(images):
            within = slot - i * each
            inside = (within >= 0) & (within < each) & (cell == order[m, i] * each + within)
            live = jnp.where(i < counts[m, 0], 1.0, 0.0)
            hit = jnp.where(inside, live, hit)
        placing_out[m] = hit.astype(bf16)
        for p in range(MASKED):
            where = m * seq_len + masks[m, p]
            pick = jnp.where((row == m * MASKED + p) & (column == where), 1.0, pick)
            masked = jnp.where(token == where, 1.0, masked)
    pick_out[...] = pick.astype(bf16)
    masked_out[...] = masked


def add_parts(x, parts):
    total = parts[0][...].astype(f32) + parts[1][...].astype(f32)
    total = total + (parts[2][...].astype(f32) + parts[3][...].astype(f32))
    return (x[...].astype(f32) + total).astype(bf16)


STEP = 272


def mlp(layer, current, up_far, down_far, up, down, sems):
    units, layers, _ = up.shape
    starts = list(range(0, units, STEP))
    copies = []
    for i, start in enumerate(starts):
        part = pl.ds(start, min(STEP, units - start))
        for j, (far, near) in enumerate(((up_far, up), (down_far, down))):
            copies.append(pltpu.make_async_copy(far.at[part], near.at[part], sems.at[i, j]))
    start_all(copies)
    normed = layer_norm(current().astype(f32)).astype(bf16)
    total = jnp.zeros(normed.shape, f32)
    for i, start in enumerate(starts):
        part = slice(start, min(start + STEP, units))
        shape = ((part.stop - start) * layers, up.shape[2])
        copies[2 * i].wait()
        inner = dot_nt(normed, up[part].reshape(shape))
        mine = lax.broadcasted_iota(jnp.int32, inner.shape, 1) % layers == layer
        inner = jnp.where(mine, jax.nn.gelu(inner, approximate=True), 0.0).astype(bf16)
        copies[2 * i + 1].wait()
        total = total + dot(inner, down[part].reshape(shape))
    return total.astype(bf16)


def encode_first(up_far, down_far, x, part, up, down, sems):
    part[...] = mlp(0, lambda: x[...], up_far, down_far, up, down, sems)


def encode_next(layer, up_far, down_far, x, p0, p1, p2, p3, part, current, up, down, sems):
    def now():
        value = add_parts(x, (p0, p1, p2, p3))
        current[...] = value
        return value

    part[...] = mlp(layer, now, up_far, down_far, up, down, sems)


def encode_last(x, p0, p1, p2, p3, projector, current, columns):
    now = add_parts(x, (p0, p1, p2, p3))
    current[...] = now
    mine = dot(now, projector[...]).astype(bf16)
    for i in range(columns.shape[0]):
        columns[i] = mine


def turn(values, cosine, sine):
    return values * cosine + pltpu.roll(values, HD // 2, 1) * sine


def load_weights(targets, blocks, w, sems):
    rows = w.shape[1] // 16
    sources = [array.at[i] for array in blocks for i in range(array.shape[0])]
    parts = []
    for number, mats in enumerate((pl.ds(3, 1), pl.ds(0, 3))):
        copies = []
        for i, source in enumerate(sources):
            start = pl.multiple_of(targets[i] * rows, rows)
            copies.append(
                pltpu.make_async_copy(
                    source.at[mats], w.at[mats, pl.ds(start, rows), :], sems.at[number, i]
                )
            )
        parts.append(copies)
    return parts


def start_all(copies):
    for copy in copies:
        copy.start()


def wait_all(copies):
    for copy in copies:
        copy.wait()


def pairs_of(tokens, seq_len, half):
    return [
        (m, slice(m * seq_len, (m + 1) * seq_len), slice(h * HD, (h + 1) * HD))
        for m in range(tokens // seq_len)
        for h in range(half // HD)
    ]


def project_heads(hidden, w, cosine, sine, copies):
    half = w.shape[2]
    normed = norm_rows(hidden.astype(f32)).astype(bf16)
    wait_all(copies)
    q_all, k_all, v_all = (dot(normed, w[i]) for i in range(3))
    repeat = hidden.shape[0] // cosine.shape[0]
    cosine = jnp.concatenate([cosine[...]] * repeat, axis=0)
    sine = jnp.concatenate([sine[...]] * repeat, axis=0)

    def turned(values):
        return jnp.concatenate(
            [
                turn(values[:, h * HD : (h + 1) * HD], cosine, sine).astype(bf16)
                for h in range(half // HD)
            ],
            axis=1,
        )

    return turned(q_all), turned(k_all), v_all.astype(bf16)


def softmax(scores):
    powers = jnp.exp(scores - jnp.max(scores, axis=-1, keepdims=True))
    return powers / jnp.sum(powers, axis=-1, keepdims=True)


def attend(queries, keys, values):
    scores = [dot_nt(q, k) * HD ** (-0.5) for q, k in zip(queries, keys)]
    probs = [softmax(x).astype(bf16) for x in scores]
    return [dot(p, v).astype(bf16) for p, v in zip(probs, values)]


def attend_back(queries, keys, values, d_mixed):
    scores = [dot_nt(q, k) * HD ** (-0.5) for q, k in zip(queries, keys)]
    d_probs = [dot_nt(d, v).astype(bf16).astype(f32) for d, v in zip(d_mixed, values)]
    probs = [softmax(x) for x in scores]
    d_scores = [
        p * (d - jnp.sum(p * d, axis=-1, keepdims=True)) for p, d in zip(probs, d_probs)
    ]
    return (
        [(d * HD ** (-0.5)).astype(bf16) for d in d_scores],
        [p.astype(bf16) for p in probs],
    )


def split_halves(scalars, partial, keep, give):
    core, rows = scalars[16], keep.shape[0]
    keep[...] = partial[pl.ds(pl.multiple_of(core * rows, rows), rows), :]
    give[...] = partial[pl.ds(pl.multiple_of((1 - core) * rows, rows), rows), :]


def join_halves(scalars, own, other, whole):
    core, rows = scalars[16], own.shape[0]
    whole[pl.ds(pl.multiple_of(core * rows, rows), rows), :] = own[...]
    whole[pl.ds(pl.multiple_of((1 - core) * rows, rows), rows), :] = other[...]


def first_section(targets, *refs):
    blocks, refs = refs[:8], refs[8:]
    images, text, mask_row, placing, masked, cosine, sine = refs[:7]
    hidden, q, k, v, keep, give, mixed, w, sems, partial = refs[7:]
    out_copies, in_copies = load_weights(targets, blocks, w, sems)
    start_all(in_copies)
    start_all(out_copies)
    micro, slots, _ = placing.shape
    seq_len = cosine.shape[0]
    tokens, width = hidden.shape
    blocks_wide = images.shape[0] // micro
    part = width // blocks_wide
    half = q.shape[1]
    for m in range(micro):
        rows = slice(m * seq_len, (m + 1) * seq_len)
        hidden[rows, :] = jnp.where(masked[rows, :] > 0.0, mask_row[...], text[m])
        place = placing[m]
        filled = jnp.sum(place.astype(f32), axis=1, keepdims=True) > 0.0
        for b in range(blocks_wide):
            placed = dot(place, images[m * blocks_wide + b]).astype(bf16)
            cols = slice(b * part, (b + 1) * part)
            hidden[m * seq_len : m * seq_len + slots, cols] = jnp.where(
                filled, placed, text[m, :slots, cols]
            )
    q_all, k_all, v_all = project_heads(hidden[...], w, cosine, sine, in_copies)
    q[...] = q_all
    k[...] = k_all
    v[...] = v_all
    pairs = pairs_of(tokens, seq_len, half)
    results = attend(*([x[rows, cols] for _, rows, cols in pairs] for x in (q_all, k_all, v_all)))
    for (_, rows, cols), result in zip(pairs, results):
        mixed[rows, cols] = result
    wait_all(out_copies)
    partial[...] = dot_nt(mixed[...], w[3]).astype(bf16)
    split_halves(targets, partial, keep, give)


def last_section(targets, *refs):
    blocks, refs = refs[:8], refs[8:]
    own, other, pick, cosine, sine, q, k, v, partial, picked, mixed, w, sems, hidden = refs
    out_copies, in_copies = load_weights(targets, blocks, w, sems)
    start_all(in_copies)
    start_all(out_copies)
    join_halves(targets, own, other, hidden)
    picked[...] = dot(pick[...], hidden[...])
    q_all, k_all, v_all = project_heads(hidden[...], w, cosine, sine, in_copies)
    q_few = dot(pick[...], q_all).astype(bf16)
    q[...] = q_few
    k[...] = k_all
    v[...] = v_all
    pairs = pairs_of(hidden.shape[0], cosine.shape[0], k.shape[1])
    few = [slice(m * MASKED, (m + 1) * MASKED) for m, _, _ in pairs]
    results = attend(
        [q_few[mine, cols] for mine, (_, _, cols) in zip(few, pairs)],
        *([x[rows, cols] for _, rows, cols in pairs] for x in (k_all, v_all)),
    )
    for mine, (_, _, cols), result in zip(few, pairs, results):
        mixed[mine, cols] = result
    wait_all(out_copies)
    partial[...] = dot_nt(mixed[...], w[3]).astype(bf16)


def back_to_width(d_all, w):
    half = w.shape[2]
    total = dot_nt(d_all[:, :half].astype(bf16), w[0])
    for i in (1, 2):
        total = total + dot_nt(d_all[:, i * half : (i + 1) * half].astype(bf16), w[i])
    return total.astype(bf16)


def last_section_back(targets, *refs):
    blocks, refs = refs[:8], refs[8:]
    grad, pick, q, k, v, cosine, sine, keep, give, d_all, w, sems, partial = refs
    out_copies, in_copies = load_weights(targets, blocks, w, sems)
    start_all(out_copies)
    start_all(in_copies)
    half = k.shape[1]
    pairs = pairs_of(k.shape[0], cosine.shape[0], half)
    few = [slice(m * MASKED, (m + 1) * MASKED) for m, _, _ in pairs]
    queries = [q[mine, cols] for mine, (_, _, cols) in zip(few, pairs)]
    keys, values = ([x[rows, cols] for _, rows, cols in pairs] for x in (k, v))
    wait_all(out_copies)
    d_mixed = dot(grad[...], w[3]).astype(bf16)
    d_heads = [d_mixed[mine, cols] for mine, (_, _, cols) in zip(few, pairs)]
    d_scores, probs = attend_back(queries, keys, values, d_heads)
    d_q = [dot(d, k_h).astype(bf16) for d, k_h in zip(d_scores, keys)]
    d_k = [dot_tn(d, q_h).astype(bf16).astype(f32) for d, q_h in zip(d_scores, queries)]
    d_v = [dot_tn(p, d_h) for p, d_h in zip(probs, d_heads)]
    d_q = [
        dot_tn(pick[mine, rows], d) for mine, (_, rows, _), d in zip(few, pairs, d_q)
    ]
    back_sine = -sine[...]
    for i, (_, rows, cols) in enumerate(pairs):
        for part, d in enumerate(
            (turn(d_q[i], cosine[...], back_sine), turn(d_k[i], cosine[...], back_sine), d_v[i])
        ):
            at = part * half + cols.start
            d_all[rows, at : at + HD] = d.astype(bf16)
    wait_all(in_copies)
    partial[...] = back_to_width(d_all, w)
    split_halves(targets, partial, keep, give)


def first_section_back(slots, targets, *refs):
    blocks, refs = refs[:8], refs[8:]
    own, other, hidden, q, k, v, cosine, sine = refs[:8]
    chunks, grad_cols, hidden_cols, factor, d_all, w, sems, grad = refs[8:]
    join_halves(targets, own, other, grad)
    out_copies, in_copies = load_weights(targets, blocks, w, sems)
    start_all(out_copies)
    start_all(in_copies)
    half = k.shape[1]
    seq_len = cosine.shape[0]
    pairs = pairs_of(k.shape[0], seq_len, half)
    queries, keys, values = ([x[rows, cols] for _, rows, cols in pairs] for x in (q, k, v))
    wait_all(out_copies)
    d_mixed = dot(grad[...], w[3]).astype(bf16)
    d_heads = [d_mixed[rows, cols] for _, rows, cols in pairs]
    d_scores, probs = attend_back(queries, keys, values, d_heads)
    d_q = [dot(d, k_h)[:slots].astype(bf16).astype(f32) for d, k_h in zip(d_scores, keys)]
    d_k = [
        dot_tn(d, q_h)[:slots].astype(bf16).astype(f32) for d, q_h in zip(d_scores, queries)
    ]
    d_v = [dot_tn(p, d_h)[:slots] for p, d_h in zip(probs, d_heads)]
    cos_top, sin_top = cosine[:slots, :], -sine[:slots, :]
    for i, (m, _, cols) in enumerate(pairs):
        top = slice(m * slots, (m + 1) * slots)
        for part, d in enumerate(
            (turn(d_q[i], cos_top, sin_top), turn(d_k[i], cos_top, sin_top), d_v[i])
        ):
            at = part * half + cols.start
            d_all[top, at : at + HD] = d
    wait_all(in_copies)
    rounded = back_to_width(d_all, w)
    line, cells, _ = chunks.shape
    cols = grad_cols.shape[1]
    at = pl.multiple_of(targets[17] * cols, cols)
    lane = lax.broadcasted_iota(jnp.int32, (slots, chunks.shape[2] - cols), 1)
    for m in range(k.shape[0] // seq_len):
        top = slice(m * slots, (m + 1) * slots)
        rows = slice(m * seq_len, m * seq_len + slots)
        values = hidden[rows, :].astype(f32)
        mine = rounded[top, :]
        along = jnp.mean(mine.astype(f32) * values, axis=1, keepdims=True)
        high = along.astype(bf16).astype(f32)
        notes = jnp.where(lane == 0, high, jnp.where(lane == 1, along - high, 0.0)).astype(bf16)
        for c in range(line):
            chunks[c, top, :cols] = mine[:, c * cols : (c + 1) * cols]
            chunks[c, top, cols:] = notes
        factor[top, :] = inverse_rms(values)
        grad_cols[top, :] = grad[rows, pl.ds(at, cols)].astype(f32)
        hidden_cols[top, :] = hidden[rows, pl.ds(at, cols)].astype(f32)


def finish(parts, grad_cols, hidden_cols, factor, placing, encoded, out):
    cells, cols = grad_cols.shape
    total = parts[0].astype(f32)
    for c in range(1, parts.shape[0]):
        total = total + parts[c].astype(f32)
    along = total[:, cols : cols + 1] + total[:, cols + 1 : cols + 2]
    scale = factor[...]
    grad = grad_cols[...] + scale * total[:, :cols] - hidden_cols[...] * scale**3 * along
    grad = grad.astype(bf16)
    micro, slots, _ = placing.shape
    d_image = jnp.concatenate(
        [
            dot_tn(placing[m], grad[m * slots : (m + 1) * slots]).astype(bf16)
            for m in range(micro)
        ],
        axis=0,
    )
    total = dot_tn(encoded[...], d_image)
    owners, rows, _ = out.shape
    for i in range(owners):
        out[i] = total[i * rows : (i + 1) * rows].astype(bf16)


def slice_order(dp_index, core):
    z, y = dp_index // 4, dp_index % 4
    step = jnp.arange(4, dtype=jnp.int32)
    outer = ((jnp.where(core == 0, z, y) + step) % 4)[:, None]
    inner = ((jnp.where(core == 0, y, z) + step) % 4)[None, :]
    return jnp.where(core == 0, outer * 4 + inner, inner * 4 + outer).reshape(-1)


def second_moves(low, high):
    return (
        side_shift(low, 1, False),
        side_shift(high, -1, False),
        side_shift(high, 1, False),
        side_shift(low, -1, False),
    )


def in_order(low, high, moves):
    behind_low, ahead_high, behind_high, ahead_low = moves
    far_low = side_shift(behind_low, 1, False)
    far_high = side_shift(ahead_high, -1, False)
    return (low, high, ahead_low, ahead_high, far_low, far_high, behind_low, behind_high)


def shards(
    patches,
    text_embed,
    mask_embed,
    image_counts,
    image_order,
    masked_positions,
    ratio_index,
    enc_up,
    enc_down,
    projector,
    lang_qkv,
    lang_out,
    head_weight,
    teacher_logits,
):
    segment = lax.axis_index("segment")
    dp_index = lax.axis_index("dp")
    place = lax.axis_index("vocab") * 2 + segment
    core = lax.axis_index("vocab") % 2
    chip = (lax.axis_index("vocab") // 2) * 2 + segment
    line = lax.axis_size(LINE)
    dp_size = lax.axis_size("dp")
    micro = text_embed.shape[0]
    seq_len, width = text_embed.shape[2:]
    slots = patches.shape[2]
    depth = patches.shape[3]

    shard = jnp.concatenate(
        [lang_qkv[0], jnp.transpose(lang_out[0])[None]], axis=0
    )
    half = shard.shape[2] // 2
    low, high = shard[:, :, :half], shard[:, :, half:]
    keep = jnp.where(segment == 0, low, high)
    give = jnp.where(segment == 0, high, low)
    got = swap(give, "segment", 1)
    with_weights = dict(
        smem=1,
        far=8,
        scratch=(
            pltpu.VMEM((4, width, half), bf16),
            pltpu.SemaphoreType.DMA((2, 16)),
            pltpu.VMEM((micro * seq_len, width), bf16),
        ),
        mb=30,
    )

    layers, _, hidden_units = enc_up.shape
    tokens = micro * seq_len
    masked_rows = micro * MASKED
    placing, pick_all, masked = call(
        prepare,
        "prepare",
        [
            ((micro, slots, slots), bf16),
            ((masked_rows, tokens), bf16),
            ((tokens, 1), f32),
        ],
        image_counts,
        image_order[:, 0],
        masked_positions[:, 0],
        smem=3,
        mb=3,
    )
    up = jnp.transpose(enc_up, (2, 0, 1))
    down = jnp.transpose(enc_down, (1, 0, 2))

    def parts_of(part):
        return [part] + [swap(part, "vocab", mask) for mask in (1, 2, 3)]

    small = ((slots, depth), bf16)
    current = lax.dynamic_index_in_dim(patches[:, 0], segment, 0, False)
    with_layers = dict(
        far=2,
        scratch=(
            pltpu.VMEM(up.shape, bf16),
            pltpu.VMEM(down.shape, bf16),
            pltpu.SemaphoreType.DMA((-(-hidden_units // STEP), 2)),
        ),
        mb=20,
    )
    (part,) = call(encode_first, "encode_first", [small], up, down, current, **with_layers)
    angles = jnp.arange(seq_len, dtype=f32)[:, None] * (
        rope_base ** (-2.0 * jnp.arange(HD // 2, dtype=f32) / HD)
    )
    cosine = jnp.concatenate([jnp.cos(angles), jnp.cos(angles)], axis=1)
    sine = jnp.concatenate([-jnp.sin(angles), jnp.sin(angles)], axis=1)
    targets = jnp.concatenate(
        [slice_order(dp_index, core), jnp.stack([core, place]).astype(jnp.int32)]
    )
    got, part, placing, pick_all, masked, cosine, sine, targets = lax.optimization_barrier(
        (got, part, placing, pick_all, masked, cosine, sine, targets)
    )
    first = segment == 0
    both = jnp.stack([jnp.where(first, keep, got), jnp.where(first, got, keep)])
    behind = side_shift(both, 1, True)
    ahead = side_shift(both, -1, True)
    first_parts = parts_of(part)
    behind, ahead, first_parts = lax.optimization_barrier((behind, ahead, first_parts))
    far = [side_shift(behind[0], 1, True), side_shift(ahead[1], -1, True)]
    part, current = call(
        functools.partial(encode_next, 1),
        "encode_next",
        [small, small],
        up,
        down,
        current,
        *first_parts,
        **with_layers,
    )
    far, part = lax.optimization_barrier((far, part))
    low = [jnp.stack([both[s], ahead[s]]) for s in range(2)]
    high = [jnp.stack([far[s], behind[s]]) for s in range(2)]
    moves = second_moves(low[0], high[0])
    encoded_own, image_cols = call(
        encode_last,
        "encode_last",
        [small, ((line, slots, projector.shape[1]), bf16)],
        current,
        *parts_of(part),
        projector,
        mb=10,
        vmem=12,
    )
    early, image_cols = lax.optimization_barrier((moves[:2], image_cols))
    moves = (*early, *moves[2:])
    w_first = in_order(low[0], high[0], moves)
    images = exchange(image_cols, TOKENS)
    w_first, images, low[1], high[1] = lax.optimization_barrier(
        (w_first, images, low[1], high[1])
    )
    moves = second_moves(low[1], high[1])
    encoded_other = swap(encoded_own, "segment", 1)
    encoded = jnp.concatenate(
        [
            jnp.where(segment == 0, encoded_own, encoded_other),
            jnp.where(segment == 0, encoded_other, encoded_own),
        ],
        axis=0,
    )

    chunk_rows = tokens // line
    row_start = (core * 4 + chip) * chunk_rows
    whole = ((tokens, width), bf16)
    halved = ((tokens // 2, width), bf16)
    heads = ((tokens, half), bf16)

    def own_rows(array):
        return lax.dynamic_slice_in_dim(array, row_start, chunk_rows, 0)

    hidden0, q0, k0, v0, keep_rows, give_rows, _ = call(
        first_section,
        "first_section",
        [whole, heads, heads, heads, halved, halved, heads],
        targets,
        *w_first,
        images,
        text_embed[:, 0],
        mask_embed[None, :],
        placing,
        masked,
        cosine,
        sine,
        **with_weights,
    )
    early, give_rows = lax.optimization_barrier((moves[:2], give_rows))
    mine = (own_rows(hidden0).astype(f32) + sum_rows(keep_rows, give_rows, chip)).astype(bf16)
    w_last = in_order(low[1], high[1], (*early, *moves[2:]))
    far, mine = lax.optimization_barrier((w_last[4:6], mine))
    w_last = (*w_last[:4], *far, *w_last[6:])
    hidden_halves = spread_rows(mine, chip)

    few_heads = ((masked_rows, half), bf16)
    q1, k1, v1, partial, picked, _ = call(
        last_section,
        "last_section",
        [
            few_heads,
            heads,
            heads,
            ((masked_rows, width), bf16),
            ((masked_rows, width), f32),
            few_heads,
        ],
        targets,
        *w_last,
        *hidden_halves,
        pick_all,
        cosine,
        sine,
        **with_weights,
    )
    cols = width // line
    parts = exchange(
        jnp.transpose(partial.reshape(masked_rows, line, cols), (1, 0, 2)), LINE
    )
    picked = lax.dynamic_slice_in_dim(picked, place * cols, cols, 1)
    last = (picked + jnp.sum(parts.astype(f32), axis=0)).astype(bf16)

    own_cols = spread_within(last, ALL, core_groups())
    other_cols = swap(own_cols, "vocab", 1)
    by_core = jnp.stack(
        [
            jnp.where(core == 0, own_cols, other_cols),
            jnp.where(core == 0, other_cols, own_cols),
        ]
    ).reshape(2, 2, dp_size, 2, masked_rows, cols)
    all_rows = jnp.transpose(by_core, (2, 4, 3, 0, 1, 5)).reshape(dp_size * masked_rows, width)
    row_count = all_rows.shape[0]
    final = norm_rows(all_rows.astype(f32)).astype(bf16)
    logits = dot_nt(final, head_weight)

    teacher = (
        jnp.transpose(teacher_logits.reshape(micro, dp_size, MASKED, -1), (1, 0, 2, 3))
        .reshape(row_count, -1)
        .astype(f32)
    )
    top = jnp.max(teacher, axis=1)
    powers = jnp.exp(teacher - top[:, None])
    stats = jnp.stack(
        [
            jnp.sum(jnp.exp(logits), axis=1),
            top,
            jnp.sum(powers, axis=1),
            jnp.sum(powers * (teacher - logits), axis=1),
        ]
    )
    stats = spread(stats, ALL).reshape(-1, 4, row_count)
    sum_student = jnp.sum(stats[:, 0], axis=0)
    top_all = jnp.max(stats[:, 1], axis=0)
    scale = jnp.exp(stats[:, 1] - top_all[None])
    sum_teacher = jnp.sum(stats[:, 2] * scale, axis=0)
    cross = jnp.sum(stats[:, 3] * scale, axis=0)
    norm_student = jnp.log(sum_student)
    norm_teacher = top_all + jnp.log(sum_teacher)
    divergence = cross / sum_teacher - norm_teacher + norm_student
    ratio = RATIOS / ratio_index.astype(f32)
    row_weights = jnp.repeat(jnp.transpose(ratio), MASKED, axis=1).reshape(-1)
    total = micro * dp_size
    loss = jnp.sum(row_weights * divergence) / total
    d_logits = (
        (row_weights / total)[:, None]
        * (jnp.exp(logits - norm_student[:, None]) - jnp.exp(teacher - norm_teacher[:, None]))
    ).astype(bf16)
    d_final = dot(d_logits, head_weight).astype(bf16)
    d_final = jnp.transpose(
        d_final.reshape(dp_size, masked_rows, 4, 2, cols), (3, 0, 2, 1, 4)
    ).reshape(-1, masked_rows, cols)
    d_own = jnp.sum(exchange(d_final, ALL).astype(f32), axis=0).astype(bf16)
    d_own = jnp.transpose(spread(d_own, LINE).reshape(line, masked_rows, cols), (1, 0, 2)).reshape(
        masked_rows, width
    )
    rows = lax.dynamic_slice_in_dim(all_rows, dp_index * masked_rows, masked_rows, 0)
    grad_rows = norm_back(rows.astype(f32), d_own.astype(f32)).astype(bf16)

    keep_rows, give_rows, _ = call(
        last_section_back,
        "last_section_back",
        [halved, halved, ((tokens, 3 * half), bf16)],
        targets,
        *w_last,
        grad_rows,
        pick_all,
        q1,
        k1,
        v1,
        cosine,
        sine,
        **with_weights,
    )
    d_normed = sum_rows(keep_rows, give_rows, chip)
    own_pick = lax.dynamic_slice_in_dim(pick_all, row_start, chunk_rows, 1)
    grad_own = dot_tn(own_pick, grad_rows)
    grad_own = (grad_own + norm_back(mine.astype(f32), d_normed)).astype(bf16)
    grad_halves = spread_rows(grad_own, chip)

    cells = micro * slots
    columns = ((cells, cols), f32)
    chunks, grad_cols, hidden_cols, factor, _ = call(
        functools.partial(first_section_back, slots),
        "first_section_back",
        [
            ((line, cells, cols + 128), bf16),
            columns,
            columns,
            ((cells, 1), f32),
            ((cells, 3 * half), f32),
        ],
        targets,
        *w_first,
        *grad_halves,
        hidden0,
        q0,
        k0,
        v0,
        cosine,
        sine,
        **with_weights,
    )
    owners = 2 * dp_size
    (proj_part,) = call(
        finish,
        "finish",
        [((owners, depth // owners, cols), bf16)],
        exchange(chunks, LINE),
        grad_cols,
        hidden_cols,
        factor,
        placing,
        encoded,
        mb=8,
    )
    parts = exchange(proj_part, ("segment", "dp"))
    parts = jnp.sum(parts.astype(f32).reshape(2, dp_size, depth // owners, cols), axis=1)
    projector_grad = jnp.transpose(parts, (1, 0, 2)).reshape(depth // owners, 2 * cols)
    return (loss, projector_grad)


def solution(mesh):
    placed = (
        P(None, "dp", None, None),
        P(None, "dp", None, None),
        P(),
        P(None, "dp"),
        P(None, "dp", None),
        P(None, "dp", None),
        P(),
        P(None, None, "vocab"),
        P(None, "vocab", None),
        P(None, "vocab"),
        P("segment", None, "dp", "vocab"),
        P("segment", "vocab", "dp"),
        P(("segment", "dp", "vocab"), None),
        P(None, ("segment", "dp", "vocab")),
    )
    return jax.shard_map(
        shards,
        mesh=mesh,
        in_specs=placed,
        out_specs=(P(), P(("segment", "dp"), "vocab")),
        check_vma=False,
    )
```

```python
import functools

import jax
import jax.numpy as jnp
from jax import lax
from jax.experimental import pallas as pl
from jax.experimental.pallas import tpu as pltpu
from jax.sharding import PartitionSpec as P

HD = 128
MASKED = 4
RATIOS = 8

epsilon = 1e-06
rope_base = 500000.0

LINE = ("vocab", "segment")
ALL = ("segment", "dp", "vocab")
f32 = jnp.float32
bf16 = jnp.bfloat16


def dot(a, b):
    return jnp.dot(a, b, preferred_element_type=f32)


def dot_nt(a, b):
    return lax.dot_general(a, b, (((1,), (1,)), ((), ())), preferred_element_type=f32)


def dot_tn(a, b):
    return lax.dot_general(a, b, (((0,), (0,)), ((), ())), preferred_element_type=f32)


def swap(block, axis, mask):
    return lax.ppermute(block, axis, [(i, i ^ mask) for i in range(lax.axis_size(axis))])


def exchange(chunks, axes):
    return lax.all_to_all(chunks, axes, 0, 0, tiled=True)


def spread(block, axes):
    size = lax.axis_size(axes)
    return exchange(jnp.broadcast_to(block[None], (size,) + block.shape), axes)


def inverse_rms(values_in):
    return lax.rsqrt(jnp.mean(values_in * values_in, axis=-1, keepdims=True) + epsilon)


def norm_rows(values_in):
    return values_in * inverse_rms(values_in)


def layer_norm(values_in):
    centred = values_in - jnp.mean(values_in, axis=-1, keepdims=True)
    return centred * lax.rsqrt(jnp.mean(centred * centred, axis=-1, keepdims=True) + epsilon)


def norm_back(values_in, cotangent):
    factor = inverse_rms(values_in)
    return factor * cotangent - values_in * factor**3 * jnp.mean(
        cotangent * values_in, axis=-1, keepdims=True
    )


SIDE = ("dp", "vocab")
TOKENS = ("segment", "vocab")


def call(body, name, outs, *args, smem=0, far=0, scratch=(), mb=0, vmem=34):
    specs = [pl.BlockSpec(memory_space=pltpu.SMEM)] * smem + [
        pl.BlockSpec(memory_space=pl.ANY)
    ] * far
    specs += [pl.BlockSpec(memory_space=pltpu.VMEM)] * (len(args) - len(specs))
    return pl.pallas_call(
        body,
        name=name,
        out_shape=[jax.ShapeDtypeStruct(shape, kind) for shape, kind in outs],
        in_specs=specs,
        out_specs=[pl.BlockSpec(memory_space=pltpu.VMEM) for _ in outs],
        scratch_shapes=list(scratch),
        cost_estimate=pl.CostEstimate(flops=0, bytes_accessed=mb * 1000000, transcendentals=0),
        compiler_params=pltpu.CompilerParams(vmem_limit_bytes=vmem << 20),
    )(*args)


def side_shift(block, step, first):
    sizes = (lax.axis_size("dp"), lax.axis_size("vocab"))
    edge = 4
    route = []
    for dp in range(sizes[0]):
        z, y = divmod(dp, edge)
        for v in range(sizes[1]):
            if (v % 2 == 0) == first:
                to = z * edge + (y + step) % edge
            else:
                to = ((z + step) % edge) * edge + y
            route.append((dp * sizes[1] + v, to * sizes[1] + v))
    return lax.ppermute(block, SIDE, route)


def line_move(block, lo, hi):
    count = lax.axis_size("vocab")
    route = [
        (s * count + v, (s ^ lo) * count + (v ^ (2 * hi)))
        for s in range(lax.axis_size("segment"))
        for v in range(count)
    ]
    return lax.ppermute(block, TOKENS, route)


def core_groups():
    total = lax.axis_size(ALL)
    return [list(range(core, total, 2)) for core in range(2)]


def spread_within(block, axes, groups):
    copies = jnp.broadcast_to(block[None], (len(groups[0]),) + block.shape)
    return lax.all_to_all(copies, axes, 0, 0, axis_index_groups=groups, tiled=True)


def sum_rows(mine, give, chip):
    rows, width = mine.shape
    both = (mine.astype(f32) + swap(give, "vocab", 1).astype(f32)).astype(bf16)
    both = both.reshape(4, rows // 4, width)

    def piece(mask):
        return lax.dynamic_index_in_dim(both, chip ^ mask, 0, False)

    moved = [line_move(piece(m), m & 1, m >> 1) for m in (1, 2, 3)]
    return (piece(0).astype(f32) + moved[0].astype(f32)) + (
        moved[1].astype(f32) + moved[2].astype(f32)
    )


def spread_rows(block, chip):
    rows, width = block.shape
    pieces = [block] + [line_move(block, m & 1, m >> 1) for m in (1, 2, 3)]
    half = jnp.zeros((4, rows, width), block.dtype)
    for mask in range(4):
        half = lax.dynamic_update_slice(half, pieces[mask][None], (chip ^ mask, 0, 0))
    half = half.reshape(4 * rows, width)
    return half, swap(half, "vocab", 1)


def prepare(counts, order, masks, placing_out, pick_out, masked_out):
    micro, slots, _ = placing_out.shape
    images = order.shape[1]
    each = slots // images
    cell = lax.broadcasted_iota(jnp.int32, (slots, slots), 0)
    slot = lax.broadcasted_iota(jnp.int32, (slots, slots), 1)
    tokens = pick_out.shape[1]
    seq_len = tokens // micro
    row = lax.broadcasted_iota(jnp.int32, pick_out.shape, 0)
    column = lax.broadcasted_iota(jnp.int32, pick_out.shape, 1)
    token = lax.broadcasted_iota(jnp.int32, masked_out.shape, 0)
    pick = jnp.zeros(pick_out.shape, f32)
    masked = jnp.zeros(masked_out.shape, f32)
    for m in range(micro):
        hit = jnp.zeros((slots, slots), f32)
        for i in range(images):
            within = slot - i * each
            inside = (within >= 0) & (within < each) & (cell == order[m, i] * each + within)
            live = jnp.where(i < counts[m, 0], 1.0, 0.0)
            hit = jnp.where(inside, live, hit)
        placing_out[m] = hit.astype(bf16)
        for p in range(MASKED):
            where = m * seq_len + masks[m, p]
            pick = jnp.where((row == m * MASKED + p) & (column == where), 1.0, pick)
            masked = jnp.where(token == where, 1.0, masked)
    pick_out[...] = pick.astype(bf16)
    masked_out[...] = masked


def add_parts(x, parts):
    total = parts[0][...].astype(f32) + parts[1][...].astype(f32)
    total = total + (parts[2][...].astype(f32) + parts[3][...].astype(f32))
    return (x[...].astype(f32) + total).astype(bf16)


STEP = 272


def mlp(layer, current, up_far, down_far, up, down, sems):
    units, layers, _ = up.shape
    starts = list(range(0, units, STEP))
    copies = []
    for i, start in enumerate(starts):
        part = pl.ds(start, min(STEP, units - start))
        for j, (far, near) in enumerate(((up_far, up), (down_far, down))):
            copies.append(pltpu.make_async_copy(far.at[part], near.at[part], sems.at[i, j]))
    start_all(copies)
    normed = layer_norm(current().astype(f32)).astype(bf16)
    total = jnp.zeros(normed.shape, f32)
    for i, start in enumerate(starts):
        part = slice(start, min(start + STEP, units))
        shape = ((part.stop - start) * layers, up.shape[2])
        copies[2 * i].wait()
        inner = dot_nt(normed, up[part].reshape(shape))
        mine = lax.broadcasted_iota(jnp.int32, inner.shape, 1) % layers == layer
        inner = jnp.where(mine, jax.nn.gelu(inner, approximate=True), 0.0).astype(bf16)
        copies[2 * i + 1].wait()
        total = total + dot(inner, down[part].reshape(shape))
    return total.astype(bf16)


def encode_first(up_far, down_far, x, part, up, down, sems):
    part[...] = mlp(0, lambda: x[...], up_far, down_far, up, down, sems)


def encode_next(layer, up_far, down_far, x, p0, p1, p2, p3, part, current, up, down, sems):
    def now():
        value = add_parts(x, (p0, p1, p2, p3))
        current[...] = value
        return value

    part[...] = mlp(layer, now, up_far, down_far, up, down, sems)


def encode_last(x, p0, p1, p2, p3, projector, current, columns):
    now = add_parts(x, (p0, p1, p2, p3))
    current[...] = now
    mine = dot(now, projector[...]).astype(bf16)
    for i in range(columns.shape[0]):
        columns[i] = mine


def turn(values, cosine, sine):
    return values * cosine + pltpu.roll(values, HD // 2, 1) * sine


def load_weights(targets, blocks, w, sems):
    rows = w.shape[1] // 16
    sources = [array.at[i] for array in blocks for i in range(array.shape[0])]
    parts = []
    for number, mats in enumerate((pl.ds(3, 1), pl.ds(0, 3))):
        copies = []
        for i, source in enumerate(sources):
            start = pl.multiple_of(targets[i] * rows, rows)
            copies.append(
                pltpu.make_async_copy(
                    source.at[mats], w.at[mats, pl.ds(start, rows), :], sems.at[number, i]
                )
            )
        parts.append(copies)
    return parts


def start_all(copies):
    for copy in copies:
        copy.start()


def wait_all(copies):
    for copy in copies:
        copy.wait()


def pairs_of(tokens, seq_len, half):
    return [
        (m, slice(m * seq_len, (m + 1) * seq_len), slice(h * HD, (h + 1) * HD))
        for m in range(tokens // seq_len)
        for h in range(half // HD)
    ]


def project_heads(hidden, w, cosine, sine, copies):
    half = w.shape[2]
    normed = norm_rows(hidden.astype(f32)).astype(bf16)
    wait_all(copies)
    q_all, k_all, v_all = (dot(normed, w[i]) for i in range(3))
    repeat = hidden.shape[0] // cosine.shape[0]
    cosine = jnp.concatenate([cosine[...]] * repeat, axis=0)
    sine = jnp.concatenate([sine[...]] * repeat, axis=0)

    def turned(values):
        return jnp.concatenate(
            [
                turn(values[:, h * HD : (h + 1) * HD], cosine, sine).astype(bf16)
                for h in range(half // HD)
            ],
            axis=1,
        )

    return turned(q_all), turned(k_all), v_all.astype(bf16)


def softmax(scores):
    powers = jnp.exp(scores - jnp.max(scores, axis=-1, keepdims=True))
    return powers / jnp.sum(powers, axis=-1, keepdims=True)


def attend(queries, keys, values):
    scores = [dot_nt(q, k) * HD ** (-0.5) for q, k in zip(queries, keys)]
    probs = [softmax(x).astype(bf16) for x in scores]
    return [dot(p, v).astype(bf16) for p, v in zip(probs, values)]


def attend_back(queries, keys, values, d_mixed):
    scores = [dot_nt(q, k) * HD ** (-0.5) for q, k in zip(queries, keys)]
    d_probs = [dot_nt(d, v).astype(bf16).astype(f32) for d, v in zip(d_mixed, values)]
    probs = [softmax(x) for x in scores]
    d_scores = [
        p * (d - jnp.sum(p * d, axis=-1, keepdims=True)) for p, d in zip(probs, d_probs)
    ]
    return (
        [(d * HD ** (-0.5)).astype(bf16) for d in d_scores],
        [p.astype(bf16) for p in probs],
    )


def split_halves(scalars, partial, keep, give):
    core, rows = scalars[16], keep.shape[0]
    keep[...] = partial[pl.ds(pl.multiple_of(core * rows, rows), rows), :]
    give[...] = partial[pl.ds(pl.multiple_of((1 - core) * rows, rows), rows), :]


def join_halves(scalars, own, other, whole):
    core, rows = scalars[16], own.shape[0]
    whole[pl.ds(pl.multiple_of(core * rows, rows), rows), :] = own[...]
    whole[pl.ds(pl.multiple_of((1 - core) * rows, rows), rows), :] = other[...]


def first_section(targets, *refs):
    blocks, refs = refs[:8], refs[8:]
    images, text, mask_row, placing, masked, cosine, sine = refs[:7]
    hidden, q, k, v, keep, give, mixed, w, sems, partial = refs[7:]
    out_copies, in_copies = load_weights(targets, blocks, w, sems)
    start_all(in_copies)
    start_all(out_copies)
    micro, slots, _ = placing.shape
    seq_len = cosine.shape[0]
    tokens, width = hidden.shape
    blocks_wide = images.shape[0] // micro
    part = width // blocks_wide
    half = q.shape[1]
    for m in range(micro):
        rows = slice(m * seq_len, (m + 1) * seq_len)
        hidden[rows, :] = jnp.where(masked[rows, :] > 0.0, mask_row[...], text[m])
        place = placing[m]
        filled = jnp.sum(place.astype(f32), axis=1, keepdims=True) > 0.0
        for b in range(blocks_wide):
            placed = dot(place, images[m * blocks_wide + b]).astype(bf16)
            cols = slice(b * part, (b + 1) * part)
            hidden[m * seq_len : m * seq_len + slots, cols] = jnp.where(
                filled, placed, text[m, :slots, cols]
            )
    q_all, k_all, v_all = project_heads(hidden[...], w, cosine, sine, in_copies)
    q[...] = q_all
    k[...] = k_all
    v[...] = v_all
    pairs = pairs_of(tokens, seq_len, half)
    results = attend(*([x[rows, cols] for _, rows, cols in pairs] for x in (q_all, k_all, v_all)))
    for (_, rows, cols), result in zip(pairs, results):
        mixed[rows, cols] = result
    wait_all(out_copies)
    partial[...] = dot_nt(mixed[...], w[3]).astype(bf16)
    split_halves(targets, partial, keep, give)


def last_section(targets, *refs):
    blocks, refs = refs[:8], refs[8:]
    own, other, pick, cosine, sine, q, k, v, partial, picked, mixed, w, sems, hidden = refs
    out_copies, in_copies = load_weights(targets, blocks, w, sems)
    start_all(in_copies)
    start_all(out_copies)
    join_halves(targets, own, other, hidden)
    picked[...] = dot(pick[...], hidden[...])
    q_all, k_all, v_all = project_heads(hidden[...], w, cosine, sine, in_copies)
    q_few = dot(pick[...], q_all).astype(bf16)
    q[...] = q_few
    k[...] = k_all
    v[...] = v_all
    pairs = pairs_of(hidden.shape[0], cosine.shape[0], k.shape[1])
    few = [slice(m * MASKED, (m + 1) * MASKED) for m, _, _ in pairs]
    results = attend(
        [q_few[mine, cols] for mine, (_, _, cols) in zip(few, pairs)],
        *([x[rows, cols] for _, rows, cols in pairs] for x in (k_all, v_all)),
    )
    for mine, (_, _, cols), result in zip(few, pairs, results):
        mixed[mine, cols] = result
    wait_all(out_copies)
    partial[...] = dot_nt(mixed[...], w[3]).astype(bf16)


def back_to_width(d_all, w):
    half = w.shape[2]
    total = dot_nt(d_all[:, :half].astype(bf16), w[0])
    for i in (1, 2):
        total = total + dot_nt(d_all[:, i * half : (i + 1) * half].astype(bf16), w[i])
    return total.astype(bf16)


def last_section_back(targets, *refs):
    blocks, refs = refs[:8], refs[8:]
    grad, pick, q, k, v, cosine, sine, keep, give, d_all, w, sems, partial = refs
    out_copies, in_copies = load_weights(targets, blocks, w, sems)
    start_all(out_copies)
    start_all(in_copies)
    half = k.shape[1]
    pairs = pairs_of(k.shape[0], cosine.shape[0], half)
    few = [slice(m * MASKED, (m + 1) * MASKED) for m, _, _ in pairs]
    queries = [q[mine, cols] for mine, (_, _, cols) in zip(few, pairs)]
    keys, values = ([x[rows, cols] for _, rows, cols in pairs] for x in (k, v))
    wait_all(out_copies)
    d_mixed = dot(grad[...], w[3]).astype(bf16)
    d_heads = [d_mixed[mine, cols] for mine, (_, _, cols) in zip(few, pairs)]
    d_scores, probs = attend_back(queries, keys, values, d_heads)
    d_q = [dot(d, k_h).astype(bf16) for d, k_h in zip(d_scores, keys)]
    d_k = [dot_tn(d, q_h).astype(bf16).astype(f32) for d, q_h in zip(d_scores, queries)]
    d_v = [dot_tn(p, d_h) for p, d_h in zip(probs, d_heads)]
    d_q = [
        dot_tn(pick[mine, rows], d) for mine, (_, rows, _), d in zip(few, pairs, d_q)
    ]
    back_sine = -sine[...]
    for i, (_, rows, cols) in enumerate(pairs):
        for part, d in enumerate(
            (turn(d_q[i], cosine[...], back_sine), turn(d_k[i], cosine[...], back_sine), d_v[i])
        ):
            at = part * half + cols.start
            d_all[rows, at : at + HD] = d.astype(bf16)
    wait_all(in_copies)
    partial[...] = back_to_width(d_all, w)
    split_halves(targets, partial, keep, give)


def first_section_back(slots, targets, *refs):
    blocks, refs = refs[:8], refs[8:]
    own, other, hidden, q, k, v, cosine, sine = refs[:8]
    chunks, grad_cols, hidden_cols, factor, d_all, w, sems, grad = refs[8:]
    join_halves(targets, own, other, grad)
    out_copies, in_copies = load_weights(targets, blocks, w, sems)
    start_all(out_copies)
    start_all(in_copies)
    half = k.shape[1]
    seq_len = cosine.shape[0]
    pairs = pairs_of(k.shape[0], seq_len, half)
    queries, keys, values = ([x[rows, cols] for _, rows, cols in pairs] for x in (q, k, v))
    wait_all(out_copies)
    d_mixed = dot(grad[...], w[3]).astype(bf16)
    d_heads = [d_mixed[rows, cols] for _, rows, cols in pairs]
    d_scores, probs = attend_back(queries, keys, values, d_heads)
    d_q = [dot(d, k_h)[:slots].astype(bf16).astype(f32) for d, k_h in zip(d_scores, keys)]
    d_k = [
        dot_tn(d, q_h)[:slots].astype(bf16).astype(f32) for d, q_h in zip(d_scores, queries)
    ]
    d_v = [dot_tn(p, d_h)[:slots] for p, d_h in zip(probs, d_heads)]
    cos_top, sin_top = cosine[:slots, :], -sine[:slots, :]
    for i, (m, _, cols) in enumerate(pairs):
        top = slice(m * slots, (m + 1) * slots)
        for part, d in enumerate(
            (turn(d_q[i], cos_top, sin_top), turn(d_k[i], cos_top, sin_top), d_v[i])
        ):
            at = part * half + cols.start
            d_all[top, at : at + HD] = d
    wait_all(in_copies)
    rounded = back_to_width(d_all, w)
    line, cells, _ = chunks.shape
    cols = grad_cols.shape[1]
    at = pl.multiple_of(targets[17] * cols, cols)
    lane = lax.broadcasted_iota(jnp.int32, (slots, chunks.shape[2] - cols), 1)
    for m in range(k.shape[0] // seq_len):
        top = slice(m * slots, (m + 1) * slots)
        rows = slice(m * seq_len, m * seq_len + slots)
        values = hidden[rows, :].astype(f32)
        mine = rounded[top, :]
        along = jnp.mean(mine.astype(f32) * values, axis=1, keepdims=True)
        high = along.astype(bf16).astype(f32)
        notes = jnp.where(lane == 0, high, jnp.where(lane == 1, along - high, 0.0)).astype(bf16)
        for c in range(line):
            chunks[c, top, :cols] = mine[:, c * cols : (c + 1) * cols]
            chunks[c, top, cols:] = notes
        factor[top, :] = inverse_rms(values)
        grad_cols[top, :] = grad[rows, pl.ds(at, cols)].astype(f32)
        hidden_cols[top, :] = hidden[rows, pl.ds(at, cols)].astype(f32)


def finish(parts, grad_cols, hidden_cols, factor, placing, encoded, out):
    cells, cols = grad_cols.shape
    total = parts[0].astype(f32)
    for c in range(1, parts.shape[0]):
        total = total + parts[c].astype(f32)
    along = total[:, cols : cols + 1] + total[:, cols + 1 : cols + 2]
    scale = factor[...]
    grad = grad_cols[...] + scale * total[:, :cols] - hidden_cols[...] * scale**3 * along
    grad = grad.astype(bf16)
    micro, slots, _ = placing.shape
    d_image = jnp.concatenate(
        [
            dot_tn(placing[m], grad[m * slots : (m + 1) * slots]).astype(bf16)
            for m in range(micro)
        ],
        axis=0,
    )
    total = dot_tn(encoded[...], d_image)
    owners, rows, _ = out.shape
    for i in range(owners):
        out[i] = total[i * rows : (i + 1) * rows].astype(bf16)


def slice_order(dp_index, core):
    z, y = dp_index // 4, dp_index % 4
    step = jnp.arange(4, dtype=jnp.int32)
    outer = ((jnp.where(core == 0, z, y) + step) % 4)[:, None]
    inner = ((jnp.where(core == 0, y, z) + step) % 4)[None, :]
    return jnp.where(core == 0, outer * 4 + inner, inner * 4 + outer).reshape(-1)


def second_moves(low, high):
    return (
        side_shift(low, 1, False),
        side_shift(high, -1, False),
        side_shift(high, 1, False),
        side_shift(low, -1, False),
    )


def in_order(low, high, moves):
    behind_low, ahead_high, behind_high, ahead_low = moves
    far_low = side_shift(behind_low, 1, False)
    far_high = side_shift(ahead_high, -1, False)
    return (low, high, ahead_low, ahead_high, far_low, far_high, behind_low, behind_high)


def shards(
    patches,
    text_embed,
    mask_embed,
    image_counts,
    image_order,
    masked_positions,
    ratio_index,
    enc_up,
    enc_down,
    projector,
    lang_qkv,
    lang_out,
    head_weight,
    teacher_logits,
):
    segment = lax.axis_index("segment")
    dp_index = lax.axis_index("dp")
    place = lax.axis_index("vocab") * 2 + segment
    core = lax.axis_index("vocab") % 2
    chip = (lax.axis_index("vocab") // 2) * 2 + segment
    line = lax.axis_size(LINE)
    dp_size = lax.axis_size("dp")
    micro = text_embed.shape[0]
    seq_len, width = text_embed.shape[2:]
    slots = patches.shape[2]
    depth = patches.shape[3]

    shard = jnp.concatenate(
        [lang_qkv[0], jnp.transpose(lang_out[0])[None]], axis=0
    )
    half = shard.shape[2] // 2
    low, high = shard[:, :, :half], shard[:, :, half:]
    keep = jnp.where(segment == 0, low, high)
    give = jnp.where(segment == 0, high, low)
    got = swap(give, "segment", 1)
    with_weights = dict(
        smem=1,
        far=8,
        scratch=(
            pltpu.VMEM((4, width, half), bf16),
            pltpu.SemaphoreType.DMA((2, 16)),
            pltpu.VMEM((micro * seq_len, width), bf16),
        ),
        mb=30,
    )

    layers, _, hidden_units = enc_up.shape
    tokens = micro * seq_len
    masked_rows = micro * MASKED
    placing, pick_all, masked = call(
        prepare,
        "prepare",
        [
            ((micro, slots, slots), bf16),
            ((masked_rows, tokens), bf16),
            ((tokens, 1), f32),
        ],
        image_counts,
        image_order[:, 0],
        masked_positions[:, 0],
        smem=3,
        mb=3,
    )
    up = jnp.transpose(enc_up, (2, 0, 1))
    down = jnp.transpose(enc_down, (1, 0, 2))

    def parts_of(part):
        return [part] + [swap(part, "vocab", mask) for mask in (1, 2, 3)]

    small = ((slots, depth), bf16)
    current = lax.dynamic_index_in_dim(patches[:, 0], segment, 0, False)
    with_layers = dict(
        far=2,
        scratch=(
            pltpu.VMEM(up.shape, bf16),
            pltpu.VMEM(down.shape, bf16),
            pltpu.SemaphoreType.DMA((-(-hidden_units // STEP), 2)),
        ),
        mb=20,
    )
    (part,) = call(encode_first, "encode_first", [small], up, down, current, **with_layers)
    angles = jnp.arange(seq_len, dtype=f32)[:, None] * (
        rope_base ** (-2.0 * jnp.arange(HD // 2, dtype=f32) / HD)
    )
    cosine = jnp.concatenate([jnp.cos(angles), jnp.cos(angles)], axis=1)
    sine = jnp.concatenate([-jnp.sin(angles), jnp.sin(angles)], axis=1)
    targets = jnp.concatenate(
        [slice_order(dp_index, core), jnp.stack([core, place]).astype(jnp.int32)]
    )
    got, part, placing, pick_all, masked, cosine, sine, targets = lax.optimization_barrier(
        (got, part, placing, pick_all, masked, cosine, sine, targets)
    )
    first = segment == 0
    both = jnp.stack([jnp.where(first, keep, got), jnp.where(first, got, keep)])
    behind = side_shift(both, 1, True)
    ahead = side_shift(both, -1, True)
    first_parts = parts_of(part)
    behind, ahead, first_parts = lax.optimization_barrier((behind, ahead, first_parts))
    far = [side_shift(behind[0], 1, True), side_shift(ahead[1], -1, True)]
    part, current = call(
        functools.partial(encode_next, 1),
        "encode_next",
        [small, small],
        up,
        down,
        current,
        *first_parts,
        **with_layers,
    )
    far, part = lax.optimization_barrier((far, part))
    low = [jnp.stack([both[s], ahead[s]]) for s in range(2)]
    high = [jnp.stack([far[s], behind[s]]) for s in range(2)]
    moves = second_moves(low[0], high[0])
    encoded_own, image_cols = call(
        encode_last,
        "encode_last",
        [small, ((line, slots, projector.shape[1]), bf16)],
        current,
        *parts_of(part),
        projector,
        mb=10,
        vmem=12,
    )
    early, image_cols = lax.optimization_barrier((moves[:2], image_cols))
    moves = (*early, *moves[2:])
    w_first = in_order(low[0], high[0], moves)
    images = exchange(image_cols, TOKENS)
    w_first, images, low[1], high[1] = lax.optimization_barrier(
        (w_first, images, low[1], high[1])
    )
    moves = second_moves(low[1], high[1])
    encoded_other = swap(encoded_own, "segment", 1)
    encoded = jnp.concatenate(
        [
            jnp.where(segment == 0, encoded_own, encoded_other),
            jnp.where(segment == 0, encoded_other, encoded_own),
        ],
        axis=0,
    )

    chunk_rows = tokens // line
    row_start = (core * 4 + chip) * chunk_rows
    whole = ((tokens, width), bf16)
    halved = ((tokens // 2, width), bf16)
    heads = ((tokens, half), bf16)

    def own_rows(array):
        return lax.dynamic_slice_in_dim(array, row_start, chunk_rows, 0)

    hidden0, q0, k0, v0, keep_rows, give_rows, _ = call(
        first_section,
        "first_section",
        [whole, heads, heads, heads, halved, halved, heads],
        targets,
        *w_first,
        images,
        text_embed[:, 0],
        mask_embed[None, :],
        placing,
        masked,
        cosine,
        sine,
        **with_weights,
    )
    early, give_rows = lax.optimization_barrier((moves[:2], give_rows))
    mine = (own_rows(hidden0).astype(f32) + sum_rows(keep_rows, give_rows, chip)).astype(bf16)
    w_last = in_order(low[1], high[1], (*early, *moves[2:]))
    far, mine = lax.optimization_barrier((w_last[4:6], mine))
    w_last = (*w_last[:4], *far, *w_last[6:])
    hidden_halves = spread_rows(mine, chip)

    few_heads = ((masked_rows, half), bf16)
    q1, k1, v1, partial, picked, _ = call(
        last_section,
        "last_section",
        [
            few_heads,
            heads,
            heads,
            ((masked_rows, width), bf16),
            ((masked_rows, width), f32),
            few_heads,
        ],
        targets,
        *w_last,
        *hidden_halves,
        pick_all,
        cosine,
        sine,
        **with_weights,
    )
    cols = width // line
    parts = exchange(
        jnp.transpose(partial.reshape(masked_rows, line, cols), (1, 0, 2)), LINE
    )
    picked = lax.dynamic_slice_in_dim(picked, place * cols, cols, 1)
    last = (picked + jnp.sum(parts.astype(f32), axis=0)).astype(bf16)

    own_cols = spread_within(last, ALL, core_groups())
    other_cols = swap(own_cols, "vocab", 1)
    by_core = jnp.stack(
        [
            jnp.where(core == 0, own_cols, other_cols),
            jnp.where(core == 0, other_cols, own_cols),
        ]
    ).reshape(2, 2, dp_size, 2, masked_rows, cols)
    all_rows = jnp.transpose(by_core, (2, 4, 3, 0, 1, 5)).reshape(dp_size * masked_rows, width)
    row_count = all_rows.shape[0]
    final = norm_rows(all_rows.astype(f32)).astype(bf16)
    logits = dot_nt(final, head_weight)

    teacher = (
        jnp.transpose(teacher_logits.reshape(micro, dp_size, MASKED, -1), (1, 0, 2, 3))
        .reshape(row_count, -1)
        .astype(f32)
    )
    top = jnp.max(teacher, axis=1)
    powers = jnp.exp(teacher - top[:, None])
    stats = jnp.stack(
        [
            jnp.sum(jnp.exp(logits), axis=1),
            top,
            jnp.sum(powers, axis=1),
            jnp.sum(powers * (teacher - logits), axis=1),
        ]
    )
    stats = spread(stats, ALL).reshape(-1, 4, row_count)
    sum_student = jnp.sum(stats[:, 0], axis=0)
    top_all = jnp.max(stats[:, 1], axis=0)
    scale = jnp.exp(stats[:, 1] - top_all[None])
    sum_teacher = jnp.sum(stats[:, 2] * scale, axis=0)
    cross = jnp.sum(stats[:, 3] * scale, axis=0)
    norm_student = jnp.log(sum_student)
    norm_teacher = top_all + jnp.log(sum_teacher)
    divergence = cross / sum_teacher - norm_teacher + norm_student
    ratio = RATIOS / ratio_index.astype(f32)
    row_weights = jnp.repeat(jnp.transpose(ratio), MASKED, axis=1).reshape(-1)
    total = micro * dp_size
    loss = jnp.sum(row_weights * divergence) / total
    d_logits = (
        (row_weights / total)[:, None]
        * (jnp.exp(logits - norm_student[:, None]) - jnp.exp(teacher - norm_teacher[:, None]))
    ).astype(bf16)
    d_final = dot(d_logits, head_weight).astype(bf16)
    d_final = jnp.transpose(
        d_final.reshape(dp_size, masked_rows, 4, 2, cols), (3, 0, 2, 1, 4)
    ).reshape(-1, masked_rows, cols)
    d_own = jnp.sum(exchange(d_final, ALL).astype(f32), axis=0).astype(bf16)
    d_own = jnp.transpose(spread(d_own, LINE).reshape(line, masked_rows, cols), (1, 0, 2)).reshape(
        masked_rows, width
    )
    rows = lax.dynamic_slice_in_dim(all_rows, dp_index * masked_rows, masked_rows, 0)
    grad_rows = norm_back(rows.astype(f32), d_own.astype(f32)).astype(bf16)

    keep_rows, give_rows, _ = call(
        last_section_back,
        "last_section_back",
        [halved, halved, ((tokens, 3 * half), bf16)],
        targets,
        *w_last,
        grad_rows,
        pick_all,
        q1,
        k1,
        v1,
        cosine,
        sine,
        **with_weights,
    )
    d_normed = sum_rows(keep_rows, give_rows, chip)
    own_pick = lax.dynamic_slice_in_dim(pick_all, row_start, chunk_rows, 1)
    grad_own = dot_tn(own_pick, grad_rows)
    grad_own = (grad_own + norm_back(mine.astype(f32), d_normed)).astype(bf16)
    grad_halves = spread_rows(grad_own, chip)

    cells = micro * slots
    columns = ((cells, cols), f32)
    chunks, grad_cols, hidden_cols, factor, _ = call(
        functools.partial(first_section_back, slots),
        "first_section_back",
        [
            ((line, cells, cols + 128), bf16),
            columns,
            columns,
            ((cells, 1), f32),
            ((cells, 3 * half), f32),
        ],
        targets,
        *w_first,
        *grad_halves,
        hidden0,
        q0,
        k0,
        v0,
        cosine,
        sine,
        **with_weights,
    )
    owners = 2 * dp_size
    (proj_part,) = call(
        finish,
        "finish",
        [((owners, depth // owners, cols), bf16)],
        exchange(chunks, LINE),
        grad_cols,
        hidden_cols,
        factor,
        placing,
        encoded,
        mb=8,
    )
    parts = exchange(proj_part, ("segment", "dp"))
    parts = jnp.sum(parts.astype(f32).reshape(2, dp_size, depth // owners, cols), axis=1)
    projector_grad = jnp.transpose(parts, (1, 0, 2)).reshape(depth // owners, 2 * cols)
    return (loss, projector_grad)


def solution(mesh):
    placed = (
        P(None, "dp", None, None),
        P(None, "dp", None, None),
        P(),
        P(None, "dp"),
        P(None, "dp", None),
        P(None, "dp", None),
        P(),
        P(None, None, "vocab"),
        P(None, "vocab", None),
        P(None, "vocab"),
        P("segment", None, "dp", "vocab"),
        P("segment", "vocab", "dp"),
        P(("segment", "dp", "vocab"), None),
        P(None, ("segment", "dp", "vocab")),
    )
    return jax.shard_map(
        shards,
        mesh=mesh,
        in_specs=placed,
        out_specs=(P(), P(("segment", "dp"), "vocab")),
        check_vma=False,
    )
```
